32 devices in a mesh: dp: 8 (over z, x), fsdp: 4 (over y, core).
Axes of the slice: x: 2, y: 2, z: 4, core: 2. Of those that a mesh axis runs over, the one named last changes fastest.
Arguments:
- token_states: bfloat16 [32, 1024, 768], P(('dp', 'fsdp')), may hold values from -6 to 6
- char_codes: int32 [32, 1024, 4], P(('dp', 'fsdp')), may hold values from 0 to 999
- lengths: int32 [32], P(('dp', 'fsdp')), may hold values from 256 to 1024, as said below
- token_cotangent: bfloat16 [32, 1024, 768], P(('dp', 'fsdp')), may hold values from -6 to 6
- char_cotangent: bfloat16 [32, 1024, 768], P(('dp', 'fsdp')), may hold values from -6 to 6
- char_table: bfloat16 [1000, 256], P(None, ('dp', 'fsdp')), may hold values from -6 to 6
- recur_input: bfloat16 [256, 2304], P(None, ('dp', 'fsdp')), may hold values from -0.375 to 0.375
- recur_state: bfloat16 [384, 2304], P(None, ('dp', 'fsdp')), may hold values from -0.3125 to 0.3125
- project_weight: bfloat16 [768, 2304], P(('dp', 'fsdp')), may hold values from -0.21875 to 0.21875
- output_weight: bfloat16 [768, 768], P(('dp', 'fsdp')), may hold values from -0.625 to 0.625
- merging_weight: bfloat16 [3, 1536, 768], P(None, ('dp', 'fsdp')), may hold values from -0.09375 to 0.09375
- up_weight: bfloat16 [768, 3072], P(('dp', 'fsdp')), may hold values from -0.21875 to 0.21875
- down_weight: bfloat16 [3072, 768], P(('dp', 'fsdp')), may hold values from -0.109375 to 0.109375
- char_weight: bfloat16 [768, 768], P(('dp', 'fsdp')), may hold values from -0.21875 to 0.21875
- attend_gain: bfloat16 [768], P(('dp', 'fsdp')), may hold values from 0.25 to 1.75
- attend_shift: bfloat16 [768], P(('dp', 'fsdp')), may hold values from -1.75 to 1.75
- feed_gain: bfloat16 [768], P(('dp', 'fsdp')), may hold values from 0.25 to 1.75
- feed_shift: bfloat16 [768], P(('dp', 'fsdp')), may hold values from -1.75 to 1.75
- char_gain: bfloat16 [768], P(('dp', 'fsdp')), may hold values from 0.25 to 1.75
- char_shift: bfloat16 [768], P(('dp', 'fsdp')), may hold values from -1.75 to 1.75
Outputs:
- token_stream: bfloat16 [32, 1024, 768], P(('dp', 'fsdp'))
- char_stream: bfloat16 [32, 1024, 768], P(('dp', 'fsdp'))
- input_gradient: bfloat16 [32, 1024, 768], P(('dp', 'fsdp'))
- table_gradient: float32 [1000, 256], P(None, ('dp', 'fsdp'))
- inlet_gradient: float32 [256, 2304], P(None, ('dp', 'fsdp'))
- recur_gradient: float32 [384, 2304], P(None, ('dp', 'fsdp'))
- project_gradient: float32 [768, 2304], P(('dp', 'fsdp'))
- output_gradient: float32 [768, 768], P(('dp', 'fsdp'))
- merging_gradient: float32 [3, 1536, 768], P(None, ('dp', 'fsdp'))
- up_gradient: float32 [768, 3072], P(('dp', 'fsdp'))
- down_gradient: float32 [3072, 768], P(('dp', 'fsdp'))
- branch_gradient: float32 [768, 768], P(('dp', 'fsdp'))
- attend_gain_gradient: float32 [768], P(('dp', 'fsdp'))
- attend_shift_gradient: float32 [768], P(('dp', 'fsdp'))
- feed_gain_gradient: float32 [768], P(('dp', 'fsdp'))
- feed_shift_gradient: float32 [768], P(('dp', 'fsdp'))
- char_gain_gradient: float32 [768], P(('dp', 'fsdp'))
- char_shift_gradient: float32 [768], P(('dp', 'fsdp'))
The draws below stay inside these ranges and needn't reach their ends.
Inputs may be any that keep to these rules, and one draw needn't show every extreme that they name: `lengths`: the valid tokens of a sequence are its first ones; at least one sequence is full.
All inputs are finite; a program needn't handle non-finite values.
Results may differ from the reference program's by a relative error of at most 0.015.
Values may be sent and summed in bfloat16 or wider, within the bound.
No kernel may reach another device: no remote copies, remote signals or barrier semaphores. Data moves between devices by JAX's collectives and lax.ppermute only.
A program may use at most 384 MiB of HBM per device.

```python
import math
import jax
import jax.numpy as jnp
from jax import lax

D = 768
HEADS = 12
HEAD_DIM = 64
FF = 3072
CE = 256
CV = 1000
CHARS = 4
L = 1024
HG = 384
SEQS = 32


def draw_lengths(key, part):
    key = jax.random.fold_in(key, 7)
    first, second = jax.random.split(key)
    drawn = jax.random.randint(first, (SEQS,), max(1, L // 4), L + 1)
    chosen = jax.random.randint(second, (), 0, SEQS)
    return jnp.where(jnp.arange(SEQS) == chosen, L, drawn).astype(jnp.int32)


def touch_ends(values, stream_key, least, largest):
    longest = values.shape.index(max(values.shape))
    spots = []
    for shift in (0, 1):
        where = [jax.random.randint(jax.random.fold_in(stream_key, axis), (), 0, length) for axis, length in enumerate(values.shape)]
        where[longest] = (where[longest] + shift) % values.shape[longest]
        spots.append(tuple(where))
    return values.at[spots[0]].set(least).at[spots[1]].set(largest)


def block_scale(stream_key, shape, shards, low, largest):
    level, own = 1.0, jax.random.fold_in(stream_key, 6)
    for position, shards_of in shards:
        steps = jnp.exp(jax.random.uniform(jax.random.fold_in(own, position), (shards_of,), jnp.float32, low / len(shards), largest / len(shards)))
        level = level * jnp.repeat(steps, shape[position] // shards_of).reshape([-1 if axis == position else 1 for axis in range(len(shape))])
    return level


def bell_draw(stream_key, extent, scale, reach, cuts=(), kind=jnp.bfloat16):
    level = block_scale(stream_key, extent, cuts, -0.22, 0.18) if cuts else 1.0
    entries = jax.random.normal(stream_key, extent, jnp.float32) * scale * level
    return jnp.minimum(jnp.maximum(entries, -reach), reach).astype(kind)


def setup_inputs(seed: int = 0) -> dict:
    streams_of = jax.random.split(jax.random.key(seed), 21)
    token_states = bell_draw(streams_of[0], (SEQS, L, D), 1.0, 6.0, ((0, 32),))
    char_codes = touch_ends(jax.random.randint(streams_of[1], (SEQS, L, CHARS), 0, CV), jax.random.fold_in(streams_of[1], 1), 0, CV - 1).astype(jnp.int32)
    lengths = draw_lengths(jax.random.fold_in(streams_of[20], 71), 0)
    token_cotangent = bell_draw(streams_of[3], (SEQS, L, D), 1.0, 6.0, ((0, 32),))
    char_cotangent = bell_draw(streams_of[4], (SEQS, L, D), 1.0, 6.0, ((0, 32),))
    char_table = bell_draw(streams_of[5], (CV, CE), 1.0, 6.0, ((1, 32),))
    recur_input = bell_draw(streams_of[6], (CE, 6 * HG), CE ** -0.5, 0.375, ((1, 32),))
    recur_state = bell_draw(streams_of[7], (HG, 6 * HG), HG ** -0.5, 0.3125, ((1, 32),))
    project_weight = bell_draw(streams_of[8], (D, 3 * D), D ** -0.5, 0.21875, ((0, 32),))
    output_weight = bell_draw(streams_of[9], (D, D), (D // 8) ** -0.5, 0.625, ((0, 32),))
    merging_weight = bell_draw(streams_of[10], (3, 2 * D, D), (6 * D) ** -0.5, 0.09375, ((1, 32),))
    up_weight = bell_draw(streams_of[11], (D, FF), D ** -0.5, 0.21875, ((0, 32),))
    down_weight = bell_draw(streams_of[12], (FF, D), FF ** -0.5, 0.109375, ((0, 32),))
    char_weight = bell_draw(streams_of[13], (D, D), D ** -0.5, 0.21875, ((0, 32),))
    attend_gain = jnp.clip(1.0 + 0.15 * jax.random.normal(streams_of[14], (D,), jnp.float32), 0.25, 1.75).astype(jnp.bfloat16)
    attend_shift = bell_draw(streams_of[15], (D,), 0.3, 1.75, ((0, 32),))
    feed_gain = jnp.clip(1.0 + 0.15 * jax.random.normal(streams_of[16], (D,), jnp.float32), 0.25, 1.75).astype(jnp.bfloat16)
    feed_shift = bell_draw(streams_of[17], (D,), 0.3, 1.75, ((0, 32),))
    char_gain = jnp.clip(1.0 + 0.15 * jax.random.normal(streams_of[18], (D,), jnp.float32), 0.25, 1.75).astype(jnp.bfloat16)
    char_shift = bell_draw(streams_of[19], (D,), 0.3, 1.75, ((0, 32),))
    return dict(token_states=token_states, char_codes=char_codes, lengths=lengths, token_cotangent=token_cotangent, char_cotangent=char_cotangent, char_table=char_table, recur_input=recur_input, recur_state=recur_state, project_weight=project_weight, output_weight=output_weight, merging_weight=merging_weight, up_weight=up_weight, down_weight=down_weight, char_weight=char_weight, attend_gain=attend_gain, attend_shift=attend_shift, feed_gain=feed_gain, feed_shift=feed_shift, char_gain=char_gain, char_shift=char_shift)


@jax.custom_vjp
def low(v):
    return lax.optimization_barrier(v.astype(jnp.bfloat16)).astype(jnp.float32)

@jax.custom_vjp
def low_back(v):
    return v

def low_keep(v):
    return (low(v), None)

def low_pass(kept, grad):
    return (grad,)

def back_keep(v):
    return (v, None)

def back_low(kept, grad):
    return (low(grad),)
low.defvjp(low_keep, low_pass)
low_back.defvjp(back_keep, back_low)
EPS = 1e-05
MASKED = -1e+30

def matmul(left, right):
    return jnp.dot(left, right, precision=lax.Precision.HIGHEST)

def norm_apply(values, gain, shift):
    average = lax.optimization_barrier(jnp.mean(values, axis=-1, keepdims=True))
    centred = values - average
    variance = lax.optimization_barrier(jnp.mean(centred * centred, axis=-1, keepdims=True))
    return centred * lax.rsqrt(variance + EPS) * gain + shift

def exact_gelu(values):
    return jax.nn.gelu(values, approximate=False)

def recur_cell(inputs, previous, weight):
    width = weight.shape[0]
    if previous is None:
        recur = jnp.zeros_like(inputs)
        before = jnp.zeros((inputs.shape[0], width), jnp.float32)
    else:
        recur = low_back(matmul(previous, weight))
        before = previous
    reset = jax.nn.sigmoid(inputs[:, :width] + recur[:, :width])
    update = jax.nn.sigmoid(inputs[:, width:2 * width] + recur[:, width:2 * width])
    fresh = jnp.tanh(inputs[:, 2 * width:] + reset * recur[:, 2 * width:])
    return low((1.0 - update) * fresh + update * before)

def forward(params, states, codes, valid):
    table, inlet, recur, project, output, merging, upper, lower, branch, gain_one, shift_one, gain_two, shift_two, gain_three, shift_three = params
    length = states.shape[0]
    triple = 3 * HG
    letters = jnp.arange(CV, dtype=jnp.int32)
    gates = []
    for slot in range(CHARS):
        picked = (codes[:, slot][:, None] == letters[None, :]).astype(jnp.float32)
        embed = low_back(matmul(picked, table))
        gates.append(low_back(matmul(embed, inlet)))
    forward_state = None
    for slot in range(CHARS):
        forward_state = recur_cell(gates[slot][:, :triple], forward_state, recur[:, :triple])
    backward_state = None
    for slot in range(CHARS - 1, -1, -1):
        backward_state = recur_cell(gates[slot][:, triple:], backward_state, recur[:, triple:])
    chars_rep = jnp.concatenate([forward_state, backward_state], axis=1)
    mixed = low(low_back(matmul(states, project)))
    queries = mixed[:, :D].reshape(length, HEADS, HEAD_DIM)
    keys_all = mixed[:, D:2 * D].reshape(length, HEADS, HEAD_DIM)
    values_all = mixed[:, 2 * D:].reshape(length, HEADS, HEAD_DIM)
    scores = jnp.einsum('qhd,khd->hqk', queries, keys_all, precision=lax.Precision.HIGHEST) * (1.0 / math.sqrt(HEAD_DIM))
    scores = low_back(jnp.where(valid[None, None, :] > 0, scores, MASKED))
    probs = jax.nn.softmax(scores, axis=-1)
    context = jnp.einsum('hqk,khd->qhd', low(probs), values_all, precision=lax.Precision.HIGHEST).reshape(length, D)
    context = low(low_back(context))
    attended = low_back(matmul(context, output))
    first = norm_apply(states + attended, gain_one, shift_one)
    joined = jnp.concatenate([low(first), chars_rep], axis=1) * valid[:, None]
    padded = jnp.pad(joined, ((1, 1), (0, 0)))
    merging_pre = low_back(matmul(padded[:-2], merging[0]) + matmul(padded[1:-1], merging[1]) + matmul(padded[2:], merging[2]))
    merged = exact_gelu(merging_pre)
    summed = first + merged
    hidden = low(exact_gelu(low_back(matmul(low(summed), upper))))
    token_stream = norm_apply(summed + low_back(matmul(hidden, lower)), gain_two, shift_two)
    char_stream = norm_apply(chars_rep + low_back(matmul(low(merged), branch)), gain_three, shift_three)
    return (token_stream, char_stream)

def reference(token_states, char_codes, lengths, token_cotangent, char_cotangent, char_table, recur_input, recur_state, project_weight, output_weight, merging_weight, up_weight, down_weight, char_weight, attend_gain, attend_shift, feed_gain, feed_shift, char_gain, char_shift):
    params = tuple((item.astype(jnp.float32) for item in (char_table, recur_input, recur_state, project_weight, output_weight, merging_weight, up_weight, down_weight, char_weight, attend_gain, attend_shift, feed_gain, feed_shift, char_gain, char_shift)))
    positions = jnp.arange(L, dtype=jnp.int32)

    def one_sequence(totals, batch):
        seq_states, seq_codes, seq_length, seq_token, seq_char = batch
        valid = (positions < seq_length).astype(jnp.float32)

        def run(params_in, states_in):
            return forward(params_in, states_in, seq_codes, valid)
        outputs, pullback = jax.vjp(run, params, seq_states.astype(jnp.float32))
        param_grads, state_grad = pullback((seq_token.astype(jnp.float32), seq_char.astype(jnp.float32)))
        totals = jax.tree.map(lambda left, right: left + right, totals, param_grads)
        return (totals, (outputs[0].astype(jnp.bfloat16), outputs[1].astype(jnp.bfloat16), state_grad.astype(jnp.bfloat16)))
    zeros = jax.tree.map(jnp.zeros_like, params)
    totals, stacked = lax.scan(one_sequence, zeros, (token_states, char_codes, lengths, token_cotangent, char_cotangent))
    return (stacked[0], stacked[1], stacked[2], totals[0], totals[1], totals[2], totals[3], totals[4], totals[5], totals[6], totals[7], totals[8], totals[9], totals[10], totals[11], totals[12], totals[13], totals[14])
```

```python
import functools
import math

import jax
import jax.numpy as jnp
from jax import lax
from jax.experimental import pallas as pl
from jax.experimental.pallas import tpu as pltpu
from jax.sharding import PartitionSpec as P

HEAD_DIM = 64
CHARS = 4
LANES = 128
EPS = 1e-05
MASKED = -1e30
SCALE = 1.0 / math.sqrt(HEAD_DIM)
SCALE2 = math.log2(math.e) / math.sqrt(HEAD_DIM)
AXES = ("dp", "fsdp")
VMEM_LIMIT = 56 * 1024 * 1024

def norm_apply(values, gain, shift):
    average = jnp.mean(values, axis=-1, keepdims=True)
    centred = values - average
    variance = jnp.mean(centred * centred, axis=-1, keepdims=True)
    return centred * lax.rsqrt(variance + EPS) * gain + shift


def exact_gelu(values):
    return jax.nn.gelu(values, approximate=False)


def product(left, right):
    return jnp.dot(left, right, preferred_element_type=jnp.float32)


def outer_sum(left, right):
    return jnp.einsum("sli,slo->io", left, right, preferred_element_type=jnp.float32)


def back_product(grad_rows, weight):
    return jnp.einsum("slo,io->sli", grad_rows, weight, preferred_element_type=jnp.float32)


def shift_down(values):
    return jnp.pad(values[:, :-1], ((0, 0), (1, 0), (0, 0)))


def shift_up(values):
    return jnp.pad(values[:, 1:], ((0, 0), (0, 1), (0, 0)))


def cell_forward(inputs, previous, weight, width):
    if previous is None:
        recur = jnp.zeros_like(inputs)
        before = jnp.zeros(inputs.shape[:-1] + (width,), jnp.float32)
    else:
        recur = back_product(previous, weight)
        before = previous.astype(jnp.float32)
    reset = jax.nn.sigmoid(inputs[..., :width] + recur[..., :width])
    update = jax.nn.sigmoid(inputs[..., width : 2 * width] + recur[..., width : 2 * width])
    fresh = jnp.tanh(inputs[..., 2 * width :] + reset * recur[..., 2 * width :])
    state = ((1.0 - update) * fresh + update * before).astype(jnp.bfloat16)
    return (state, (reset, update, fresh, recur[..., 2 * width :], before, previous))


def cell_backward(grad_state, kept, weight):
    reset, update, fresh, recur_new, before, previous = kept
    fresh_pre = grad_state * (1.0 - update) * (1.0 - fresh * fresh)
    update_pre = grad_state * (before - fresh) * update * (1.0 - update)
    reset_pre = fresh_pre * recur_new * reset * (1.0 - reset)
    grad_inputs = jnp.concatenate([reset_pre, update_pre, fresh_pre], axis=-1)
    if previous is None:
        return (grad_inputs, None, None)
    grad_recur = jnp.concatenate([reset_pre, update_pre, fresh_pre * reset], axis=-1).astype(
        jnp.bfloat16
    )
    grad_weight = outer_sum(grad_recur, previous)
    grad_previous = grad_state * update + product(grad_recur, weight)
    return (grad_inputs, grad_weight, grad_previous)


def dotf(a,b,ca=1,cb=0):
    return lax.dot_general(a,b,(((ca,),(cb,)),((),())),preferred_element_type=jnp.float32)

def lane_half(shape):
    return lax.broadcasted_iota(jnp.int32, shape, 1) < HEAD_DIM

def attend_kernel(rows, length_ref, q_ref, k_ref, v_ref, ctx_ref, lse_ref, kx_ref, vx_ref):
    length = k_ref.shape[0]
    lane = lax.broadcasted_iota(jnp.int32, (length, LANES), 1)
    place = lax.broadcasted_iota(jnp.int32, (length, LANES), 0)
    kx_ref[:, :LANES] = k_ref[...]
    kx_ref[:, LANES:] = jnp.where((lane == 0) & (place >= length_ref[0]), MASKED, 0.0).astype(jnp.bfloat16)
    vx_ref[:, :LANES] = v_ref[...]
    vx_ref[:, LANES:] = jnp.ones((length, LANES), jnp.bfloat16)
    low = lane_half((rows, LANES))
    one = jnp.where(lax.broadcasted_iota(jnp.int32, (rows, LANES), 1) == 0, 1.0, 0.0).astype(jnp.bfloat16)
    def step(c, _):
        at = pl.ds(pl.multiple_of(c * rows, rows), rows)
        q = q_ref[at, :].astype(jnp.float32)
        outs = []
        for h in range(2):
            mine = low if h == 0 else jnp.logical_not(low)
            qx = jnp.concatenate([jnp.where(mine, q, 0.0).astype(jnp.bfloat16), one], axis=1)
            s = dotf(qx, kx_ref[...], 1, 1)
            peak = jnp.max(s, axis=1, keepdims=True) * SCALE2
            p = jnp.exp2(s * SCALE2 - peak).astype(jnp.bfloat16)
            o = dotf(p, vx_ref[...])
            total = o[:, LANES:]
            outs.append((o[:, :LANES] / total, peak + jnp.log2(total)))
        ctx_ref[at, :] = jnp.where(low, outs[0][0], outs[1][0]).astype(jnp.bfloat16)
        lse_ref[at, :] = jnp.where(low, outs[0][1], outs[1][1])
        return 0
    lax.fori_loop(0, length // rows, step, 0, unroll=True)

def attend(mixed, lengths, width, rows=256):
    length = mixed.shape[0]
    pairs = width // LANES
    spec = lambda o: pl.BlockSpec((length, LANES), lambda p, o=o: (0, p+o))
    return pl.pallas_call(
        functools.partial(attend_kernel, rows),
        grid=(pairs,),
        in_specs=[pl.BlockSpec(memory_space=pltpu.SMEM), spec(0), spec(pairs), spec(2 * pairs)],
        out_specs=[spec(0), spec(0)],
        out_shape=[jax.ShapeDtypeStruct((length, width), jnp.bfloat16), jax.ShapeDtypeStruct((length, width), jnp.float32)],
        scratch_shapes=[pltpu.VMEM((length, 2*LANES), jnp.bfloat16), pltpu.VMEM((length, 2*LANES), jnp.bfloat16)],
        compiler_params=pltpu.CompilerParams(vmem_limit_bytes=VMEM_LIMIT),
        cost_estimate=pl.CostEstimate(flops=4*12*length*length*64, bytes_accessed=10*length*width, transcendentals=12*length*length),
    )(lengths, mixed, mixed, mixed)

def back_kernel(rows, length_ref, q_ref, k_ref, v_ref, do_ref, o_ref, lse_ref, out_ref, kx_ref, vx_ref, qt_ref, dot_ref, dk_ref, dv_ref):
    length = k_ref.shape[0]
    lane = lax.broadcasted_iota(jnp.int32, (length, LANES), 1)
    place = lax.broadcasted_iota(jnp.int32, (length, LANES), 0)
    kx_ref[:, :LANES] = k_ref[...]
    kx_ref[:, LANES:] = jnp.where((lane == 0) & (place >= length_ref[0]), MASKED, 0.0).astype(jnp.bfloat16)
    qt_ref[...] = q_ref[...].T
    dot_ref[...] = do_ref[...].T
    dk_ref[...] = jnp.zeros_like(dk_ref)
    dv_ref[...] = jnp.zeros_like(dv_ref)
    low = lane_half((rows, LANES))
    one = jnp.where(lax.broadcasted_iota(jnp.int32, (rows, LANES), 1) == 0, 1.0, 0.0).astype(jnp.bfloat16)
    def step(c, _):
        at = pl.ds(pl.multiple_of(c * rows, rows), rows)
        q = q_ref[at, :].astype(jnp.float32)
        do = do_ref[at, :].astype(jnp.float32)
        doo = do * o_ref[at, :].astype(jnp.float32)
        lse = lse_ref[at, :]
        dqs = []
        for h in range(2):
            mine = low if h == 0 else jnp.logical_not(low)
            qx = jnp.concatenate([jnp.where(mine, q, 0.0).astype(jnp.bfloat16), one], axis=1)
            s = dotf(qx, kx_ref[...], 1, 1)
            p = jnp.exp2(s * SCALE2 - lse[:, h*HEAD_DIM:h*HEAD_DIM+1])
            dp = dotf(jnp.where(mine, do, 0.0).astype(jnp.bfloat16), v_ref[...], 1, 1)
            delta = jnp.sum(jnp.where(mine, doo, 0.0), axis=1, keepdims=True)
            ds = (p * (dp - delta)).astype(jnp.bfloat16)
            pb = p.astype(jnp.bfloat16)
            hs = slice(h*HEAD_DIM, (h+1)*HEAD_DIM)
            dqs.append(dotf(ds, k_ref[...]))
            dk_ref[hs, :] += dotf(qt_ref[hs, at], ds)
            dv_ref[hs, :] += dotf(dot_ref[hs, at], pb)
        out_ref[0, at, :] = (jnp.where(low, dqs[0], dqs[1]) * SCALE).astype(jnp.bfloat16)
        return 0
    lax.fori_loop(0, length // rows, step, 0, unroll=True)
    out_ref[1] = (dk_ref[...] * SCALE).T.astype(jnp.bfloat16)
    out_ref[2] = dv_ref[...].T.astype(jnp.bfloat16)

def attend_back(mixed, context_grad, context, log_totals, lengths, width, rows=256):
    length = mixed.shape[0]
    pairs = width // LANES
    spec = lambda o: pl.BlockSpec((length, LANES), lambda p, o=o: (0, p+o))
    return pl.pallas_call(
        functools.partial(back_kernel, rows),
        grid=(pairs,),
        in_specs=[pl.BlockSpec(memory_space=pltpu.SMEM), spec(0), spec(pairs), spec(2 * pairs), spec(0), spec(0), spec(0)],
        out_specs=pl.BlockSpec((3, length, LANES), lambda p: (0, 0, p)),
        out_shape=jax.ShapeDtypeStruct((3, length, width), jnp.bfloat16),
        scratch_shapes=[pltpu.VMEM((length, 2*LANES), jnp.bfloat16), pltpu.VMEM((length, 2*LANES), jnp.bfloat16),
            pltpu.VMEM((LANES, length), jnp.bfloat16), pltpu.VMEM((LANES, length), jnp.bfloat16),
            pltpu.VMEM((LANES, length), jnp.float32), pltpu.VMEM((LANES, length), jnp.float32)],
        compiler_params=pltpu.CompilerParams(vmem_limit_bytes=VMEM_LIMIT),
        cost_estimate=pl.CostEstimate(flops=10*12*length*length*64, bytes_accessed=20*length*width, transcendentals=12*length*length),
    )(lengths, mixed, mixed, mixed, context_grad, context, log_totals)


def side_by_side(rows, groups):
    r = rows.shape[-2] // groups
    return jnp.concatenate(
        [rows[..., i * r : (i + 1) * r, :] for i in range(groups)], axis=-1
    )


def one_below_other(rows, groups):
    w = rows.shape[-1] // groups
    return jnp.concatenate(
        [rows[..., i * w : (i + 1) * w] for i in range(groups)], axis=-2
    )


def whole(part):
    return part.reshape(-1, part.shape[-1])


def shares(full, devices):
    return full.reshape(devices, -1, full.shape[-1]).astype(jnp.bfloat16)


def on_device(
    token_states,
    char_codes,
    lengths,
    token_cotangent,
    char_cotangent,
    char_table,
    recur_input,
    recur_state,
    project_weight,
    output_weight,
    merging_weight,
    up_weight,
    down_weight,
    char_weight,
    attend_gain,
    attend_shift,
    feed_gain,
    feed_shift,
    char_gain,
    char_shift,
):
    count, length, width = token_states.shape
    half = width // 2
    triple = 3 * half
    letters_count, embed_width = char_table.shape
    r = project_weight.shape[0]
    devices = width // r
    ff_blocks = up_weight.shape[1] // width
    low = jnp.bfloat16

    gains = jnp.concatenate(
        [attend_gain, attend_shift, feed_gain, feed_shift, char_gain, char_shift]
    )
    own_table = char_table.T
    gain_rows = jnp.pad(gains[None, :], ((0, own_table.shape[0] - 1), (0, 0)))
    table_rows = jnp.concatenate([own_table, gain_rows], axis=1)
    table_rows = jnp.pad(table_rows, ((0, 0), (0, triple - table_rows.shape[1])))
    first_rows = jnp.concatenate(
        [
            project_weight,
            jnp.concatenate(
                [
                    side_by_side(recur_input.T, 3),
                    side_by_side(recur_state.T, 3),
                    one_below_other(table_rows, 3),
                ],
                axis=1,
            ),
        ],
        axis=0,
    )
    first_all = lax.all_gather(first_rows, AXES, axis=0)
    second_rows = jnp.concatenate(
        [
            output_weight,
            char_weight,
            merging_weight.reshape(-1, width),
            one_below_other(up_weight, ff_blocks),
            down_weight,
        ],
        axis=0,
    )
    second_all = lax.all_gather(second_rows, AXES, axis=0)

    project_full = whole(first_all[:, :r])
    chars_all = first_all[:, r:]
    inlet_full = whole(one_below_other(chars_all[:, :, :width], 3))
    recur_full = whole(one_below_other(chars_all[:, :, width : width + triple], 3))
    table_all = side_by_side(chars_all[:, :, width + triple :], 3)
    table_full = whole(table_all[:, :, :letters_count])
    gains_all = table_all[:, 0, letters_count : letters_count + 6 * r]
    gains_all = gains_all.reshape(devices, 6, r).transpose(1, 0, 2).reshape(6, width)
    gains_all = gains_all.astype(jnp.float32)

    at = 0
    parts = []
    for rows in (r, r) + (merging_weight.shape[1],) * 3 + (ff_blocks * r, down_weight.shape[0]):
        parts.append(second_all[:, at : at + rows])
        at += rows
    output_full, branch_full = whole(parts[0]), whole(parts[1])
    merging_full = [whole(part) for part in parts[2:5]]
    upper_full = whole(side_by_side(parts[5], ff_blocks))
    lower_full = whole(parts[6])

    positions = lax.broadcasted_iota(jnp.int32, (count, length), 1)
    valid = positions < lengths[:, None]
    letters = lax.broadcasted_iota(jnp.int32, (1, 1, letters_count), 2)
    picks = []
    embeds = []
    gates = []
    for slot in range(CHARS):
        picked = (char_codes[:, :, slot][:, :, None] == letters).astype(low)
        embed = back_product(picked, table_full).astype(low)
        picks.append(picked)
        embeds.append(embed)
        gates.append(back_product(embed, inlet_full))
    forward_kept = [None] * CHARS
    state = None
    for slot in range(CHARS):
        state, forward_kept[slot] = cell_forward(
            gates[slot][..., :triple], state, recur_full[:triple], half
        )
    forward_last = state
    backward_kept = [None] * CHARS
    state = None
    for slot in range(CHARS - 1, -1, -1):
        state, backward_kept[slot] = cell_forward(
            gates[slot][..., triple:], state, recur_full[triple:], half
        )
    chars_rep = jnp.concatenate([forward_last, state], axis=-1)
    mixed = product(token_states, project_full).astype(low)[0]
    context_low, log_totals = attend(mixed, lengths, width)
    context_low = context_low[None]
    first_pre = token_states.astype(jnp.float32) + product(context_low, output_full)
    first, pull_first = jax.vjp(norm_apply, first_pre, gains_all[0], gains_all[1])
    joined = jnp.where(
        valid[..., None],
        jnp.concatenate([first.astype(low), chars_rep], axis=-1),
        jnp.zeros((), low),
    )
    merging_pre = (
        shift_down(product(joined, merging_full[0]))
        + product(joined, merging_full[1])
        + shift_up(product(joined, merging_full[2]))
    )
    merged, pull_merged = jax.vjp(exact_gelu, merging_pre)
    summed = first + merged
    summed_low = summed.astype(low)
    hidden, pull_hidden = jax.vjp(exact_gelu, product(summed_low, upper_full))
    hidden_low = hidden.astype(low)
    token_stream, pull_token = jax.vjp(
        norm_apply, summed + product(hidden_low, lower_full), gains_all[2], gains_all[3]
    )
    merged_low = merged.astype(low)
    char_stream, pull_char = jax.vjp(
        norm_apply,
        chars_rep.astype(jnp.float32) + product(merged_low, branch_full),
        gains_all[4],
        gains_all[5],
    )
    token_pre_grad, feed_gain_grad, feed_shift_grad = pull_token(
        token_cotangent.astype(jnp.float32)
    )
    feed_grad = token_pre_grad.astype(low)
    down_grad = outer_sum(hidden_low, feed_grad)
    hidden_grad = pull_hidden(back_product(feed_grad, lower_full))[0].astype(low)
    up_grad = outer_sum(summed_low, hidden_grad)
    summed_grad = token_pre_grad + back_product(hidden_grad, upper_full)
    char_pre_grad, char_gain_grad, char_shift_grad = pull_char(char_cotangent.astype(jnp.float32))
    branch_grad = char_pre_grad.astype(low)
    branch_weight_grad = outer_sum(merged_low, branch_grad)
    merging_grad = pull_merged(summed_grad + back_product(branch_grad, branch_full))[0].astype(low)
    merging_weight_grads = [
        outer_sum(shift_down(joined), merging_grad),
        outer_sum(joined, merging_grad),
        outer_sum(shift_up(joined), merging_grad),
    ]
    early = jnp.concatenate(
        [shares(branch_weight_grad, devices)]
        + [shares(part, devices) for part in merging_weight_grads]
        + [one_below_other(shares(up_grad, devices), ff_blocks)]
        + [shares(down_grad, devices)],
        axis=1,
    )
    early = lax.psum_scatter(early, AXES, scatter_dimension=0, tiled=True)[0]
    joined_grad = (
        shift_up(back_product(merging_grad, merging_full[0]))
        + back_product(merging_grad, merging_full[1])
        + shift_down(back_product(merging_grad, merging_full[2]))
    )
    joined_grad = jnp.where(valid[..., None], joined_grad, 0.0)
    first_grad = summed_grad + joined_grad[..., :width]
    rep_grad = char_pre_grad + joined_grad[..., width:]
    first_pre_grad, attend_gain_grad, attend_shift_grad = pull_first(first_grad)
    attended_grad = first_pre_grad.astype(low)
    output_weight_grad = outer_sum(context_low, attended_grad)
    context_grad = back_product(attended_grad, output_full).astype(low)
    head_grads = attend_back(mixed, context_grad[0], context_low[0], log_totals, lengths, width)
    mixed_grad = jnp.concatenate([head_grads[0], head_grads[1], head_grads[2]], axis=-1)[None]
    project_grad = outer_sum(token_states, mixed_grad)
    input_gradient = (first_pre_grad + back_product(mixed_grad, project_full)).astype(low)
    forward_inputs = [None] * CHARS
    grad_state = rep_grad[..., :half]
    forward_weight_grad = jnp.zeros((triple, half), jnp.float32)
    for slot in range(CHARS - 1, -1, -1):
        grad_in, grad_weight, grad_state = cell_backward(
            grad_state, forward_kept[slot], recur_full[:triple]
        )
        forward_inputs[slot] = grad_in
        if grad_weight is not None:
            forward_weight_grad = forward_weight_grad + grad_weight
    backward_inputs = [None] * CHARS
    grad_state = rep_grad[..., half:]
    backward_weight_grad = jnp.zeros((triple, half), jnp.float32)
    for slot in range(CHARS):
        grad_in, grad_weight, grad_state = cell_backward(
            grad_state, backward_kept[slot], recur_full[triple:]
        )
        backward_inputs[slot] = grad_in
        if grad_weight is not None:
            backward_weight_grad = backward_weight_grad + grad_weight
    recur_weight_grad = jnp.concatenate([forward_weight_grad, backward_weight_grad], axis=0)
    inlet_grad = jnp.zeros(inlet_full.shape, jnp.float32)
    table_grad = jnp.zeros(table_full.shape, jnp.float32)
    for slot in range(CHARS):
        gate_grad = jnp.concatenate([forward_inputs[slot], backward_inputs[slot]], axis=-1).astype(
            low
        )
        inlet_grad = inlet_grad + outer_sum(gate_grad, embeds[slot])
        embed_grad = product(gate_grad, inlet_full).astype(low)
        table_grad = table_grad + outer_sum(embed_grad, picks[slot])
    gain_grads = jnp.stack(
        [
            attend_gain_grad,
            attend_shift_grad,
            feed_gain_grad,
            feed_shift_grad,
            char_gain_grad,
            char_shift_grad,
        ]
    )
    gain_shares = gain_grads.reshape(6, devices, r).transpose(1, 0, 2).reshape(devices, 1, 6 * r)
    table_shares = shares(table_grad, devices)
    gain_shares = jnp.pad(
        gain_shares.astype(low), ((0, 0), (0, table_shares.shape[1] - 1), (0, 0))
    )
    table_shares = jnp.concatenate([table_shares, gain_shares], axis=2)
    table_shares = jnp.pad(
        table_shares, ((0, 0), (0, 0), (0, triple - table_shares.shape[2]))
    )
    late = jnp.concatenate(
        [
            shares(project_grad, devices),
            jnp.concatenate(
                [
                    side_by_side(shares(inlet_grad, devices), 3),
                    side_by_side(shares(recur_weight_grad, devices), 3),
                    one_below_other(table_shares, 3),
                ],
                axis=2,
            ),
            side_by_side(shares(output_weight_grad, devices), 3),
        ],
        axis=1,
    )
    late = lax.psum_scatter(late, AXES, scatter_dimension=0, tiled=True)[0].astype(jnp.float32)
    early = early.astype(jnp.float32)
    own_chars = late[r : 2 * r]
    own_table_rows = side_by_side(own_chars[:, width + triple :], 3)
    own_gains = own_table_rows[0, letters_count : letters_count + 6 * r].reshape(6, r)
    spots = []
    at = 0
    for rows in (r, 3 * merging_weight.shape[1], ff_blocks * r, down_weight.shape[0]):
        spots.append(early[at : at + rows])
        at += rows
    return (
        token_stream.astype(low),
        char_stream.astype(low),
        input_gradient,
        own_table_rows[:, :letters_count].T,
        one_below_other(own_chars[:, :width], 3).T,
        one_below_other(own_chars[:, width : width + triple], 3).T,
        late[:r],
        one_below_other(late[2 * r :], 3),
        spots[1].reshape(merging_weight.shape),
        side_by_side(spots[2], ff_blocks),
        spots[3],
        spots[0],
        own_gains[0],
        own_gains[1],
        own_gains[2],
        own_gains[3],
        own_gains[4],
        own_gains[5],
    )

def solution(mesh):
    placed = (
        P(AXES, None, None),
        P(AXES, None, None),
        P(AXES),
        P(AXES, None, None),
        P(AXES, None, None),
        P(None, AXES),
        P(None, AXES),
        P(None, AXES),
        P(AXES, None),
        P(AXES, None),
        P(None, AXES, None),
        P(AXES, None),
        P(AXES, None),
        P(AXES, None),
        P(AXES),
        P(AXES),
        P(AXES),
        P(AXES),
        P(AXES),
        P(AXES),
    )
    return jax.shard_map(
        on_device,
        mesh=mesh,
        in_specs=placed,
        out_specs=(
            P(AXES, None, None),
            P(AXES, None, None),
            P(AXES, None, None),
            P(None, AXES),
            P(None, AXES),
            P(None, AXES),
            P(AXES, None),
            P(AXES, None),
            P(None, AXES, None),
            P(AXES, None),
            P(AXES, None),
            P(AXES, None),
            P(AXES),
            P(AXES),
            P(AXES),
            P(AXES),
            P(AXES),
            P(AXES),
        ),
        check_vma=False,
    )
```

```python
import functools
import math

import jax
import jax.numpy as jnp
from jax import lax
from jax.experimental import pallas as pl
from jax.experimental.pallas import tpu as pltpu
from jax.sharding import PartitionSpec as P

HEAD_DIM = 64
CHARS = 4
LANES = 128
EPS = 1e-05
MASKED = -1e30
SCALE = 1.0 / math.sqrt(HEAD_DIM)
SCALE2 = math.log2(math.e) / math.sqrt(HEAD_DIM)
AXES = ("dp", "fsdp")
VMEM_LIMIT = 56 * 1024 * 1024

def norm_apply(values, gain, shift):
    average = jnp.mean(values, axis=-1, keepdims=True)
    centred = values - average
    variance = jnp.mean(centred * centred, axis=-1, keepdims=True)
    return centred * lax.rsqrt(variance + EPS) * gain + shift


def product(left, right):
    return jnp.dot(left, right, preferred_element_type=jnp.float32)


def outer_sum(left, right):
    return jnp.einsum("li,lo->io", left, right, preferred_element_type=jnp.float32)


def back_product(grad_rows, weight):
    return jnp.einsum("lo,io->li", grad_rows, weight, preferred_element_type=jnp.float32)


def shift_down(values):
    return jnp.pad(values[:-1], ((1, 0), (0, 0)))


def shift_up(values):
    return jnp.pad(values[1:], ((0, 1), (0, 0)))


def dotf(a,b,ca=1,cb=0):
    return lax.dot_general(a,b,(((ca,),(cb,)),((),())),preferred_element_type=jnp.float32)

def lane_half(shape):
    return lax.broadcasted_iota(jnp.int32, shape, 1) < HEAD_DIM

def attend_kernel(rows, length_ref, q_ref, k_ref, v_ref, ctx_ref, lse_ref, kx_ref, vx_ref):
    length = k_ref.shape[0]
    lane = lax.broadcasted_iota(jnp.int32, (length, LANES), 1)
    place = lax.broadcasted_iota(jnp.int32, (length, LANES), 0)
    kx_ref[:, :LANES] = k_ref[...]
    kx_ref[:, LANES:] = jnp.where((lane == 0) & (place >= length_ref[0]), MASKED, 0.0).astype(jnp.bfloat16)
    vx_ref[:, :LANES] = v_ref[...]
    vx_ref[:, LANES:] = jnp.ones((length, LANES), jnp.bfloat16)
    low = lane_half((rows, LANES))
    one = jnp.where(lax.broadcasted_iota(jnp.int32, (rows, LANES), 1) == 0, 1.0, 0.0).astype(jnp.bfloat16)
    def step(c, _):
        at = pl.ds(pl.multiple_of(c * rows, rows), rows)
        q = q_ref[at, :].astype(jnp.float32)
        outs = []
        for h in range(2):
            mine = low if h == 0 else jnp.logical_not(low)
            qx = jnp.concatenate([jnp.where(mine, q, 0.0).astype(jnp.bfloat16), one], axis=1)
            s = dotf(qx, kx_ref[...], 1, 1)
            peak = jnp.max(s, axis=1, keepdims=True) * SCALE2
            p = jnp.exp2(s * SCALE2 - peak).astype(jnp.bfloat16)
            o = dotf(p, vx_ref[...])
            total = o[:, LANES:]
            outs.append((o[:, :LANES] / total, peak + jnp.log2(total)))
        ctx_ref[at, :] = jnp.where(low, outs[0][0], outs[1][0]).astype(jnp.bfloat16)
        lse_ref[at, :] = jnp.where(low, outs[0][1], outs[1][1])
        return 0
    lax.fori_loop(0, length // rows, step, 0, unroll=True)

def attend(mixed, lengths, width, rows=256):
    length = mixed.shape[0]
    pairs = width // LANES
    spec = lambda o: pl.BlockSpec((length, LANES), lambda p, o=o: (0, p+o))
    return pl.pallas_call(
        functools.partial(attend_kernel, rows),
        grid=(pairs,),
        in_specs=[pl.BlockSpec(memory_space=pltpu.SMEM), spec(0), spec(pairs), spec(2 * pairs)],
        out_specs=[spec(0), spec(0)],
        out_shape=[jax.ShapeDtypeStruct((length, width), jnp.bfloat16), jax.ShapeDtypeStruct((length, width), jnp.float32)],
        scratch_shapes=[pltpu.VMEM((length, 2*LANES), jnp.bfloat16), pltpu.VMEM((length, 2*LANES), jnp.bfloat16)],
        compiler_params=pltpu.CompilerParams(vmem_limit_bytes=VMEM_LIMIT),
        cost_estimate=pl.CostEstimate(flops=4*12*length*length*64, bytes_accessed=10*length*width, transcendentals=12*length*length),
    )(lengths, mixed, mixed, mixed)

def back_kernel(rows, length_ref, q_ref, k_ref, v_ref, do_ref, o_ref, lse_ref, out_ref, kx_ref, vx_ref, qt_ref, dot_ref, dk_ref, dv_ref):
    length = k_ref.shape[0]
    lane = lax.broadcasted_iota(jnp.int32, (length, LANES), 1)
    place = lax.broadcasted_iota(jnp.int32, (length, LANES), 0)
    kx_ref[:, :LANES] = k_ref[...]
    kx_ref[:, LANES:] = jnp.where((lane == 0) & (place >= length_ref[0]), MASKED, 0.0).astype(jnp.bfloat16)
    qt_ref[...] = q_ref[...].T
    dot_ref[...] = do_ref[...].T
    dk_ref[...] = jnp.zeros_like(dk_ref)
    dv_ref[...] = jnp.zeros_like(dv_ref)
    low = lane_half((rows, LANES))
    one = jnp.where(lax.broadcasted_iota(jnp.int32, (rows, LANES), 1) == 0, 1.0, 0.0).astype(jnp.bfloat16)
    def step(c, _):
        at = pl.ds(pl.multiple_of(c * rows, rows), rows)
        q = q_ref[at, :].astype(jnp.float32)
        do = do_ref[at, :].astype(jnp.float32)
        doo = do * o_ref[at, :].astype(jnp.float32)
        lse = lse_ref[at, :]
        dqs = []
        for h in range(2):
            mine = low if h == 0 else jnp.logical_not(low)
            qx = jnp.concatenate([jnp.where(mine, q, 0.0).astype(jnp.bfloat16), one], axis=1)
            s = dotf(qx, kx_ref[...], 1, 1)
            p = jnp.exp2(s * SCALE2 - lse[:, h*HEAD_DIM:h*HEAD_DIM+1])
            dp = dotf(jnp.where(mine, do, 0.0).astype(jnp.bfloat16), v_ref[...], 1, 1)
            delta = jnp.sum(jnp.where(mine, doo, 0.0), axis=1, keepdims=True)
            ds = (p * (dp - delta)).astype(jnp.bfloat16)
            pb = p.astype(jnp.bfloat16)
            hs = slice(h*HEAD_DIM, (h+1)*HEAD_DIM)
            dqs.append(dotf(ds, k_ref[...]))
            dk_ref[hs, :] += dotf(qt_ref[hs, at], ds)
            dv_ref[hs, :] += dotf(dot_ref[hs, at], pb)
        out_ref[0, at, :] = (jnp.where(low, dqs[0], dqs[1]) * SCALE).astype(jnp.bfloat16)
        return 0
    lax.fori_loop(0, length // rows, step, 0, unroll=True)
    out_ref[1] = (dk_ref[...] * SCALE).T.astype(jnp.bfloat16)
    out_ref[2] = dv_ref[...].T.astype(jnp.bfloat16)

def attend_back(mixed, context_grad, context, log_totals, lengths, width, rows=256):
    length = mixed.shape[0]
    pairs = width // LANES
    spec = lambda o: pl.BlockSpec((length, LANES), lambda p, o=o: (0, p+o))
    return pl.pallas_call(
        functools.partial(back_kernel, rows),
        grid=(pairs,),
        in_specs=[pl.BlockSpec(memory_space=pltpu.SMEM), spec(0), spec(pairs), spec(2 * pairs), spec(0), spec(0), spec(0)],
        out_specs=pl.BlockSpec((3, length, LANES), lambda p: (0, 0, p)),
        out_shape=jax.ShapeDtypeStruct((3, length, width), jnp.bfloat16),
        scratch_shapes=[pltpu.VMEM((length, 2*LANES), jnp.bfloat16), pltpu.VMEM((length, 2*LANES), jnp.bfloat16),
            pltpu.VMEM((LANES, length), jnp.bfloat16), pltpu.VMEM((LANES, length), jnp.bfloat16),
            pltpu.VMEM((LANES, length), jnp.float32), pltpu.VMEM((LANES, length), jnp.float32)],
        compiler_params=pltpu.CompilerParams(vmem_limit_bytes=VMEM_LIMIT),
        cost_estimate=pl.CostEstimate(flops=10*12*length*length*64, bytes_accessed=20*length*width, transcendentals=12*length*length),
    )(lengths, mixed, mixed, mixed, context_grad, context, log_totals)


ROOT_HALF = math.sqrt(0.5)
DENSITY = 1.0 / math.sqrt(2.0 * math.pi)

def gelu_both(values):
    below = 0.5 + 0.5 * lax.erf(values * ROOT_HALF)
    return values * below, below + values * (DENSITY * jnp.exp(-0.5 * values * values))

def norm_parts(values):
    average = jnp.mean(values, axis=-1, keepdims=True)
    centred = values - average
    spread = lax.rsqrt(jnp.mean(centred * centred, axis=-1, keepdims=True) + EPS)
    return centred * spread, spread

def norm_back(normed, spread, scaled):
    return spread * (scaled - jnp.mean(scaled, axis=-1, keepdims=True)
                     - normed * jnp.mean(scaled * normed, axis=-1, keepdims=True))

def column_sums(values):
    rows, width = values.shape
    return jnp.sum(values.reshape(rows // 8, 8, width), axis=0)

def chars_kernel(half, codes_ref, table_ref, inlet_ref, recur_ref, embed_ref, rep_ref, states_ref, coef_ref):
    rows = codes_ref.shape[0]
    triple = 3 * half
    width = embed_ref.shape[1] // CHARS
    letters = lax.broadcasted_iota(jnp.int32, (rows, table_ref.shape[1]), 1)
    embeds = []
    for slot in range(CHARS):
        picked = jnp.where(codes_ref[:, slot : slot + 1] == letters, 1.0, 0.0).astype(jnp.bfloat16)
        embed = dotf(picked, table_ref[...], 1, 1).astype(jnp.bfloat16)
        embed_ref[:, slot * width : (slot + 1) * width] = embed
        embeds.append(embed)
    low = jnp.bfloat16
    for side in range(2):
        state = None
        base = side * triple
        order = range(CHARS) if side == 0 else range(CHARS - 1, -1, -1)
        for step, slot in enumerate(order):
            gates = dotf(embeds[slot], inlet_ref[base : base + triple, :], 1, 1)
            if state is None:
                update = jax.nn.sigmoid(gates[:, half : 2 * half])
                fresh = jnp.tanh(gates[:, 2 * half :])
                new = (1.0 - update) * fresh
                coef_ref[side, 0] = ((1.0 - update) * (1.0 - fresh * fresh)).astype(low)
                coef_ref[side, 1] = (-fresh * update * (1.0 - update)).astype(low)
            else:
                recur = dotf(state, recur_ref[base : base + triple, :], 1, 1)
                reset = jax.nn.sigmoid(gates[:, :half] + recur[:, :half])
                update = jax.nn.sigmoid(gates[:, half : 2 * half] + recur[:, half : 2 * half])
                recur_new = recur[:, 2 * half :]
                fresh = jnp.tanh(gates[:, 2 * half :] + reset * recur_new)
                before = state.astype(jnp.float32)
                new = (1.0 - update) * fresh + update * before
                at = 2 + 5 * (step - 1)
                coef_ref[side, at] = ((1.0 - update) * (1.0 - fresh * fresh)).astype(low)
                coef_ref[side, at + 1] = ((before - fresh) * update * (1.0 - update)).astype(low)
                coef_ref[side, at + 2] = (recur_new * reset * (1.0 - reset)).astype(low)
                coef_ref[side, at + 3] = reset.astype(low)
                coef_ref[side, at + 4] = update.astype(low)
            state = new.astype(low)
            if step < CHARS - 1:
                states_ref[side, step] = state
        rep_ref[:, side * half : (side + 1) * half] = state

COEFS = 2 + 5 * (CHARS - 1)

def chars_forward(codes, table, inlet, recur, rows=256):
    length = codes.shape[0]
    embed, half = inlet.shape[1], recur.shape[1]
    low = jnp.bfloat16
    full = lambda a: pl.BlockSpec(a.shape, lambda b: (0, 0))
    return pl.pallas_call(
        functools.partial(chars_kernel, half),
        grid=(length // rows,),
        in_specs=[pl.BlockSpec((rows, CHARS), lambda b: (b, 0)), full(table), full(inlet), full(recur)],
        out_specs=[
            pl.BlockSpec((rows, CHARS * embed), lambda b: (b, 0)),
            pl.BlockSpec((rows, 2 * half), lambda b: (b, 0)),
            pl.BlockSpec((2, CHARS - 1, rows, half), lambda b: (0, 0, b, 0)),
            pl.BlockSpec((2, COEFS, rows, half), lambda b: (0, 0, b, 0)),
        ],
        out_shape=[
            jax.ShapeDtypeStruct((length, CHARS * embed), low),
            jax.ShapeDtypeStruct((length, 2 * half), low),
            jax.ShapeDtypeStruct((2, CHARS - 1, length, half), low),
            jax.ShapeDtypeStruct((2, COEFS, length, half), low),
        ],
        compiler_params=pltpu.CompilerParams(vmem_limit_bytes=VMEM_LIMIT),
        cost_estimate=pl.CostEstimate(flops=12 * 10**9, bytes_accessed=40 * 10**6, transcendentals=10**7),
    )(codes, table, inlet, recur)

def chars_back_kernel(half, codes_ref, inlet_ref, recur_ref, embed_ref, states_ref, coef_ref, grad_ref,
                      table_out, inlet_out, recur_out, gates_ref, lets_ref, table_acc, inlet_acc, recur_acc):
    rows = codes_ref.shape[0]
    triple = 3 * half
    width = embed_ref.shape[1] // CHARS
    low = jnp.bfloat16
    first, last = pl.program_id(0) == 0, pl.program_id(0) == pl.num_programs(0) - 1

    @pl.when(first)
    def _():
        table_acc[...] = jnp.zeros_like(table_acc)
        inlet_acc[...] = jnp.zeros_like(inlet_acc)
        recur_acc[...] = jnp.zeros_like(recur_acc)

    for side in range(2):
        grad = grad_ref[:, side * half : (side + 1) * half]
        base = side * triple
        order = range(CHARS) if side == 0 else range(CHARS - 1, -1, -1)
        for step, slot in reversed(list(enumerate(order))):
            at = 2 + 5 * (step - 1) if step else 0
            load = lambda k: coef_ref[side, at + k].astype(jnp.float32)
            fresh_pre = grad * load(0)
            update_pre = grad * load(1)
            spot = slice(slot * rows, (slot + 1) * rows)
            gates_ref[spot, base + half : base + 2 * half] = update_pre.astype(low)
            gates_ref[spot, base + 2 * half : base + triple] = fresh_pre.astype(low)
            if step == 0:
                gates_ref[spot, base : base + half] = jnp.zeros((rows, half), low)
                continue
            reset_pre = fresh_pre * load(2)
            gates_ref[spot, base : base + half] = reset_pre.astype(low)
            recur_grad = jnp.concatenate(
                [reset_pre.astype(low), update_pre.astype(low), (fresh_pre * load(3)).astype(low)], axis=1)
            recur_acc[base : base + triple, :] += dotf(recur_grad, states_ref[side, step - 1], 0, 0)
            grad = grad * load(4) + dotf(recur_grad, recur_ref[base : base + triple, :])
    embed_all = jnp.concatenate([embed_ref[:, j * width : (j + 1) * width] for j in range(CHARS)], axis=0)
    inlet_acc[...] += dotf(gates_ref[...], embed_all, 0, 0)
    embed_grad = dotf(gates_ref[...], inlet_ref[...]).astype(low)
    letters = lax.broadcasted_iota(jnp.int32, (rows, table_acc.shape[1]), 1)
    for slot in range(CHARS):
        lets_ref[slot * rows : (slot + 1) * rows, :] = jnp.where(
            codes_ref[:, slot : slot + 1] == letters, 1.0, 0.0).astype(low)
    table_acc[...] += dotf(embed_grad, lets_ref[...], 0, 0)

    @pl.when(last)
    def _():
        table_out[...] = table_acc[...].astype(low)
        inlet_out[...] = inlet_acc[...].astype(low)
        recur_out[...] = recur_acc[...].astype(low)

def chars_back(codes, inlet, recur, embeds, states, coefs, grad, letters, rows=256):
    length = codes.shape[0]
    embed, half = inlet.shape[1], recur.shape[1]
    low = jnp.bfloat16
    full = lambda a: pl.BlockSpec(a.shape, lambda b: (0, 0))
    outs = [(embed, letters), inlet.shape, recur.shape]
    return pl.pallas_call(
        functools.partial(chars_back_kernel, half),
        grid=(length // rows,),
        in_specs=[
            pl.BlockSpec((rows, CHARS), lambda b: (b, 0)), full(inlet), full(recur),
            pl.BlockSpec((rows, CHARS * embed), lambda b: (b, 0)),
            pl.BlockSpec((2, CHARS - 1, rows, half), lambda b: (0, 0, b, 0)),
            pl.BlockSpec((2, COEFS, rows, half), lambda b: (0, 0, b, 0)),
            pl.BlockSpec((rows, 2 * half), lambda b: (b, 0)),
        ],
        out_specs=[pl.BlockSpec(s, lambda b: (0, 0)) for s in outs],
        out_shape=[jax.ShapeDtypeStruct(s, low) for s in outs],
        scratch_shapes=[
            pltpu.VMEM((CHARS * rows, 6 * half), low), pltpu.VMEM((CHARS * rows, letters), low),
            ] + [pltpu.VMEM(s, jnp.float32) for s in outs],
        compiler_params=pltpu.CompilerParams(vmem_limit_bytes=VMEM_LIMIT),
        cost_estimate=pl.CostEstimate(flops=22 * 10**9, bytes_accessed=40 * 10**6, transcendentals=0),
    )(codes, inlet, recur, embeds, states, coefs, grad)

def feed_kernel(blocks, joined_ref, first_ref, rep_ref, token_cot_ref, char_cot_ref, gains_ref,
                merging_ref, up_ref, down_ref, branch_ref,
                token_ref, char_ref, summed_ref, merged_ref, hidden_ref, feed_grad_ref, hidden_grad_ref,
                branch_grad_ref, merging_grad_ref, summed_grad_ref, char_grad_ref, sums_ref, slope_ref):
    low = jnp.bfloat16
    width = first_ref.shape[1]
    step = up_ref.shape[1] // blocks

    @pl.when(pl.program_id(0) == 0)
    def _():
        sums_ref[...] = jnp.zeros_like(sums_ref)

    merged, merging_slope = gelu_both(dotf(joined_ref[...], merging_ref[...]))
    merged_low = merged.astype(low)
    merged_ref[...] = merged_low
    summed = first_ref[...] + merged
    summed_low = summed.astype(low)
    summed_ref[...] = summed_low
    total = summed
    for c in range(blocks):
        cols = slice(c * step, (c + 1) * step)
        hidden, slope = gelu_both(dotf(summed_low, up_ref[:, cols]))
        slope_ref[:, cols] = slope
        hidden_low = hidden.astype(low)
        hidden_ref[:, cols] = hidden_low
        total = total + dotf(hidden_low, down_ref[cols, :])
    normed, spread = norm_parts(total)
    gain, shift = gains_ref[2:3, :], gains_ref[3:4, :]
    token_ref[...] = (normed * gain + shift).astype(low)
    cot = token_cot_ref[...].astype(jnp.float32)
    sums_ref[0] += column_sums(cot * normed)
    sums_ref[1] += column_sums(cot)
    token_grad = norm_back(normed, spread, cot * gain)
    feed_grad = token_grad.astype(low)
    feed_grad_ref[...] = feed_grad
    total = token_grad
    for c in range(blocks):
        cols = slice(c * step, (c + 1) * step)
        hidden_grad = (slope_ref[:, cols] * dotf(feed_grad, down_ref[cols, :], 1, 1)).astype(low)
        hidden_grad_ref[:, cols] = hidden_grad
        total = total + dotf(hidden_grad, up_ref[:, cols], 1, 1)
    summed_grad_ref[...] = total
    normed, spread = norm_parts(rep_ref[...].astype(jnp.float32) + dotf(merged_low, branch_ref[...]))
    gain, shift = gains_ref[4:5, :], gains_ref[5:6, :]
    char_ref[...] = (normed * gain + shift).astype(low)
    cot = char_cot_ref[...].astype(jnp.float32)
    sums_ref[2] += column_sums(cot * normed)
    sums_ref[3] += column_sums(cot)
    char_grad = norm_back(normed, spread, cot * gain)
    char_grad_ref[...] = char_grad
    branch_grad = char_grad.astype(low)
    branch_grad_ref[...] = branch_grad
    merging_grad_ref[...] = (merging_slope * (total + dotf(branch_grad, branch_ref[...], 1, 1))).astype(low)

def feed(joined, first, rep, token_cot, char_cot, gains, merging, up, down, branch, rows=256, blocks=2):
    length, width = first.shape
    ff = up.shape[1]
    low, wide = jnp.bfloat16, jnp.float32
    row = lambda w: pl.BlockSpec((rows, w), lambda b: (b, 0))
    full = lambda a: pl.BlockSpec(a.shape, lambda b: (0, 0), pipeline_mode=pl.Buffered(1))
    outs = [(width, low), (width, low), (width, low), (width, low), (ff, low), (width, low), (ff, low),
            (width, low), (width, low), (width, wide), (width, wide)]
    return pl.pallas_call(
        functools.partial(feed_kernel, blocks),
        grid=(length // rows,),
        in_specs=[row(joined.shape[1]), row(width), row(width), row(width), row(width), full(gains),
                  full(merging), full(up), full(down), full(branch)],
        out_specs=[row(w) for w, _ in outs] + [pl.BlockSpec((4, 8, width), lambda b: (0, 0, 0))],
        out_shape=[jax.ShapeDtypeStruct((length, w), t) for w, t in outs] + [jax.ShapeDtypeStruct((4, 8, width), wide)],
        scratch_shapes=[pltpu.VMEM((rows, ff), wide)],
        compiler_params=pltpu.CompilerParams(vmem_limit_bytes=VMEM_LIMIT),
        cost_estimate=pl.CostEstimate(flops=30 * 10**9, bytes_accessed=70 * 10**6, transcendentals=10**7),
    )(joined, first, rep, token_cot, char_cot, gains, merging, up, down, branch)


def side_by_side(rows, groups):
    r = rows.shape[-2] // groups
    return jnp.concatenate(
        [rows[..., i * r : (i + 1) * r, :] for i in range(groups)], axis=-1
    )


def one_below_other(rows, groups):
    w = rows.shape[-1] // groups
    return jnp.concatenate(
        [rows[..., i * w : (i + 1) * w] for i in range(groups)], axis=-2
    )


def whole(part):
    return part.reshape(-1, part.shape[-1])


def shares(full, devices):
    return full.reshape(devices, -1, full.shape[-1]).astype(jnp.bfloat16)


def on_device(
    token_states,
    char_codes,
    lengths,
    token_cotangent,
    char_cotangent,
    char_table,
    recur_input,
    recur_state,
    project_weight,
    output_weight,
    merging_weight,
    up_weight,
    down_weight,
    char_weight,
    attend_gain,
    attend_shift,
    feed_gain,
    feed_shift,
    char_gain,
    char_shift,
):
    length, width = token_states.shape[1:]
    half = width // 2
    triple = 3 * half
    letters_count = char_table.shape[0]
    r = project_weight.shape[0]
    devices = width // r
    ff_blocks = up_weight.shape[1] // width
    low = jnp.bfloat16

    gains = jnp.concatenate(
        [attend_gain, attend_shift, feed_gain, feed_shift, char_gain, char_shift]
    )
    own_table = char_table.T
    gain_rows = jnp.pad(gains[None, :], ((0, own_table.shape[0] - 1), (0, 0)))
    table_rows = jnp.concatenate([own_table, gain_rows], axis=1)
    table_rows = jnp.pad(table_rows, ((0, 0), (0, triple - table_rows.shape[1])))
    first_rows = jnp.concatenate(
        [
            project_weight,
            jnp.concatenate(
                [
                    side_by_side(recur_input.T, 3),
                    side_by_side(recur_state.T, 3),
                    one_below_other(table_rows, 3),
                ],
                axis=1,
            ),
        ],
        axis=0,
    )
    first_all = lax.all_gather(first_rows, AXES, axis=0)
    second_rows = jnp.concatenate(
        [
            output_weight,
            char_weight,
            merging_weight.reshape(-1, width),
            one_below_other(up_weight, ff_blocks),
            down_weight,
        ],
        axis=0,
    )
    second_all = lax.all_gather(second_rows, AXES, axis=0)

    project_full = whole(first_all[:, :r])
    chars_all = first_all[:, r:]
    inlet_full = whole(one_below_other(chars_all[:, :, :width], 3))
    recur_full = whole(one_below_other(chars_all[:, :, width : width + triple], 3))
    table_all = side_by_side(chars_all[:, :, width + triple :], 3)
    table_full = whole(table_all[:, :, : pl.cdiv(letters_count, LANES) * LANES])
    gains_all = table_all[:, 0, letters_count : letters_count + 6 * r]
    gains_all = gains_all.reshape(devices, 6, r).transpose(1, 0, 2).reshape(6, width)
    gains_all = gains_all.astype(jnp.float32)

    at = 0
    parts = []
    for rows in (r, r) + (merging_weight.shape[1],) * 3 + (ff_blocks * r, down_weight.shape[0]):
        parts.append(second_all[:, at : at + rows])
        at += rows
    output_full, branch_full = whole(parts[0]), whole(parts[1])
    merging_full = [whole(part) for part in parts[2:5]]
    upper_full = whole(side_by_side(parts[5], ff_blocks))
    lower_full = whole(parts[6])

    states, codes = token_states[0], char_codes[0]
    valid = lax.broadcasted_iota(jnp.int32, (length, 1), 0) < lengths
    embeds, chars_rep, char_states, coefs = chars_forward(
        codes, table_full, inlet_full, recur_full
    )
    mixed = product(states, project_full).astype(low)
    context_low, log_totals = attend(mixed, lengths, width)
    first_pre = states.astype(jnp.float32) + product(context_low, output_full)
    first, pull_first = jax.vjp(norm_apply, first_pre, gains_all[0], gains_all[1])
    joined = jnp.where(
        valid, jnp.concatenate([first.astype(low), chars_rep], axis=-1), jnp.zeros((), low)
    )
    joined = jnp.concatenate([shift_down(joined), joined, shift_up(joined)], axis=1)
    (
        token_stream,
        char_stream,
        summed_low,
        merged_low,
        hidden_low,
        feed_grad,
        hidden_grad,
        branch_grad,
        merging_grad,
        summed_grad,
        char_pre_grad,
        gain_sums,
    ) = feed(
        joined,
        first,
        chars_rep,
        token_cotangent[0],
        char_cotangent[0],
        gains_all,
        jnp.concatenate(merging_full, axis=0),
        upper_full,
        lower_full,
        branch_full,
    )
    feed_gain_grad, feed_shift_grad, char_gain_grad, char_shift_grad = jnp.sum(gain_sums, axis=1)
    early = jnp.concatenate(
        [shares(outer_sum(merged_low, branch_grad), devices)]
        + [
            shares(outer_sum(joined[:, 2 * i * width : 2 * (i + 1) * width], merging_grad), devices)
            for i in range(3)
        ]
        + [one_below_other(shares(outer_sum(summed_low, hidden_grad), devices), ff_blocks)]
        + [shares(outer_sum(hidden_low, feed_grad), devices)],
        axis=1,
    )
    early, merging_grad = lax.optimization_barrier((early, merging_grad))
    early = lax.psum_scatter(early, AXES, scatter_dimension=0, tiled=True)[0]
    joined_grad = (
        shift_up(back_product(merging_grad, merging_full[0]))
        + back_product(merging_grad, merging_full[1])
        + shift_down(back_product(merging_grad, merging_full[2]))
    )
    joined_grad = jnp.where(valid, joined_grad, 0.0)
    first_grad = summed_grad + joined_grad[:, :width]
    rep_grad = char_pre_grad + joined_grad[:, width:]
    first_pre_grad, attend_gain_grad, attend_shift_grad = pull_first(first_grad)
    table_grad, inlet_grad, recur_weight_grad = chars_back(
        codes, inlet_full, recur_full, embeds, char_states, coefs, rep_grad, table_full.shape[1]
    )
    attended_grad = first_pre_grad.astype(low)
    output_weight_grad = outer_sum(context_low, attended_grad)
    context_grad = back_product(attended_grad, output_full).astype(low)
    head_grads = attend_back(mixed, context_grad, context_low, log_totals, lengths, width)
    mixed_grad = jnp.concatenate([head_grads[0], head_grads[1], head_grads[2]], axis=-1)
    project_grad = outer_sum(states, mixed_grad)
    input_gradient = (first_pre_grad + back_product(mixed_grad, project_full)).astype(low)
    gain_grads = jnp.stack(
        [
            attend_gain_grad,
            attend_shift_grad,
            feed_gain_grad,
            feed_shift_grad,
            char_gain_grad,
            char_shift_grad,
        ]
    )
    gain_shares = gain_grads.reshape(6, devices, r).transpose(1, 0, 2).reshape(devices, 1, 6 * r)
    table_shares = shares(table_grad, devices)[:, :, :letters_count]
    gain_shares = jnp.pad(
        gain_shares.astype(low), ((0, 0), (0, table_shares.shape[1] - 1), (0, 0))
    )
    table_shares = jnp.concatenate([table_shares, gain_shares], axis=2)
    table_shares = jnp.pad(
        table_shares, ((0, 0), (0, 0), (0, triple - table_shares.shape[2]))
    )
    late = jnp.concatenate(
        [
            shares(project_grad, devices),
            jnp.concatenate(
                [
                    side_by_side(shares(inlet_grad, devices), 3),
                    side_by_side(shares(recur_weight_grad, devices), 3),
                    one_below_other(table_shares, 3),
                ],
                axis=2,
            ),
            side_by_side(shares(output_weight_grad, devices), 3),
        ],
        axis=1,
    )
    late = lax.psum_scatter(late, AXES, scatter_dimension=0, tiled=True)[0].astype(jnp.float32)
    early = early.astype(jnp.float32)
    own_chars = late[r : 2 * r]
    own_table_rows = side_by_side(own_chars[:, width + triple :], 3)
    own_gains = own_table_rows[0, letters_count : letters_count + 6 * r].reshape(6, r)
    spots = []
    at = 0
    for rows in (r, 3 * merging_weight.shape[1], ff_blocks * r, down_weight.shape[0]):
        spots.append(early[at : at + rows])
        at += rows
    return (
        token_stream[None],
        char_stream[None],
        input_gradient[None],
        own_table_rows[:, :letters_count].T,
        one_below_other(own_chars[:, :width], 3).T,
        one_below_other(own_chars[:, width : width + triple], 3).T,
        late[:r],
        one_below_other(late[2 * r :], 3),
        spots[1].reshape(merging_weight.shape),
        side_by_side(spots[2], ff_blocks),
        spots[3],
        spots[0],
        own_gains[0],
        own_gains[1],
        own_gains[2],
        own_gains[3],
        own_gains[4],
        own_gains[5],
    )

def solution(mesh):
    placed = (
        P(AXES, None, None),
        P(AXES, None, None),
        P(AXES),
        P(AXES, None, None),
        P(AXES, None, None),
        P(None, AXES),
        P(None, AXES),
        P(None, AXES),
        P(AXES, None),
        P(AXES, None),
        P(None, AXES, None),
        P(AXES, None),
        P(AXES, None),
        P(AXES, None),
        P(AXES),
        P(AXES),
        P(AXES),
        P(AXES),
        P(AXES),
        P(AXES),
    )
    return jax.shard_map(
        on_device,
        mesh=mesh,
        in_specs=placed,
        out_specs=(
            P(AXES, None, None),
            P(AXES, None, None),
            P(AXES, None, None),
            P(None, AXES),
            P(None, AXES),
            P(None, AXES),
            P(AXES, None),
            P(AXES, None),
            P(None, AXES, None),
            P(AXES, None),
            P(AXES, None),
            P(AXES, None),
            P(AXES),
            P(AXES),
            P(AXES),
            P(AXES),
            P(AXES),
            P(AXES),
        ),
        check_vma=False,
    )
```

```python
import functools
import itertools
import math

import jax
import jax.numpy as jnp
from jax import lax
from jax.experimental import pallas as pl
from jax.experimental.pallas import tpu as pltpu
from jax.sharding import PartitionSpec as P

HEAD_DIM = 64
CHARS = 4
LANES = 128
EPS = 1e-05
MASKED = -1e30
SCALE = 1.0 / math.sqrt(HEAD_DIM)
SCALE2 = math.log2(math.e) / math.sqrt(HEAD_DIM)
AXES = ("dp", "fsdp")
VMEM_LIMIT = 56 * 1024 * 1024

def norm_apply(values, gain, shift):
    average = jnp.mean(values, axis=-1, keepdims=True)
    centred = values - average
    variance = jnp.mean(centred * centred, axis=-1, keepdims=True)
    return centred * lax.rsqrt(variance + EPS) * gain + shift


def product(left, right):
    return jnp.dot(left, right, preferred_element_type=jnp.float32)


def outer_sum(left, right):
    return jnp.einsum("li,lo->io", left, right, preferred_element_type=jnp.float32)


def back_product(grad_rows, weight):
    return jnp.einsum("lo,io->li", grad_rows, weight, preferred_element_type=jnp.float32)


def shift_down(values):
    return jnp.pad(values[:-1], ((1, 0), (0, 0)))


def shift_up(values):
    return jnp.pad(values[1:], ((0, 1), (0, 0)))


def dotf(a,b,ca=1,cb=0):
    return lax.dot_general(a,b,(((ca,),(cb,)),((),())),preferred_element_type=jnp.float32)

def lane_half(shape):
    return lax.broadcasted_iota(jnp.int32, shape, 1) < HEAD_DIM

def attend_kernel(rows, length_ref, q_ref, k_ref, v_ref, ctx_ref, lse_ref, kx_ref, vx_ref):
    length = k_ref.shape[0]
    lane = lax.broadcasted_iota(jnp.int32, (length, LANES), 1)
    place = lax.broadcasted_iota(jnp.int32, (length, LANES), 0)
    kx_ref[:, :LANES] = k_ref[...]
    kx_ref[:, LANES:] = jnp.where((lane == 0) & (place >= length_ref[0]), MASKED, 0.0).astype(jnp.bfloat16)
    vx_ref[:, :LANES] = v_ref[...]
    vx_ref[:, LANES:] = jnp.ones((length, LANES), jnp.bfloat16)
    low = lane_half((rows, LANES))
    one = jnp.where(lax.broadcasted_iota(jnp.int32, (rows, LANES), 1) == 0, 1.0, 0.0).astype(jnp.bfloat16)
    def step(c, _):
        at = pl.ds(pl.multiple_of(c * rows, rows), rows)
        q = q_ref[at, :].astype(jnp.float32)
        outs = []
        for h in range(2):
            mine = low if h == 0 else jnp.logical_not(low)
            qx = jnp.concatenate([jnp.where(mine, q, 0.0).astype(jnp.bfloat16), one], axis=1)
            s = dotf(qx, kx_ref[...], 1, 1)
            peak = jnp.max(s, axis=1, keepdims=True) * SCALE2
            p = jnp.exp2(s * SCALE2 - peak).astype(jnp.bfloat16)
            o = dotf(p, vx_ref[...])
            total = o[:, LANES:]
            outs.append((o[:, :LANES] / total, peak + jnp.log2(total)))
        ctx_ref[at, :] = jnp.where(low, outs[0][0], outs[1][0]).astype(jnp.bfloat16)
        lse_ref[at, :] = jnp.where(low, outs[0][1], outs[1][1])
        return 0
    lax.fori_loop(0, length // rows, step, 0, unroll=True)

def attend(mixed, lengths, width, rows=256):
    length = mixed.shape[0]
    pairs = width // LANES
    spec = lambda o: pl.BlockSpec((length, LANES), lambda p, o=o: (0, p+o))
    return pl.pallas_call(
        functools.partial(attend_kernel, rows),
        grid=(pairs,),
        in_specs=[pl.BlockSpec(memory_space=pltpu.SMEM), spec(0), spec(pairs), spec(2 * pairs)],
        out_specs=[spec(0), spec(0)],
        out_shape=[jax.ShapeDtypeStruct((length, width), jnp.bfloat16), jax.ShapeDtypeStruct((length, width), jnp.float32)],
        scratch_shapes=[pltpu.VMEM((length, 2*LANES), jnp.bfloat16), pltpu.VMEM((length, 2*LANES), jnp.bfloat16)],
        compiler_params=pltpu.CompilerParams(vmem_limit_bytes=VMEM_LIMIT),
        cost_estimate=pl.CostEstimate(flops=4*12*length*length*64, bytes_accessed=10*length*width, transcendentals=12*length*length),
    )(lengths, mixed, mixed, mixed)

def back_kernel(rows, length_ref, q_ref, k_ref, v_ref, do_ref, o_ref, lse_ref, out_ref, kx_ref, vx_ref, qt_ref, dot_ref, dk_ref, dv_ref):
    length = k_ref.shape[0]
    lane = lax.broadcasted_iota(jnp.int32, (length, LANES), 1)
    place = lax.broadcasted_iota(jnp.int32, (length, LANES), 0)
    kx_ref[:, :LANES] = k_ref[...]
    kx_ref[:, LANES:] = jnp.where((lane == 0) & (place >= length_ref[0]), MASKED, 0.0).astype(jnp.bfloat16)
    qt_ref[...] = q_ref[...].T
    dot_ref[...] = do_ref[...].T
    dk_ref[...] = jnp.zeros_like(dk_ref)
    dv_ref[...] = jnp.zeros_like(dv_ref)
    low = lane_half((rows, LANES))
    one = jnp.where(lax.broadcasted_iota(jnp.int32, (rows, LANES), 1) == 0, 1.0, 0.0).astype(jnp.bfloat16)
    def step(c, _):
        at = pl.ds(pl.multiple_of(c * rows, rows), rows)
        q = q_ref[at, :].astype(jnp.float32)
        do = do_ref[at, :].astype(jnp.float32)
        doo = do * o_ref[at, :].astype(jnp.float32)
        lse = lse_ref[at, :]
        dqs = []
        for h in range(2):
            mine = low if h == 0 else jnp.logical_not(low)
            qx = jnp.concatenate([jnp.where(mine, q, 0.0).astype(jnp.bfloat16), one], axis=1)
            s = dotf(qx, kx_ref[...], 1, 1)
            p = jnp.exp2(s * SCALE2 - lse[:, h*HEAD_DIM:h*HEAD_DIM+1])
            dp = dotf(jnp.where(mine, do, 0.0).astype(jnp.bfloat16), v_ref[...], 1, 1)
            delta = jnp.sum(jnp.where(mine, doo, 0.0), axis=1, keepdims=True)
            ds = (p * (dp - delta)).astype(jnp.bfloat16)
            pb = p.astype(jnp.bfloat16)
            hs = slice(h*HEAD_DIM, (h+1)*HEAD_DIM)
            dqs.append(dotf(ds, k_ref[...]))
            dk_ref[hs, :] += dotf(qt_ref[hs, at], ds)
            dv_ref[hs, :] += dotf(dot_ref[hs, at], pb)
        out_ref[0, at, :] = (jnp.where(low, dqs[0], dqs[1]) * SCALE).astype(jnp.bfloat16)
        return 0
    lax.fori_loop(0, length // rows, step, 0, unroll=True)
    out_ref[1] = (dk_ref[...] * SCALE).T.astype(jnp.bfloat16)
    out_ref[2] = dv_ref[...].T.astype(jnp.bfloat16)

def attend_back(mixed, context_grad, context, log_totals, lengths, width, rows=256):
    length = mixed.shape[0]
    pairs = width // LANES
    spec = lambda o: pl.BlockSpec((length, LANES), lambda p, o=o: (0, p+o))
    return pl.pallas_call(
        functools.partial(back_kernel, rows),
        grid=(pairs,),
        in_specs=[pl.BlockSpec(memory_space=pltpu.SMEM), spec(0), spec(pairs), spec(2 * pairs), spec(0), spec(0), spec(0)],
        out_specs=pl.BlockSpec((3, length, LANES), lambda p: (0, 0, p)),
        out_shape=jax.ShapeDtypeStruct((3, length, width), jnp.bfloat16),
        scratch_shapes=[pltpu.VMEM((length, 2*LANES), jnp.bfloat16), pltpu.VMEM((length, 2*LANES), jnp.bfloat16),
            pltpu.VMEM((LANES, length), jnp.bfloat16), pltpu.VMEM((LANES, length), jnp.bfloat16),
            pltpu.VMEM((LANES, length), jnp.float32), pltpu.VMEM((LANES, length), jnp.float32)],
        compiler_params=pltpu.CompilerParams(vmem_limit_bytes=VMEM_LIMIT),
        cost_estimate=pl.CostEstimate(flops=10*12*length*length*64, bytes_accessed=20*length*width, transcendentals=12*length*length),
    )(lengths, mixed, mixed, mixed, context_grad, context, log_totals)


ROOT_HALF = math.sqrt(0.5)
DENSITY = 1.0 / math.sqrt(2.0 * math.pi)

def gelu_both(values):
    below = 0.5 + 0.5 * lax.erf(values * ROOT_HALF)
    return values * below, below + values * (DENSITY * jnp.exp(-0.5 * values * values))

def norm_parts(values):
    average = jnp.mean(values, axis=-1, keepdims=True)
    centred = values - average
    spread = lax.rsqrt(jnp.mean(centred * centred, axis=-1, keepdims=True) + EPS)
    return centred * spread, spread

def norm_back(normed, spread, scaled):
    return spread * (scaled - jnp.mean(scaled, axis=-1, keepdims=True)
                     - normed * jnp.mean(scaled * normed, axis=-1, keepdims=True))

def column_sums(values):
    rows, width = values.shape
    return jnp.sum(values.reshape(rows // 8, 8, width), axis=0)

def chars_kernel(half, codes_ref, table_ref, inlet_ref, recur_ref, embed_ref, rep_ref, states_ref, coef_ref):
    rows = codes_ref.shape[0]
    triple = 3 * half
    width = embed_ref.shape[1] // CHARS
    letters = lax.broadcasted_iota(jnp.int32, (rows, table_ref.shape[1]), 1)
    embeds = []
    for slot in range(CHARS):
        picked = jnp.where(codes_ref[:, slot : slot + 1] == letters, 1.0, 0.0).astype(jnp.bfloat16)
        embed = dotf(picked, table_ref[...], 1, 1).astype(jnp.bfloat16)
        embed_ref[:, slot * width : (slot + 1) * width] = embed
        embeds.append(embed)
    low = jnp.bfloat16
    for side in range(2):
        state = None
        base = side * triple
        order = range(CHARS) if side == 0 else range(CHARS - 1, -1, -1)
        for step, slot in enumerate(order):
            gates = dotf(embeds[slot], inlet_ref[base : base + triple, :], 1, 1)
            if state is None:
                update = jax.nn.sigmoid(gates[:, half : 2 * half])
                fresh = jnp.tanh(gates[:, 2 * half :])
                new = (1.0 - update) * fresh
                coef_ref[side, 0] = ((1.0 - update) * (1.0 - fresh * fresh)).astype(low)
                coef_ref[side, 1] = (-fresh * update * (1.0 - update)).astype(low)
            else:
                recur = dotf(state, recur_ref[base : base + triple, :], 1, 1)
                reset = jax.nn.sigmoid(gates[:, :half] + recur[:, :half])
                update = jax.nn.sigmoid(gates[:, half : 2 * half] + recur[:, half : 2 * half])
                recur_new = recur[:, 2 * half :]
                fresh = jnp.tanh(gates[:, 2 * half :] + reset * recur_new)
                before = state.astype(jnp.float32)
                new = (1.0 - update) * fresh + update * before
                at = 2 + 5 * (step - 1)
                coef_ref[side, at] = ((1.0 - update) * (1.0 - fresh * fresh)).astype(low)
                coef_ref[side, at + 1] = ((before - fresh) * update * (1.0 - update)).astype(low)
                coef_ref[side, at + 2] = (recur_new * reset * (1.0 - reset)).astype(low)
                coef_ref[side, at + 3] = reset.astype(low)
                coef_ref[side, at + 4] = update.astype(low)
            state = new.astype(low)
            if step < CHARS - 1:
                states_ref[side, step] = state
        rep_ref[:, side * half : (side + 1) * half] = state

COEFS = 2 + 5 * (CHARS - 1)

def chars_forward(codes, table, inlet, recur, rows=256):
    length = codes.shape[0]
    embed, half = inlet.shape[1], recur.shape[1]
    low = jnp.bfloat16
    full = lambda a: pl.BlockSpec(a.shape, lambda b: (0, 0))
    return pl.pallas_call(
        functools.partial(chars_kernel, half),
        grid=(length // rows,),
        in_specs=[pl.BlockSpec((rows, CHARS), lambda b: (b, 0)), full(table), full(inlet), full(recur)],
        out_specs=[
            pl.BlockSpec((rows, CHARS * embed), lambda b: (b, 0)),
            pl.BlockSpec((rows, 2 * half), lambda b: (b, 0)),
            pl.BlockSpec((2, CHARS - 1, rows, half), lambda b: (0, 0, b, 0)),
            pl.BlockSpec((2, COEFS, rows, half), lambda b: (0, 0, b, 0)),
        ],
        out_shape=[
            jax.ShapeDtypeStruct((length, CHARS * embed), low),
            jax.ShapeDtypeStruct((length, 2 * half), low),
            jax.ShapeDtypeStruct((2, CHARS - 1, length, half), low),
            jax.ShapeDtypeStruct((2, COEFS, length, half), low),
        ],
        compiler_params=pltpu.CompilerParams(vmem_limit_bytes=VMEM_LIMIT),
        cost_estimate=pl.CostEstimate(flops=12 * 10**9, bytes_accessed=40 * 10**6, transcendentals=10**7),
    )(codes, table, inlet, recur)

def chars_back_kernel(half, codes_ref, inlet_ref, recur_ref, embed_ref, states_ref, coef_ref, grad_ref,
                      table_out, inlet_out, recur_out, gates_ref, lets_ref, table_acc, inlet_acc, recur_acc):
    rows = codes_ref.shape[0]
    triple = 3 * half
    width = embed_ref.shape[1] // CHARS
    low = jnp.bfloat16
    first, last = pl.program_id(0) == 0, pl.program_id(0) == pl.num_programs(0) - 1

    @pl.when(first)
    def _():
        table_acc[...] = jnp.zeros_like(table_acc)
        inlet_acc[...] = jnp.zeros_like(inlet_acc)
        recur_acc[...] = jnp.zeros_like(recur_acc)

    for side in range(2):
        grad = grad_ref[:, side * half : (side + 1) * half]
        base = side * triple
        order = range(CHARS) if side == 0 else range(CHARS - 1, -1, -1)
        for step, slot in reversed(list(enumerate(order))):
            at = 2 + 5 * (step - 1) if step else 0
            load = lambda k: coef_ref[side, at + k].astype(jnp.float32)
            fresh_pre = grad * load(0)
            update_pre = grad * load(1)
            spot = slice(slot * rows, (slot + 1) * rows)
            gates_ref[spot, base + half : base + 2 * half] = update_pre.astype(low)
            gates_ref[spot, base + 2 * half : base + triple] = fresh_pre.astype(low)
            if step == 0:
                gates_ref[spot, base : base + half] = jnp.zeros((rows, half), low)
                continue
            reset_pre = fresh_pre * load(2)
            gates_ref[spot, base : base + half] = reset_pre.astype(low)
            recur_grad = jnp.concatenate(
                [reset_pre.astype(low), update_pre.astype(low), (fresh_pre * load(3)).astype(low)], axis=1)
            recur_acc[base : base + triple, :] += dotf(recur_grad, states_ref[side, step - 1], 0, 0)
            grad = grad * load(4) + dotf(recur_grad, recur_ref[base : base + triple, :])
    embed_all = jnp.concatenate([embed_ref[:, j * width : (j + 1) * width] for j in range(CHARS)], axis=0)
    inlet_acc[...] += dotf(gates_ref[...], embed_all, 0, 0)
    embed_grad = dotf(gates_ref[...], inlet_ref[...]).astype(low)
    letters = lax.broadcasted_iota(jnp.int32, (rows, table_acc.shape[1]), 1)
    for slot in range(CHARS):
        lets_ref[slot * rows : (slot + 1) * rows, :] = jnp.where(
            codes_ref[:, slot : slot + 1] == letters, 1.0, 0.0).astype(low)
    table_acc[...] += dotf(embed_grad, lets_ref[...], 0, 0)

    @pl.when(last)
    def _():
        table_out[...] = table_acc[...].astype(low)
        inlet_out[...] = inlet_acc[...].astype(low)
        recur_out[...] = recur_acc[...].astype(low)

def chars_back(codes, inlet, recur, embeds, states, coefs, grad, letters, rows=256):
    length = codes.shape[0]
    embed, half = inlet.shape[1], recur.shape[1]
    low = jnp.bfloat16
    full = lambda a: pl.BlockSpec(a.shape, lambda b: (0, 0))
    outs = [(embed, letters), inlet.shape, recur.shape]
    return pl.pallas_call(
        functools.partial(chars_back_kernel, half),
        grid=(length // rows,),
        in_specs=[
            pl.BlockSpec((rows, CHARS), lambda b: (b, 0)), full(inlet), full(recur),
            pl.BlockSpec((rows, CHARS * embed), lambda b: (b, 0)),
            pl.BlockSpec((2, CHARS - 1, rows, half), lambda b: (0, 0, b, 0)),
            pl.BlockSpec((2, COEFS, rows, half), lambda b: (0, 0, b, 0)),
            pl.BlockSpec((rows, 2 * half), lambda b: (b, 0)),
        ],
        out_specs=[pl.BlockSpec(s, lambda b: (0, 0)) for s in outs],
        out_shape=[jax.ShapeDtypeStruct(s, low) for s in outs],
        scratch_shapes=[
            pltpu.VMEM((CHARS * rows, 6 * half), low), pltpu.VMEM((CHARS * rows, letters), low),
            ] + [pltpu.VMEM(s, jnp.float32) for s in outs],
        compiler_params=pltpu.CompilerParams(vmem_limit_bytes=VMEM_LIMIT),
        cost_estimate=pl.CostEstimate(flops=22 * 10**9, bytes_accessed=40 * 10**6, transcendentals=0),
    )(codes, inlet, recur, embeds, states, coefs, grad)

def feed_kernel(blocks, joined_ref, first_ref, rep_ref, token_cot_ref, char_cot_ref, gains_ref,
                merging_ref, up_ref, down_ref, branch_ref,
                token_ref, char_ref, summed_ref, merged_ref, hidden_ref, feed_grad_ref, hidden_grad_ref,
                branch_grad_ref, merging_grad_ref, summed_grad_ref, char_grad_ref, sums_ref, slope_ref):
    low = jnp.bfloat16
    width = first_ref.shape[1]
    step = up_ref.shape[1] // blocks

    @pl.when(pl.program_id(0) == 0)
    def _():
        sums_ref[...] = jnp.zeros_like(sums_ref)

    merged, merging_slope = gelu_both(dotf(joined_ref[...], merging_ref[...]))
    merged_low = merged.astype(low)
    merged_ref[...] = merged_low
    summed = first_ref[...] + merged
    summed_low = summed.astype(low)
    summed_ref[...] = summed_low
    total = summed
    for c in range(blocks):
        cols = slice(c * step, (c + 1) * step)
        hidden, slope = gelu_both(dotf(summed_low, up_ref[:, cols]))
        slope_ref[:, cols] = slope
        hidden_low = hidden.astype(low)
        hidden_ref[:, cols] = hidden_low
        total = total + dotf(hidden_low, down_ref[cols, :])
    normed, spread = norm_parts(total)
    gain, shift = gains_ref[2:3, :], gains_ref[3:4, :]
    token_ref[...] = (normed * gain + shift).astype(low)
    cot = token_cot_ref[...].astype(jnp.float32)
    sums_ref[0] += column_sums(cot * normed)
    sums_ref[1] += column_sums(cot)
    token_grad = norm_back(normed, spread, cot * gain)
    feed_grad = token_grad.astype(low)
    feed_grad_ref[...] = feed_grad
    total = token_grad
    for c in range(blocks):
        cols = slice(c * step, (c + 1) * step)
        hidden_grad = (slope_ref[:, cols] * dotf(feed_grad, down_ref[cols, :], 1, 1)).astype(low)
        hidden_grad_ref[:, cols] = hidden_grad
        total = total + dotf(hidden_grad, up_ref[:, cols], 1, 1)
    summed_grad_ref[...] = total
    normed, spread = norm_parts(rep_ref[...].astype(jnp.float32) + dotf(merged_low, branch_ref[...]))
    gain, shift = gains_ref[4:5, :], gains_ref[5:6, :]
    char_ref[...] = (normed * gain + shift).astype(low)
    cot = char_cot_ref[...].astype(jnp.float32)
    sums_ref[2] += column_sums(cot * normed)
    sums_ref[3] += column_sums(cot)
    char_grad = norm_back(normed, spread, cot * gain)
    char_grad_ref[...] = char_grad
    branch_grad = char_grad.astype(low)
    branch_grad_ref[...] = branch_grad
    merging_grad_ref[...] = (merging_slope * (total + dotf(branch_grad, branch_ref[...], 1, 1))).astype(low)

def feed(joined, first, rep, token_cot, char_cot, gains, merging, up, down, branch, rows=256, blocks=2):
    length, width = first.shape
    ff = up.shape[1]
    low, wide = jnp.bfloat16, jnp.float32
    row = lambda w: pl.BlockSpec((rows, w), lambda b: (b, 0))
    full = lambda a: pl.BlockSpec(a.shape, lambda b: (0, 0), pipeline_mode=pl.Buffered(1))
    outs = [(width, low), (width, low), (width, low), (width, low), (ff, low), (width, low), (ff, low),
            (width, low), (width, low), (width, wide), (width, wide)]
    return pl.pallas_call(
        functools.partial(feed_kernel, blocks),
        grid=(length // rows,),
        in_specs=[row(joined.shape[1]), row(width), row(width), row(width), row(width), full(gains),
                  full(merging), full(up), full(down), full(branch)],
        out_specs=[row(w) for w, _ in outs] + [pl.BlockSpec((4, 8, width), lambda b: (0, 0, 0))],
        out_shape=[jax.ShapeDtypeStruct((length, w), t) for w, t in outs] + [jax.ShapeDtypeStruct((4, 8, width), wide)],
        scratch_shapes=[pltpu.VMEM((rows, ff), wide)],
        compiler_params=pltpu.CompilerParams(vmem_limit_bytes=VMEM_LIMIT),
        cost_estimate=pl.CostEstimate(flops=30 * 10**9, bytes_accessed=70 * 10**6, transcendentals=10**7),
    )(joined, first, rep, token_cot, char_cot, gains, merging, up, down, branch)


def side_by_side(rows, groups):
    r = rows.shape[-2] // groups
    return jnp.concatenate(
        [rows[..., i * r : (i + 1) * r, :] for i in range(groups)], axis=-1
    )


def one_below_other(rows, groups):
    w = rows.shape[-1] // groups
    return jnp.concatenate(
        [rows[..., i * w : (i + 1) * w] for i in range(groups)], axis=-2
    )


def whole(part):
    return part.reshape(-1, part.shape[-1])


def shares(full, devices):
    return full.reshape(devices, -1, full.shape[-1]).astype(jnp.bfloat16)


class Grid:
    def __init__(self, sizes):
        dp, fsdp = sizes
        z = 4 if dp % 4 == 0 else 1
        core = 2 if fsdp % 2 == 0 else 1
        self.fsdp = fsdp
        self.shape = (z, dp // z, fsdp // core, core)
        self.devices = dp * fsdp

    def own(self):
        z, x, y, core = self.shape
        dp, fsdp = lax.axis_index("dp"), lax.axis_index("fsdp")
        return dp // x, dp % x, fsdp // core, fsdp % core

    def send(self, values, shift):
        pairs = []
        for source, place in enumerate(itertools.product(*map(range, self.shape))):
            target = 0
            for at, by, size in zip(place, shift, self.shape):
                target = target * size + (at + by) % size
            pairs.append((source, target))
        return lax.ppermute(values, AXES, pairs)

    def plane(self):
        z, x, y, core = self.shape
        return [(i, j) for i in range(x) for j in range(y) if i or j]


def gather_rows(grid, part):
    nz, nx, ny, ncore = grid.shape
    z, x, y, core = grid.own()
    put = lax.dynamic_update_slice
    rows, width = part.shape
    column = jnp.zeros((nz, rows, width), part.dtype)
    column = put(column, part[None], (z, 0, 0))
    for s in range(1, nz):
        came = grid.send(part, (s, 0, 0, 0))
        column = put(column, came[None], ((z - s) % nz, 0, 0))
    layer = jnp.zeros((nz, nx, ny, rows, width), part.dtype)
    layer = put(layer, column[:, None, None], (0, x, y, 0, 0))
    for i, j in grid.plane():
        came = grid.send(column, (0, i, j, 0))
        layer = put(layer, came[:, None, None], (0, (x - i) % nx, (y - j) % ny, 0, 0))
    full = jnp.zeros((nz, nx, ny, ncore, rows, width), part.dtype)
    full = put(full, layer[:, :, :, None], (0, 0, 0, core, 0, 0))
    for s in range(1, ncore):
        came = grid.send(layer, (0, 0, 0, s))
        full = put(full, came[:, :, :, None], (0, 0, 0, (core - s) % ncore, 0, 0))
    return full.reshape(-1, width)


def scatter_sums(grid, parts):
    nz, nx, ny, ncore = grid.shape
    z, x, y, core = grid.own()
    rows, width = parts.shape[1:]
    wide, low = jnp.float32, jnp.bfloat16
    parts = parts.reshape(nz, nx, ny, ncore, rows, width)

    def of_core(at):
        return lax.dynamic_index_in_dim(parts, at, 3, False)

    total = of_core(core).astype(wide)
    for s in range(1, ncore):
        total = total + grid.send(of_core((core + s) % ncore), (0, 0, 0, s)).astype(wide)
    layer = total.astype(low)

    def of_column(i, j):
        return lax.dynamic_slice(layer, (0, i, j, 0, 0), (nz, 1, 1, rows, width))[:, 0, 0]

    total = of_column(x, y).astype(wide)
    for i, j in grid.plane():
        total = total + grid.send(of_column((x + i) % nx, (y + j) % ny), (0, i, j, 0)).astype(wide)
    column = total.astype(low)
    total = lax.dynamic_index_in_dim(column, z, 0, False).astype(wide)
    for s in range(1, nz):
        came = grid.send(lax.dynamic_index_in_dim(column, (z + s) % nz, 0, False), (s, 0, 0, 0))
        total = total + came.astype(wide)
    return total


def on_device(
    sizes,
    token_states,
    char_codes,
    lengths,
    token_cotangent,
    char_cotangent,
    char_table,
    recur_input,
    recur_state,
    project_weight,
    output_weight,
    merging_weight,
    up_weight,
    down_weight,
    char_weight,
    attend_gain,
    attend_shift,
    feed_gain,
    feed_shift,
    char_gain,
    char_shift,
):
    length, width = token_states.shape[1:]
    half = width // 2
    triple = 3 * half
    letters_count = char_table.shape[0]
    r = project_weight.shape[0]
    grid = Grid(sizes)
    devices = grid.devices
    ff_blocks = up_weight.shape[1] // width
    low = jnp.bfloat16

    second_rows = jnp.concatenate(
        [
            output_weight,
            char_weight,
            merging_weight.reshape(-1, width),
            one_below_other(up_weight, ff_blocks),
            down_weight,
        ],
        axis=0,
    )
    second_all = lax.all_gather(second_rows, AXES, axis=0)
    gains = jnp.stack(
        [attend_gain, attend_shift, feed_gain, feed_shift, char_gain, char_shift]
    ).reshape(1, 6 * r)
    own_table = char_table.T
    gain_rows = jnp.pad(gains, ((0, own_table.shape[0] - 1), (0, 0)))
    table_rows = jnp.concatenate([own_table, gain_rows], axis=1)
    table_rows = jnp.pad(table_rows, ((0, 0), (0, triple - table_rows.shape[1])))
    char_rows = jnp.concatenate(
        [
            side_by_side(recur_input.T, 3),
            side_by_side(recur_state.T, 3),
            one_below_other(table_rows, 3),
        ],
        axis=1,
    )
    project_full = gather_rows(grid, project_weight)
    chars_all = gather_rows(grid, char_rows).reshape(devices, r, 3 * width)
    inlet_full = whole(one_below_other(chars_all[:, :, :width], 3))
    recur_full = whole(one_below_other(chars_all[:, :, width : width + triple], 3))
    table_all = side_by_side(chars_all[:, :, width + triple :], 3)
    table_full = whole(table_all[:, :, : pl.cdiv(letters_count, LANES) * LANES])
    gains_all = table_all[:, 0, letters_count : letters_count + 6 * r]
    gains_all = gains_all.reshape(devices, 6, r).transpose(1, 0, 2).reshape(6, width)
    gains_all = gains_all.astype(jnp.float32)

    at = 0
    parts = []
    for rows in (r, r) + (merging_weight.shape[1],) * 3 + (ff_blocks * r, down_weight.shape[0]):
        parts.append(second_all[:, at : at + rows])
        at += rows
    output_full, branch_full = whole(parts[0]), whole(parts[1])
    merging_full = [whole(part) for part in parts[2:5]]
    upper_full = whole(side_by_side(parts[5], ff_blocks))
    lower_full = whole(parts[6])

    states, codes = token_states[0], char_codes[0]
    valid = lax.broadcasted_iota(jnp.int32, (length, 1), 0) < lengths
    embeds, chars_rep, char_states, coefs = chars_forward(
        codes, table_full, inlet_full, recur_full
    )
    mixed = product(states, project_full).astype(low)
    context_low, log_totals = attend(mixed, lengths, width)
    first_pre = states.astype(jnp.float32) + product(context_low, output_full)
    first, pull_first = jax.vjp(norm_apply, first_pre, gains_all[0], gains_all[1])
    joined = jnp.where(
        valid, jnp.concatenate([first.astype(low), chars_rep], axis=-1), jnp.zeros((), low)
    )
    joined = jnp.concatenate([shift_down(joined), joined, shift_up(joined)], axis=1)
    (
        token_stream,
        char_stream,
        summed_low,
        merged_low,
        hidden_low,
        feed_grad,
        hidden_grad,
        branch_grad,
        merging_grad,
        summed_grad,
        char_pre_grad,
        gain_sums,
    ) = feed(
        joined,
        first,
        chars_rep,
        token_cotangent[0],
        char_cotangent[0],
        gains_all,
        jnp.concatenate(merging_full, axis=0),
        upper_full,
        lower_full,
        branch_full,
    )
    feed_gain_grad, feed_shift_grad, char_gain_grad, char_shift_grad = jnp.sum(gain_sums, axis=1)
    early = jnp.concatenate(
        [shares(outer_sum(merged_low, branch_grad), devices)]
        + [
            shares(outer_sum(joined[:, 2 * i * width : 2 * (i + 1) * width], merging_grad), devices)
            for i in range(3)
        ]
        + [one_below_other(shares(outer_sum(summed_low, hidden_grad), devices), ff_blocks)]
        + [shares(outer_sum(hidden_low, feed_grad), devices)],
        axis=1,
    )
    early, merging_grad = lax.optimization_barrier((early, merging_grad))
    early = lax.psum_scatter(early, AXES, scatter_dimension=0, tiled=True)[0]
    joined_grad = (
        shift_up(back_product(merging_grad, merging_full[0]))
        + back_product(merging_grad, merging_full[1])
        + shift_down(back_product(merging_grad, merging_full[2]))
    )
    joined_grad = jnp.where(valid, joined_grad, 0.0)
    first_grad = summed_grad + joined_grad[:, :width]
    rep_grad = char_pre_grad + joined_grad[:, width:]
    first_pre_grad, attend_gain_grad, attend_shift_grad = pull_first(first_grad)
    table_grad, inlet_grad, recur_weight_grad = chars_back(
        codes, inlet_full, recur_full, embeds, char_states, coefs, rep_grad, table_full.shape[1]
    )
    attended_grad = first_pre_grad.astype(low)
    output_weight_grad = outer_sum(context_low, attended_grad)
    context_grad = back_product(attended_grad, output_full).astype(low)
    gain_grads = jnp.stack(
        [
            attend_gain_grad,
            attend_shift_grad,
            feed_gain_grad,
            feed_shift_grad,
            char_gain_grad,
            char_shift_grad,
        ]
    )
    gain_shares = gain_grads.reshape(6, devices, r).transpose(1, 0, 2).reshape(devices, 1, 6 * r)
    table_shares = shares(table_grad, devices)[:, :, :letters_count]
    gain_shares = jnp.pad(
        gain_shares.astype(low), ((0, 0), (0, table_shares.shape[1] - 1), (0, 0))
    )
    table_shares = jnp.concatenate([table_shares, gain_shares], axis=2)
    table_shares = jnp.pad(
        table_shares, ((0, 0), (0, 0), (0, triple - table_shares.shape[2]))
    )
    late = jnp.concatenate(
        [
            jnp.concatenate(
                [
                    side_by_side(shares(inlet_grad, devices), 3),
                    side_by_side(shares(recur_weight_grad, devices), 3),
                    one_below_other(table_shares, 3),
                ],
                axis=2,
            ),
            side_by_side(shares(output_weight_grad, devices), 3),
        ],
        axis=1,
    )
    late, context_grad = lax.optimization_barrier((late, context_grad))
    late = scatter_sums(grid, late)
    head_grads = attend_back(mixed, context_grad, context_low, log_totals, lengths, width)
    mixed_grad = jnp.concatenate([head_grads[0], head_grads[1], head_grads[2]], axis=-1)
    own_project = scatter_sums(grid, shares(outer_sum(states, mixed_grad), devices))
    input_gradient = (first_pre_grad + back_product(mixed_grad, project_full)).astype(low)
    early = early.astype(jnp.float32)
    own_chars = late[:r]
    own_table_rows = side_by_side(own_chars[:, width + triple :], 3)
    own_gains = own_table_rows[0, letters_count : letters_count + 6 * r].reshape(6, r)
    spots = []
    at = 0
    for rows in (r, 3 * merging_weight.shape[1], ff_blocks * r, down_weight.shape[0]):
        spots.append(early[at : at + rows])
        at += rows
    return (
        token_stream[None],
        char_stream[None],
        input_gradient[None],
        own_table_rows[:, :letters_count].T,
        one_below_other(own_chars[:, :width], 3).T,
        one_below_other(own_chars[:, width : width + triple], 3).T,
        own_project,
        one_below_other(late[r:], 3),
        spots[1].reshape(merging_weight.shape),
        side_by_side(spots[2], ff_blocks),
        spots[3],
        spots[0],
        own_gains[0],
        own_gains[1],
        own_gains[2],
        own_gains[3],
        own_gains[4],
        own_gains[5],
    )

def solution(mesh):
    placed = (
        P(AXES, None, None),
        P(AXES, None, None),
        P(AXES),
        P(AXES, None, None),
        P(AXES, None, None),
        P(None, AXES),
        P(None, AXES),
        P(None, AXES),
        P(AXES, None),
        P(AXES, None),
        P(None, AXES, None),
        P(AXES, None),
        P(AXES, None),
        P(AXES, None),
        P(AXES),
        P(AXES),
        P(AXES),
        P(AXES),
        P(AXES),
        P(AXES),
    )
    sizes = (mesh.shape["dp"], mesh.shape["fsdp"])
    return jax.shard_map(
        functools.partial(on_device, sizes),
        mesh=mesh,
        in_specs=placed,
        out_specs=(
            P(AXES, None, None),
            P(AXES, None, None),
            P(AXES, None, None),
            P(None, AXES),
            P(None, AXES),
            P(None, AXES),
            P(AXES, None),
            P(AXES, None),
            P(None, AXES, None),
            P(AXES, None),
            P(AXES, None),
            P(AXES, None),
            P(AXES),
            P(AXES),
            P(AXES),
            P(AXES),
            P(AXES),
            P(AXES),
        ),
        check_vma=False,
    )
```

```python
import functools
import itertools
import math

import jax
import jax.numpy as jnp
from jax import lax
from jax.experimental import pallas as pl
from jax.experimental.pallas import tpu as pltpu
from jax.sharding import PartitionSpec as P

HEAD_DIM = 64
CHARS = 4
LANES = 128
EPS = 1e-05
MASKED = -1e30
SCALE = 1.0 / math.sqrt(HEAD_DIM)
SCALE2 = math.log2(math.e) / math.sqrt(HEAD_DIM)
AXES = ("dp", "fsdp")
VMEM_LIMIT = 56 * 1024 * 1024
BRIEF = pl.CostEstimate(flops=200 * 10**9, bytes_accessed=10**6, transcendentals=0)

def product(left, right):
    return jnp.dot(left, right, preferred_element_type=jnp.float32)


def outer_sum(left, right):
    return jnp.einsum("li,lo->io", left, right, preferred_element_type=jnp.float32)


def back_product(grad_rows, weight):
    return jnp.einsum("lo,io->li", grad_rows, weight, preferred_element_type=jnp.float32)


def dotf(a,b,ca=1,cb=0):
    return lax.dot_general(a,b,(((ca,),(cb,)),((),())),preferred_element_type=jnp.float32)

def lane_half(shape):
    return lax.broadcasted_iota(jnp.int32, shape, 1) < HEAD_DIM

def attend_kernel(rows, length_ref, q_ref, k_ref, v_ref, ctx_ref, lse_ref, kx_ref, vx_ref):
    length = k_ref.shape[0]
    lane = lax.broadcasted_iota(jnp.int32, (length, LANES), 1)
    place = lax.broadcasted_iota(jnp.int32, (length, LANES), 0)
    kx_ref[:, :LANES] = k_ref[...]
    kx_ref[:, LANES:] = jnp.where((lane == 0) & (place >= length_ref[0]), MASKED, 0.0).astype(jnp.bfloat16)
    vx_ref[:, :LANES] = v_ref[...]
    vx_ref[:, LANES:] = jnp.ones((length, LANES), jnp.bfloat16)
    low = lane_half((rows, LANES))
    one = jnp.where(lax.broadcasted_iota(jnp.int32, (rows, LANES), 1) == 0, 1.0, 0.0).astype(jnp.bfloat16)
    def step(c, _):
        at = pl.ds(pl.multiple_of(c * rows, rows), rows)
        q = q_ref[at, :].astype(jnp.float32)
        outs = []
        for h in range(2):
            mine = low if h == 0 else jnp.logical_not(low)
            qx = jnp.concatenate([jnp.where(mine, q, 0.0).astype(jnp.bfloat16), one], axis=1)
            s = dotf(qx, kx_ref[...], 1, 1)
            peak = jnp.max(s, axis=1, keepdims=True) * SCALE2
            p = jnp.exp2(s * SCALE2 - peak).astype(jnp.bfloat16)
            o = dotf(p, vx_ref[...])
            total = o[:, LANES:]
            outs.append((o[:, :LANES] / total, peak + jnp.log2(total)))
        ctx_ref[at, :] = jnp.where(low, outs[0][0], outs[1][0]).astype(jnp.bfloat16)
        lse_ref[at, :] = jnp.where(low, outs[0][1], outs[1][1])
        return 0
    lax.fori_loop(0, length // rows, step, 0, unroll=True)

def attend(mixed, lengths, width, rows=256):
    length = mixed.shape[0]
    pairs = width // LANES
    spec = lambda o: pl.BlockSpec((length, LANES), lambda p, o=o: (0, p+o))
    return pl.pallas_call(
        functools.partial(attend_kernel, rows),
        grid=(pairs,),
        in_specs=[pl.BlockSpec(memory_space=pltpu.SMEM), spec(0), spec(pairs), spec(2 * pairs)],
        out_specs=[spec(0), spec(0)],
        out_shape=[jax.ShapeDtypeStruct((length, width), jnp.bfloat16), jax.ShapeDtypeStruct((length, width), jnp.float32)],
        scratch_shapes=[pltpu.VMEM((length, 2*LANES), jnp.bfloat16), pltpu.VMEM((length, 2*LANES), jnp.bfloat16)],
        compiler_params=pltpu.CompilerParams(vmem_limit_bytes=VMEM_LIMIT),
        cost_estimate=BRIEF,
    )(lengths, mixed, mixed, mixed)

def back_kernel(rows, length_ref, q_ref, k_ref, v_ref, do_ref, o_ref, lse_ref, *rest):
    dq_ref, dk_out, dv_out, kx_ref, qt_ref, dot_ref, dk_ref, dv_ref = rest[-8:]
    length = k_ref.shape[0]
    lane = lax.broadcasted_iota(jnp.int32, (length, LANES), 1)
    place = lax.broadcasted_iota(jnp.int32, (length, LANES), 0)
    kx_ref[:, :LANES] = k_ref[...]
    kx_ref[:, LANES:] = jnp.where((lane == 0) & (place >= length_ref[0]), MASKED, 0.0).astype(jnp.bfloat16)
    qt_ref[...] = q_ref[...].T
    dot_ref[...] = do_ref[...].T
    dk_ref[...] = jnp.zeros_like(dk_ref)
    dv_ref[...] = jnp.zeros_like(dv_ref)
    low = lane_half((rows, LANES))
    one = jnp.where(lax.broadcasted_iota(jnp.int32, (rows, LANES), 1) == 0, 1.0, 0.0).astype(jnp.bfloat16)
    def step(c, _):
        at = pl.ds(pl.multiple_of(c * rows, rows), rows)
        q = q_ref[at, :].astype(jnp.float32)
        do = do_ref[at, :].astype(jnp.float32)
        doo = do * o_ref[at, :].astype(jnp.float32)
        lse = lse_ref[at, :]
        dqs = []
        for h in range(2):
            mine = low if h == 0 else jnp.logical_not(low)
            qx = jnp.concatenate([jnp.where(mine, q, 0.0).astype(jnp.bfloat16), one], axis=1)
            s = dotf(qx, kx_ref[...], 1, 1)
            p = jnp.exp2(s * SCALE2 - lse[:, h*HEAD_DIM:h*HEAD_DIM+1])
            dp = dotf(jnp.where(mine, do, 0.0).astype(jnp.bfloat16), v_ref[...], 1, 1)
            delta = jnp.sum(jnp.where(mine, doo, 0.0), axis=1, keepdims=True)
            ds = (p * (dp - delta)).astype(jnp.bfloat16)
            pb = p.astype(jnp.bfloat16)
            hs = slice(h*HEAD_DIM, (h+1)*HEAD_DIM)
            dqs.append(dotf(ds, k_ref[...]))
            dk_ref[hs, :] += dotf(qt_ref[hs, at], ds)
            dv_ref[hs, :] += dotf(dot_ref[hs, at], pb)
        dq_ref[at, :] = (jnp.where(low, dqs[0], dqs[1]) * SCALE).astype(jnp.bfloat16)
        return 0
    lax.fori_loop(0, length // rows, step, 0, unroll=True)
    dk_out[...] = (dk_ref[...] * SCALE).T.astype(jnp.bfloat16)
    dv_out[...] = dv_ref[...].T.astype(jnp.bfloat16)

def attend_back(
    mixed, context_grad, context, log_totals, lengths, width, start, pairs, earlier, rows=256
):
    length = mixed.shape[0]
    every = width // LANES
    spec = lambda o: pl.BlockSpec((length, LANES), lambda p, o=o: (0, p + o + start))
    scratch = lambda a, b, t: pltpu.VMEM((a, b), t)
    return pl.pallas_call(
        functools.partial(back_kernel, rows),
        grid=(pairs,),
        in_specs=[pl.BlockSpec(memory_space=pltpu.SMEM), spec(0), spec(every), spec(2 * every)]
        + [spec(0)] * 3
        + [pl.BlockSpec(memory_space=pl.ANY)] * len(earlier),
        out_specs=[spec(0)] * 3,
        out_shape=[jax.ShapeDtypeStruct((length, width), jnp.bfloat16)] * 3,
        input_output_aliases={7 + i: i for i in range(len(earlier))},
        scratch_shapes=[
            scratch(length, 2 * LANES, jnp.bfloat16),
            scratch(LANES, length, jnp.bfloat16),
            scratch(LANES, length, jnp.bfloat16),
            scratch(LANES, length, jnp.float32),
            scratch(LANES, length, jnp.float32),
        ],
        compiler_params=pltpu.CompilerParams(vmem_limit_bytes=VMEM_LIMIT),
        cost_estimate=BRIEF,
    )(lengths, mixed, mixed, mixed, context_grad, context, log_totals, *earlier)


ROOT_HALF = math.sqrt(0.5)
DENSITY = 1.0 / math.sqrt(2.0 * math.pi)

def gelu_both(values):
    below = 0.5 + 0.5 * lax.erf(values * ROOT_HALF)
    return values * below, below + values * (DENSITY * jnp.exp(-0.5 * values * values))

def norm_parts(values):
    average = jnp.mean(values, axis=-1, keepdims=True)
    centred = values - average
    spread = lax.rsqrt(jnp.mean(centred * centred, axis=-1, keepdims=True) + EPS)
    return centred * spread, spread

def norm_back(normed, spread, scaled):
    return spread * (scaled - jnp.mean(scaled, axis=-1, keepdims=True)
                     - normed * jnp.mean(scaled * normed, axis=-1, keepdims=True))

def column_sums(values):
    rows, width = values.shape
    return jnp.sum(values.reshape(rows // 8, 8, width), axis=0)

def chars_kernel(half, codes_ref, table_ref, inlet_ref, recur_ref, embed_ref, rep_ref, states_ref, coef_ref):
    rows = codes_ref.shape[0]
    triple = 3 * half
    width = embed_ref.shape[1] // CHARS
    letters = lax.broadcasted_iota(jnp.int32, (rows, table_ref.shape[1]), 1)
    embeds = []
    for slot in range(CHARS):
        picked = jnp.where(codes_ref[:, slot : slot + 1] == letters, 1.0, 0.0).astype(jnp.bfloat16)
        embed = dotf(picked, table_ref[...], 1, 1).astype(jnp.bfloat16)
        embed_ref[:, slot * width : (slot + 1) * width] = embed
        embeds.append(embed)
    low = jnp.bfloat16
    for side in range(2):
        state = None
        base = side * triple
        order = range(CHARS) if side == 0 else range(CHARS - 1, -1, -1)
        for step, slot in enumerate(order):
            gates = dotf(embeds[slot], inlet_ref[base : base + triple, :], 1, 1)
            if state is None:
                update = jax.nn.sigmoid(gates[:, half : 2 * half])
                fresh = jnp.tanh(gates[:, 2 * half :])
                new = (1.0 - update) * fresh
                coef_ref[side, 0] = ((1.0 - update) * (1.0 - fresh * fresh)).astype(low)
                coef_ref[side, 1] = (-fresh * update * (1.0 - update)).astype(low)
            else:
                recur = dotf(state, recur_ref[base : base + triple, :], 1, 1)
                reset = jax.nn.sigmoid(gates[:, :half] + recur[:, :half])
                update = jax.nn.sigmoid(gates[:, half : 2 * half] + recur[:, half : 2 * half])
                recur_new = recur[:, 2 * half :]
                fresh = jnp.tanh(gates[:, 2 * half :] + reset * recur_new)
                before = state.astype(jnp.float32)
                new = (1.0 - update) * fresh + update * before
                at = 2 + 5 * (step - 1)
                coef_ref[side, at] = ((1.0 - update) * (1.0 - fresh * fresh)).astype(low)
                coef_ref[side, at + 1] = ((before - fresh) * update * (1.0 - update)).astype(low)
                coef_ref[side, at + 2] = (recur_new * reset * (1.0 - reset)).astype(low)
                coef_ref[side, at + 3] = reset.astype(low)
                coef_ref[side, at + 4] = update.astype(low)
            state = new.astype(low)
            if step < CHARS - 1:
                states_ref[side, step] = state
        rep_ref[:, side * half : (side + 1) * half] = state

COEFS = 2 + 5 * (CHARS - 1)

def chars_forward(codes, table, inlet, recur, rows=256):
    length = codes.shape[0]
    embed, half = inlet.shape[1], recur.shape[1]
    low = jnp.bfloat16
    full = lambda a: pl.BlockSpec(a.shape, lambda b: (0, 0))
    return pl.pallas_call(
        functools.partial(chars_kernel, half),
        grid=(length // rows,),
        in_specs=[pl.BlockSpec((rows, CHARS), lambda b: (b, 0)), full(table), full(inlet), full(recur)],
        out_specs=[
            pl.BlockSpec((rows, CHARS * embed), lambda b: (b, 0)),
            pl.BlockSpec((rows, 2 * half), lambda b: (b, 0)),
            pl.BlockSpec((2, CHARS - 1, rows, half), lambda b: (0, 0, b, 0)),
            pl.BlockSpec((2, COEFS, rows, half), lambda b: (0, 0, b, 0)),
        ],
        out_shape=[
            jax.ShapeDtypeStruct((length, CHARS * embed), low),
            jax.ShapeDtypeStruct((length, 2 * half), low),
            jax.ShapeDtypeStruct((2, CHARS - 1, length, half), low),
            jax.ShapeDtypeStruct((2, COEFS, length, half), low),
        ],
        compiler_params=pltpu.CompilerParams(vmem_limit_bytes=VMEM_LIMIT),
        cost_estimate=BRIEF,
    )(codes, table, inlet, recur)

def chars_back_kernel(half, codes_ref, inlet_ref, recur_ref, embed_ref, states_ref, coef_ref, grad_ref,
                      table_out, inlet_out, recur_out, gates_ref, lets_ref, table_acc, inlet_acc, recur_acc):
    rows = codes_ref.shape[0]
    triple = 3 * half
    width = embed_ref.shape[1] // CHARS
    low = jnp.bfloat16
    first, last = pl.program_id(0) == 0, pl.program_id(0) == pl.num_programs(0) - 1

    @pl.when(first)
    def _():
        table_acc[...] = jnp.zeros_like(table_acc)
        inlet_acc[...] = jnp.zeros_like(inlet_acc)
        recur_acc[...] = jnp.zeros_like(recur_acc)

    for side in range(2):
        grad = grad_ref[:, side * half : (side + 1) * half]
        base = side * triple
        order = range(CHARS) if side == 0 else range(CHARS - 1, -1, -1)
        for step, slot in reversed(list(enumerate(order))):
            at = 2 + 5 * (step - 1) if step else 0
            load = lambda k: coef_ref[side, at + k].astype(jnp.float32)
            fresh_pre = grad * load(0)
            update_pre = grad * load(1)
            spot = slice(slot * rows, (slot + 1) * rows)
            gates_ref[spot, base + half : base + 2 * half] = update_pre.astype(low)
            gates_ref[spot, base + 2 * half : base + triple] = fresh_pre.astype(low)
            if step == 0:
                gates_ref[spot, base : base + half] = jnp.zeros((rows, half), low)
                continue
            reset_pre = fresh_pre * load(2)
            gates_ref[spot, base : base + half] = reset_pre.astype(low)
            recur_grad = jnp.concatenate(
                [reset_pre.astype(low), update_pre.astype(low), (fresh_pre * load(3)).astype(low)], axis=1)
            recur_acc[base : base + triple, :] += dotf(recur_grad, states_ref[side, step - 1], 0, 0)
            grad = grad * load(4) + dotf(recur_grad, recur_ref[base : base + triple, :])
    embed_all = jnp.concatenate([embed_ref[:, j * width : (j + 1) * width] for j in range(CHARS)], axis=0)
    inlet_acc[...] += dotf(gates_ref[...], embed_all, 0, 0)
    embed_grad = dotf(gates_ref[...], inlet_ref[...]).astype(low)
    letters = lax.broadcasted_iota(jnp.int32, (rows, table_acc.shape[1]), 1)
    for slot in range(CHARS):
        lets_ref[slot * rows : (slot + 1) * rows, :] = jnp.where(
            codes_ref[:, slot : slot + 1] == letters, 1.0, 0.0).astype(low)
    table_acc[...] += dotf(embed_grad, lets_ref[...], 0, 0)

    @pl.when(last)
    def _():
        table_out[...] = table_acc[...].astype(low)
        inlet_out[...] = inlet_acc[...].astype(low)
        recur_out[...] = recur_acc[...].astype(low)

def chars_back(codes, inlet, recur, embeds, states, coefs, grad, letters, rows=256):
    length = codes.shape[0]
    embed, half = inlet.shape[1], recur.shape[1]
    low = jnp.bfloat16
    full = lambda a: pl.BlockSpec(a.shape, lambda b: (0, 0))
    outs = [(embed, letters), inlet.shape, recur.shape]
    return pl.pallas_call(
        functools.partial(chars_back_kernel, half),
        grid=(length // rows,),
        in_specs=[
            pl.BlockSpec((rows, CHARS), lambda b: (b, 0)), full(inlet), full(recur),
            pl.BlockSpec((rows, CHARS * embed), lambda b: (b, 0)),
            pl.BlockSpec((2, CHARS - 1, rows, half), lambda b: (0, 0, b, 0)),
            pl.BlockSpec((2, COEFS, rows, half), lambda b: (0, 0, b, 0)),
            pl.BlockSpec((rows, 2 * half), lambda b: (b, 0)),
        ],
        out_specs=[pl.BlockSpec(s, lambda b: (0, 0)) for s in outs],
        out_shape=[jax.ShapeDtypeStruct(s, low) for s in outs],
        scratch_shapes=[
            pltpu.VMEM((CHARS * rows, 6 * half), low), pltpu.VMEM((CHARS * rows, letters), low),
            ] + [pltpu.VMEM(s, jnp.float32) for s in outs],
        compiler_params=pltpu.CompilerParams(vmem_limit_bytes=VMEM_LIMIT),
        cost_estimate=BRIEF,
    )(codes, inlet, recur, embeds, states, coefs, grad)

def flat(ref, part=0, parts=1):
    count = ref.shape[0] // parts
    block = ref[part * count : (part + 1) * count]
    return block.reshape(-1, block.shape[-1])


PAD = 8


def spread_rows(rows_ref, wide_ref):
    length, width = rows_ref.shape
    blank = jnp.zeros((PAD, width), jnp.float32)
    wide_ref[:PAD] = blank
    wide_ref[PAD + length :] = blank
    for start in range(0, length, 256):
        block = rows_ref[start : start + 256]
        wide_ref[PAD + start : PAD + start + block.shape[0]] = block.astype(jnp.float32)


def neighbours(wide_ref, rows):
    base = pl.multiple_of(pl.program_id(0) * rows, rows)
    window = wide_ref[pl.ds(base, rows + 2 * PAD)]
    return [window[PAD + i : PAD + i + rows].astype(jnp.bfloat16) for i in (-1, 0, 1)]


def feed_kernel(blocks, joined_ref, first_ref, rep_ref, token_cot_ref, char_cot_ref, gains_ref,
                up_ref, branch_ref, tap0_ref, tap1_ref, tap2_ref, down_ref,
                token_ref, char_ref, summed_ref, merged_ref, hidden_ref, feed_grad_ref, hidden_grad_ref,
                branch_grad_ref, merging_grad_ref, summed_grad_ref, char_grad_ref, sums_ref, slope_ref, wide_ref):
    low = jnp.bfloat16
    width = first_ref.shape[1]
    step = up_ref.shape[1] // blocks
    merging_refs = (tap0_ref, tap1_ref, tap2_ref)

    @pl.when(pl.program_id(0) == 0)
    def _():
        sums_ref[...] = jnp.zeros_like(sums_ref)
        spread_rows(joined_ref, wide_ref)

    merging_pre = 0.0
    for moved, ref in zip(neighbours(wide_ref, first_ref.shape[0]), merging_refs):
        merging_pre = merging_pre + dotf(moved, flat(ref))
    merged, merging_slope = gelu_both(merging_pre)
    merged_low = merged.astype(low)
    merged_ref[...] = merged_low
    summed = first_ref[...] + merged
    summed_low = summed.astype(low)
    summed_ref[...] = summed_low
    total = summed
    for c in range(blocks):
        cols = slice(c * step, (c + 1) * step)
        hidden, slope = gelu_both(dotf(summed_low, up_ref[:, cols]))
        slope_ref[:, cols] = slope
        hidden_low = hidden.astype(low)
        hidden_ref[:, cols] = hidden_low
        total = total + dotf(hidden_low, flat(down_ref, c, blocks))
    normed, spread = norm_parts(total)
    gain, shift = gains_ref[2:3, :], gains_ref[3:4, :]
    token_ref[...] = (normed * gain + shift).astype(low)
    cot = token_cot_ref[...].astype(jnp.float32)
    sums_ref[0] += column_sums(cot * normed)
    sums_ref[1] += column_sums(cot)
    token_grad = norm_back(normed, spread, cot * gain)
    feed_grad = token_grad.astype(low)
    feed_grad_ref[...] = feed_grad
    total = token_grad
    for c in range(blocks):
        cols = slice(c * step, (c + 1) * step)
        hidden_grad = (slope_ref[:, cols] * dotf(feed_grad, flat(down_ref, c, blocks), 1, 1)).astype(low)
        hidden_grad_ref[:, cols] = hidden_grad
        total = total + dotf(hidden_grad, up_ref[:, cols], 1, 1)
    summed_grad_ref[...] = total
    normed, spread = norm_parts(rep_ref[...].astype(jnp.float32) + dotf(merged_low, branch_ref[...]))
    gain, shift = gains_ref[4:5, :], gains_ref[5:6, :]
    char_ref[...] = (normed * gain + shift).astype(low)
    cot = char_cot_ref[...].astype(jnp.float32)
    sums_ref[2] += column_sums(cot * normed)
    sums_ref[3] += column_sums(cot)
    char_grad = norm_back(normed, spread, cot * gain)
    char_grad_ref[...] = char_grad
    branch_grad = char_grad.astype(low)
    branch_grad_ref[...] = branch_grad
    merging_grad_ref[...] = (merging_slope * (total + dotf(branch_grad, branch_ref[...], 1, 1))).astype(low)

def feed(joined, first, rep, token_cot, char_cot, gains, up, branch, merging, down, rows=256, blocks=2):
    length, width = first.shape
    ff = up.shape[1]
    low, wide = jnp.bfloat16, jnp.float32
    row = lambda w: pl.BlockSpec((rows, w), lambda b: (b, 0))
    full = lambda a: pl.BlockSpec(a.shape, lambda b: (0,) * a.ndim, pipeline_mode=pl.Buffered(1))
    outs = [(width, low), (width, low), (width, low), (width, low), (ff, low), (width, low), (ff, low),
            (width, low), (width, low), (width, wide), (width, wide)]
    return pl.pallas_call(
        functools.partial(feed_kernel, blocks),
        grid=(length // rows,),
        in_specs=[full(joined), row(width), row(width), row(width), row(width), full(gains),
                  full(up), full(branch)] + [spec for _, spec in merging + [down]],
        out_specs=[row(w) for w, _ in outs] + [pl.BlockSpec((4, 8, width), lambda b: (0, 0, 0))],
        out_shape=[jax.ShapeDtypeStruct((length, w), t) for w, t in outs] + [jax.ShapeDtypeStruct((4, 8, width), wide)],
        scratch_shapes=[pltpu.VMEM((rows, ff), wide), pltpu.VMEM((length + 2 * PAD, joined.shape[1]), wide)],
        compiler_params=pltpu.CompilerParams(vmem_limit_bytes=VMEM_LIMIT),
        cost_estimate=BRIEF,
    )(joined, first, rep, token_cot, char_cot, gains, up, branch, *[part for part, _ in merging + [down]])


def merging_back_kernel(length_ref, grad_ref, summed_ref, char_ref, pre_ref, gains_ref, output_ref,
                        tap0_ref, tap1_ref, tap2_ref,
                        pre_grad_ref, attended_ref, context_ref, rep_ref, sums_ref, wide_ref):
    rows, width = pre_ref.shape
    low = jnp.bfloat16

    @pl.when(pl.program_id(0) == 0)
    def _():
        sums_ref[...] = jnp.zeros_like(sums_ref)
        spread_rows(grad_ref, wide_ref)

    joined = 0.0
    for moved, ref in zip(neighbours(wide_ref, rows), (tap2_ref, tap1_ref, tap0_ref)):
        joined = joined + dotf(moved, flat(ref), 1, 1)
    place = pl.program_id(0) * rows + lax.broadcasted_iota(jnp.int32, (rows, 1), 0)
    joined = jnp.where(place < length_ref[0], joined, 0.0)
    rep_ref[...] = char_ref[...] + joined[:, width:]
    first_grad = summed_ref[...] + joined[:, :width]
    normed, spread = norm_parts(pre_ref[...])
    sums_ref[0] += column_sums(first_grad * normed)
    sums_ref[1] += column_sums(first_grad)
    pre_grad = norm_back(normed, spread, first_grad * gains_ref[0:1, :])
    pre_grad_ref[...] = pre_grad
    attended = pre_grad.astype(low)
    attended_ref[...] = attended
    context_ref[...] = dotf(attended, output_ref[...], 1, 1).astype(low)


def merging_back(lengths, grad, summed_grad, char_grad, pre, gains, output, merging, rows=256):
    length, width = pre.shape
    low, wide = jnp.bfloat16, jnp.float32
    row = pl.BlockSpec((rows, width), lambda b: (b, 0))
    full = lambda a: pl.BlockSpec(a.shape, lambda b: (0, 0), pipeline_mode=pl.Buffered(1))
    kinds = (wide, low, low, wide)
    return pl.pallas_call(
        merging_back_kernel,
        grid=(length // rows,),
        in_specs=[pl.BlockSpec(memory_space=pltpu.SMEM), full(grad), row, row, row, full(gains), full(output)]
        + [spec for _, spec in merging],
        out_specs=[row] * 4 + [pl.BlockSpec((2, 8, width), lambda b: (0, 0, 0))],
        out_shape=[jax.ShapeDtypeStruct((length, width), t) for t in kinds]
        + [jax.ShapeDtypeStruct((2, 8, width), wide)],
        scratch_shapes=[pltpu.VMEM((length + 2 * PAD, width), wide)],
        compiler_params=pltpu.CompilerParams(vmem_limit_bytes=VMEM_LIMIT),
        cost_estimate=BRIEF,
    )(lengths, grad, summed_grad, char_grad, pre, gains, output, *[part for part, _ in merging])


def side_by_side(rows, groups):
    r = rows.shape[-2] // groups
    return jnp.concatenate(
        [rows[..., i * r : (i + 1) * r, :] for i in range(groups)], axis=-1
    )


def one_below_other(rows, groups):
    w = rows.shape[-1] // groups
    return jnp.concatenate(
        [rows[..., i * w : (i + 1) * w] for i in range(groups)], axis=-2
    )


def whole(part):
    return part.reshape(-1, part.shape[-1])


def shares(full, devices):
    return full.reshape(devices, -1, full.shape[-1]).astype(jnp.bfloat16)


class Grid:
    def __init__(self, sizes):
        dp, fsdp = sizes
        z = 4 if dp % 4 == 0 else 1
        core = 2 if fsdp % 2 == 0 else 1
        self.fsdp = fsdp
        self.shape = (z, dp // z, fsdp // core, core)
        self.devices = dp * fsdp

    def own(self):
        z, x, y, core = self.shape
        dp, fsdp = lax.axis_index("dp"), lax.axis_index("fsdp")
        return dp // x, dp % x, fsdp // core, fsdp % core

    def send(self, values, shift):
        pairs = []
        for source, place in enumerate(itertools.product(*map(range, self.shape))):
            target = 0
            for at, by, size in zip(place, shift, self.shape):
                target = target * size + (at + by) % size
            pairs.append((source, target))
        return lax.ppermute(values, AXES, pairs)

    def plane(self):
        z, x, y, core = self.shape
        return [(i, j) for i in range(x) for j in range(y) if i or j]


def column_sends(grid, part):
    return [grid.send(part, (s, 0, 0, 0)) for s in range(1, grid.shape[0])]


def column_of(grid, part, came):
    nz = grid.shape[0]
    z = grid.own()[0]
    column = jnp.zeros((nz,) + part.shape, part.dtype)
    for s, piece in enumerate([part] + came):
        column = lax.dynamic_update_slice(column, piece[None], ((z - s) % nz, 0, 0))
    return column


def plane_sends(grid, column):
    return [grid.send(column, (0, i, j, 0)) for i, j in grid.plane()]


def plane_of(grid, column, came):
    nz, nx, ny, _ = grid.shape
    _, x, y, _ = grid.own()
    layer = jnp.zeros((nz, nx, ny) + column.shape[1:], column.dtype)
    for (i, j), piece in zip([(0, 0)] + grid.plane(), [column] + came):
        layer = lax.dynamic_update_slice(
            layer, piece[:, None, None], (0, (x - i) % nx, (y - j) % ny, 0, 0)
        )
    return layer


def cores_sends(grid, layer):
    return [grid.send(layer, (0, 0, 0, s)) for s in range(1, grid.shape[3])]


def cores_of(grid, layer, came):
    ncore = grid.shape[3]
    core = grid.own()[3]
    full = jnp.zeros(grid.shape + layer.shape[3:], layer.dtype)
    for s, piece in enumerate([layer] + came):
        full = lax.dynamic_update_slice(
            full, piece[:, :, :, None], (0, 0, 0, (core - s) % ncore, 0, 0)
        )
    return full.reshape(-1, layer.shape[-1])


def core_terms(grid, parts):
    ncore = grid.shape[3]
    core = grid.own()[3]
    parts = parts.reshape(grid.shape + parts.shape[1:])
    terms = [lax.dynamic_index_in_dim(parts, core, 3, False)]
    for s in range(1, ncore):
        chunk = lax.dynamic_index_in_dim(parts, (core + s) % ncore, 3, False)
        terms.append(grid.send(chunk, (0, 0, 0, s)))
    return terms


def plane_terms(grid, layer):
    nz, nx, ny, _ = grid.shape
    _, x, y, _ = grid.own()
    rows, width = layer.shape[3:]

    def of(i, j):
        return lax.dynamic_slice(layer, (0, i, j, 0, 0), (nz, 1, 1, rows, width))[:, 0, 0]

    return [of(x, y)] + [
        grid.send(of((x + i) % nx, (y + j) % ny), (0, i, j, 0)) for i, j in grid.plane()
    ]


def column_terms(grid, column):
    nz = grid.shape[0]
    z = grid.own()[0]
    terms = [lax.dynamic_index_in_dim(column, z, 0, False)]
    for s in range(1, nz):
        chunk = lax.dynamic_index_in_dim(column, (z + s) % nz, 0, False)
        terms.append(grid.send(chunk, (s, 0, 0, 0)))
    return terms


def added(terms):
    return functools.reduce(lambda a, b: a + b, [t.astype(jnp.float32) for t in terms])


def added_low(terms):
    return added(terms).astype(jnp.bfloat16)


def after(first, *then):
    return lax.optimization_barrier((first,) + then)


def on_device(
    sizes,
    token_states,
    char_codes,
    lengths,
    token_cotangent,
    char_cotangent,
    char_table,
    recur_input,
    recur_state,
    project_weight,
    output_weight,
    merging_weight,
    up_weight,
    down_weight,
    char_weight,
    attend_gain,
    attend_shift,
    feed_gain,
    feed_shift,
    char_gain,
    char_shift,
):
    length, width = token_states.shape[1:]
    half = width // 2
    triple = 3 * half
    letters_count = char_table.shape[0]
    r = project_weight.shape[0]
    grid = Grid(sizes)
    devices = grid.devices
    ff_blocks = up_weight.shape[1] // width
    low = jnp.bfloat16

    taps, tap_rows = merging_weight.shape[:2]
    down_rows = down_weight.shape[0]
    second_rows = jnp.concatenate(
        [
            down_weight,
            merging_weight.reshape(-1, width),
            one_below_other(up_weight, ff_blocks),
            char_weight,
        ],
        axis=0,
    )
    second_all = lax.all_gather(second_rows, AXES, axis=0)
    gains = jnp.stack(
        [attend_gain, attend_shift, feed_gain, feed_shift, char_gain, char_shift]
    ).reshape(1, 6 * r)
    own_table = char_table.T
    gain_rows = jnp.pad(gains, ((0, own_table.shape[0] - 1), (0, 0)))
    table_rows = jnp.concatenate([own_table, gain_rows], axis=1)
    table_rows = jnp.pad(table_rows, ((0, 0), (0, triple - table_rows.shape[1])))
    char_rows = jnp.concatenate(
        [
            side_by_side(recur_input.T, 3),
            side_by_side(recur_state.T, 3),
            one_below_other(table_rows, 3),
        ],
        axis=1,
    )
    char_rows = jnp.concatenate([char_rows, side_by_side(output_weight, 3)], axis=0)
    project_came = column_sends(grid, project_weight)
    project_came, char_rows = after(project_came, char_rows)
    char_came = column_sends(grid, char_rows)
    project_column = column_of(grid, project_weight, project_came)
    project_came = plane_sends(grid, project_column)
    project_came, char_came = after(project_came, char_came)
    char_column = column_of(grid, char_rows, char_came)
    char_came = plane_sends(grid, char_column)
    project_layer = plane_of(grid, project_column, project_came)
    project_full = cores_of(grid, project_layer, cores_sends(grid, project_layer))
    states, codes = token_states[0], char_codes[0]
    mixed = product(states, project_full).astype(low)
    context_low, log_totals = attend(mixed, lengths, width)
    char_came, context_low = after(char_came, context_low)
    char_layer = plane_of(grid, char_column, char_came)
    first_all = cores_of(grid, char_layer, cores_sends(grid, char_layer))
    first_all = first_all.reshape(devices, -1, 3 * width)
    output_full = whole(one_below_other(first_all[:, r:], 3))
    chars_all = first_all[:, :r]
    inlet_full = whole(one_below_other(chars_all[:, :, :width], 3))
    recur_full = whole(one_below_other(chars_all[:, :, width : width + triple], 3))
    table_all = side_by_side(chars_all[:, :, width + triple :], 3)
    table_full = whole(table_all[:, :, : pl.cdiv(letters_count, LANES) * LANES])
    gains_all = table_all[:, 0, letters_count : letters_count + 6 * r]
    gains_all = gains_all.reshape(devices, 6, r).transpose(1, 0, 2).reshape(6, width)
    gains_all = gains_all.astype(jnp.float32)

    def second(start, rows):
        return second_all[:, start : start + rows]

    up_start = down_rows + taps * tap_rows
    upper_full = whole(side_by_side(second(up_start, ff_blocks * r), ff_blocks))
    branch_full = whole(second(up_start + ff_blocks * r, r))

    def rows_spec(start, rows):
        if rows % 16 == 0 and start % rows == 0:
            place = start // rows
            return second_all, pl.BlockSpec(
                (devices, rows, width), lambda b: (0, place, 0), pipeline_mode=pl.Buffered(1)
            )
        part = second(start, rows).reshape(ff_blocks, -1, width)
        return part, pl.BlockSpec(part.shape, lambda b: (0, 0, 0), pipeline_mode=pl.Buffered(1))

    valid = lax.broadcasted_iota(jnp.int32, (length, 1), 0) < lengths
    embeds, chars_rep, char_states, coefs = chars_forward(
        codes, table_full, inlet_full, recur_full
    )
    first_pre = states.astype(jnp.float32) + product(context_low, output_full)
    first = norm_parts(first_pre)[0] * gains_all[0] + gains_all[1]
    joined = jnp.where(
        valid, jnp.concatenate([first.astype(low), chars_rep], axis=-1), jnp.zeros((), low)
    )
    merging_parts = [rows_spec(down_rows + i * tap_rows, tap_rows) for i in range(taps)]
    (
        token_stream,
        char_stream,
        summed_low,
        merged_low,
        hidden_low,
        feed_grad,
        hidden_grad,
        branch_grad,
        merging_grad,
        summed_grad,
        char_pre_grad,
        gain_sums,
    ) = feed(
        joined,
        first,
        chars_rep,
        token_cotangent[0],
        char_cotangent[0],
        gains_all,
        upper_full,
        branch_full,
        merging_parts,
        rows_spec(0, down_rows),
    )
    feed_gain_grad, feed_shift_grad, char_gain_grad, char_shift_grad = jnp.sum(gain_sums, axis=1)
    early = jnp.concatenate(
        [shares(outer_sum(hidden_low, feed_grad), devices)]
        + [
            shares(outer_sum(*pair), devices)
            for pair in (
                (joined[:-1], merging_grad[1:]),
                (joined, merging_grad),
                (joined[1:], merging_grad[:-1]),
            )
        ],
        axis=1,
    )
    early, merging_grad, summed_low, merged_low = after(
        early, merging_grad, summed_low, merged_low
    )
    early = lax.psum_scatter(early, AXES, scatter_dimension=0, tiled=True)[0]
    up_parts = jnp.concatenate(
        [
            shares(outer_sum(summed_low, hidden_grad), devices),
            shares(outer_sum(merged_low, branch_grad), devices),
        ],
        axis=2,
    )
    up_parts, merging_grad = after(up_parts, merging_grad)
    up_terms = core_terms(grid, up_parts)
    first_pre_grad, attended_grad, context_grad, rep_grad, attend_sums = merging_back(
        lengths,
        merging_grad,
        summed_grad,
        char_pre_grad,
        first_pre,
        gains_all,
        output_full,
        merging_parts,
    )
    up_terms, rep_grad, context_grad, attended_grad = after(
        up_terms, rep_grad, context_grad, attended_grad
    )
    attend_gain_grad, attend_shift_grad = jnp.sum(attend_sums, axis=1)
    up_layer, rep_grad = after(added_low(up_terms), rep_grad)
    up_terms = plane_terms(grid, up_layer)
    char_grads = chars_back(
        codes, inlet_full, recur_full, embeds, char_states, coefs, rep_grad, table_full.shape[1]
    )
    up_terms, char_grads, context_grad = after(up_terms, char_grads, context_grad)
    table_grad, inlet_grad, recur_weight_grad = char_grads
    up_column = added_low(up_terms)
    output_weight_grad = outer_sum(context_low, attended_grad)
    gain_grads = jnp.stack(
        [
            attend_gain_grad,
            attend_shift_grad,
            feed_gain_grad,
            feed_shift_grad,
            char_gain_grad,
            char_shift_grad,
        ]
    )
    gain_shares = gain_grads.reshape(6, devices, r).transpose(1, 0, 2).reshape(devices, 1, 6 * r)
    table_shares = shares(table_grad, devices)[:, :, :letters_count]
    gain_shares = jnp.pad(
        gain_shares.astype(low), ((0, 0), (0, table_shares.shape[1] - 1), (0, 0))
    )
    table_shares = jnp.concatenate([table_shares, gain_shares], axis=2)
    table_shares = jnp.pad(
        table_shares, ((0, 0), (0, 0), (0, triple - table_shares.shape[2]))
    )
    late = jnp.concatenate(
        [
            jnp.concatenate(
                [
                    side_by_side(shares(inlet_grad, devices), 3),
                    side_by_side(shares(recur_weight_grad, devices), 3),
                    one_below_other(table_shares, 3),
                ],
                axis=2,
            ),
            side_by_side(shares(output_weight_grad, devices), 3),
        ],
        axis=1,
    )
    def back(start, pairs, context_grad, earlier):
        return attend_back(
            mixed, context_grad, context_low, log_totals, lengths, width, start, pairs, earlier
        )

    every = width // LANES
    cuts = (0, every // 6, 5 * every // 6, every)
    up_column, late, context_grad = after(up_column, late, context_grad)
    up_terms = column_terms(grid, up_column)
    late_terms = core_terms(grid, late)
    grads = back(cuts[0], cuts[1] - cuts[0], context_grad, ())
    late_terms, grads, context_grad = after(late_terms, grads, context_grad)
    late_layer, context_grad = after(added_low(late_terms), context_grad)
    late_terms = plane_terms(grid, late_layer)
    grads = back(cuts[1], cuts[2] - cuts[1], context_grad, grads)
    late_terms, up_terms, grads, context_grad = after(late_terms, up_terms, grads, context_grad)
    late_column, context_grad = after(added_low(late_terms), context_grad)
    late_terms = column_terms(grid, late_column)
    grads = back(cuts[2], cuts[3] - cuts[2], context_grad, grads)
    mixed_grad = jnp.concatenate(grads, axis=-1)
    project_parts = shares(outer_sum(states, mixed_grad), devices)
    project_parts, late_terms = after(project_parts, late_terms)
    up_own, late = added(up_terms), added(late_terms)
    project_terms = core_terms(grid, project_parts)
    project_terms, early = after(project_terms, early)
    project_layer = added_low(project_terms)
    project_column = added_low(plane_terms(grid, project_layer))
    own_project = added(column_terms(grid, project_column))
    input_gradient = (first_pre_grad + back_product(mixed_grad, project_full)).astype(low)
    early = early.astype(jnp.float32)
    own_chars = late[:r]
    own_table_rows = side_by_side(own_chars[:, width + triple :], 3)
    own_gains = own_table_rows[0, letters_count : letters_count + 6 * r].reshape(6, r)
    return (
        token_stream[None],
        char_stream[None],
        input_gradient[None],
        own_table_rows[:, :letters_count].T,
        one_below_other(own_chars[:, :width], 3).T,
        one_below_other(own_chars[:, width : width + triple], 3).T,
        own_project,
        one_below_other(late[r:], 3),
        early[down_rows:].reshape(merging_weight.shape),
        up_own[:, : ff_blocks * width],
        early[:down_rows],
        up_own[:, ff_blocks * width :],
        own_gains[0],
        own_gains[1],
        own_gains[2],
        own_gains[3],
        own_gains[4],
        own_gains[5],
    )

def solution(mesh):
    placed = (
        P(AXES, None, None),
        P(AXES, None, None),
        P(AXES),
        P(AXES, None, None),
        P(AXES, None, None),
        P(None, AXES),
        P(None, AXES),
        P(None, AXES),
        P(AXES, None),
        P(AXES, None),
        P(None, AXES, None),
        P(AXES, None),
        P(AXES, None),
        P(AXES, None),
        P(AXES),
        P(AXES),
        P(AXES),
        P(AXES),
        P(AXES),
        P(AXES),
    )
    sizes = (mesh.shape["dp"], mesh.shape["fsdp"])
    return jax.shard_map(
        functools.partial(on_device, sizes),
        mesh=mesh,
        in_specs=placed,
        out_specs=(
            P(AXES, None, None),
            P(AXES, None, None),
            P(AXES, None, None),
            P(None, AXES),
            P(None, AXES),
            P(None, AXES),
            P(AXES, None),
            P(AXES, None),
            P(None, AXES, None),
            P(AXES, None),
            P(AXES, None),
            P(AXES, None),
            P(AXES),
            P(AXES),
            P(AXES),
            P(AXES),
            P(AXES),
            P(AXES),
        ),
        check_vma=False,
    )
```

```python
import functools
import itertools
import math

import jax
import jax.numpy as jnp
from jax import lax
from jax.experimental import pallas as pl
from jax.experimental.pallas import tpu as pltpu
from jax.sharding import PartitionSpec as P

HEAD_DIM = 64
CHARS = 4
LANES = 128
EPS = 1e-05
MASKED = -1e30
SCALE = 1.0 / math.sqrt(HEAD_DIM)
SCALE2 = math.log2(math.e) / math.sqrt(HEAD_DIM)
AXES = ("dp", "fsdp")
VMEM_LIMIT = 56 * 1024 * 1024
BRIEF = pl.CostEstimate(flops=200 * 10**9, bytes_accessed=10**6, transcendentals=0)

def product(left, right):
    return jnp.dot(left, right, preferred_element_type=jnp.float32)


def outer_sum(left, right):
    return jnp.einsum("li,lo->io", left, right, preferred_element_type=jnp.float32)


def back_product(grad_rows, weight):
    return jnp.einsum("lo,io->li", grad_rows, weight, preferred_element_type=jnp.float32)


def dotf(a,b,ca=1,cb=0):
    return lax.dot_general(a,b,(((ca,),(cb,)),((),())),preferred_element_type=jnp.float32)

def lane_half(shape):
    return lax.broadcasted_iota(jnp.int32, shape, 1) < HEAD_DIM

def attend_kernel(rows, length_ref, q_ref, k_ref, v_ref, ctx_ref, lse_ref, kx_ref, vx_ref):
    length = k_ref.shape[0]
    lane = lax.broadcasted_iota(jnp.int32, (length, LANES), 1)
    place = lax.broadcasted_iota(jnp.int32, (length, LANES), 0)
    kx_ref[:, :LANES] = k_ref[...]
    kx_ref[:, LANES:] = jnp.where((lane == 0) & (place >= length_ref[0]), MASKED, 0.0).astype(jnp.bfloat16)
    vx_ref[:, :LANES] = v_ref[...]
    vx_ref[:, LANES:] = jnp.ones((length, LANES), jnp.bfloat16)
    low = lane_half((rows, LANES))
    one = jnp.where(lax.broadcasted_iota(jnp.int32, (rows, LANES), 1) == 0, 1.0, 0.0).astype(jnp.bfloat16)
    def step(c, _):
        at = pl.ds(pl.multiple_of(c * rows, rows), rows)
        q = q_ref[at, :].astype(jnp.float32)
        outs = []
        for h in range(2):
            mine = low if h == 0 else jnp.logical_not(low)
            qx = jnp.concatenate([jnp.where(mine, q, 0.0).astype(jnp.bfloat16), one], axis=1)
            s = dotf(qx, kx_ref[...], 1, 1)
            peak = jnp.max(s, axis=1, keepdims=True) * SCALE2
            p = jnp.exp2(s * SCALE2 - peak).astype(jnp.bfloat16)
            o = dotf(p, vx_ref[...])
            total = o[:, LANES:]
            outs.append((o[:, :LANES] / total, peak + jnp.log2(total)))
        ctx_ref[at, :] = jnp.where(low, outs[0][0], outs[1][0]).astype(jnp.bfloat16)
        lse_ref[at, :] = jnp.where(low, outs[0][1], outs[1][1])
        return 0
    lax.fori_loop(0, length // rows, step, 0, unroll=True)

def attend(mixed, lengths, width, rows=256):
    length = mixed.shape[0]
    pairs = width // LANES
    spec = lambda o: pl.BlockSpec((length, LANES), lambda p, o=o: (0, p+o))
    return pl.pallas_call(
        functools.partial(attend_kernel, rows),
        grid=(pairs,),
        in_specs=[pl.BlockSpec(memory_space=pltpu.SMEM), spec(0), spec(pairs), spec(2 * pairs)],
        out_specs=[spec(0), spec(0)],
        out_shape=[jax.ShapeDtypeStruct((length, width), jnp.bfloat16), jax.ShapeDtypeStruct((length, width), jnp.float32)],
        scratch_shapes=[pltpu.VMEM((length, 2*LANES), jnp.bfloat16), pltpu.VMEM((length, 2*LANES), jnp.bfloat16)],
        compiler_params=pltpu.CompilerParams(vmem_limit_bytes=VMEM_LIMIT),
        cost_estimate=BRIEF,
    )(lengths, mixed, mixed, mixed)

def back_kernel(rows, length_ref, q_ref, k_ref, v_ref, do_ref, o_ref, lse_ref, *rest):
    dq_ref, dk_out, dv_out, kx_ref, qt_ref, dot_ref, dk_ref, dv_ref = rest[-8:]
    length = k_ref.shape[0]
    lane = lax.broadcasted_iota(jnp.int32, (length, LANES), 1)
    place = lax.broadcasted_iota(jnp.int32, (length, LANES), 0)
    kx_ref[:, :LANES] = k_ref[...]
    kx_ref[:, LANES:] = jnp.where((lane == 0) & (place >= length_ref[0]), MASKED, 0.0).astype(jnp.bfloat16)
    qt_ref[...] = q_ref[...].T
    dot_ref[...] = do_ref[...].T
    dk_ref[...] = jnp.zeros_like(dk_ref)
    dv_ref[...] = jnp.zeros_like(dv_ref)
    low = lane_half((rows, LANES))
    one = jnp.where(lax.broadcasted_iota(jnp.int32, (rows, LANES), 1) == 0, 1.0, 0.0).astype(jnp.bfloat16)
    def step(c, _):
        at = pl.ds(pl.multiple_of(c * rows, rows), rows)
        q = q_ref[at, :].astype(jnp.float32)
        do = do_ref[at, :].astype(jnp.float32)
        doo = do * o_ref[at, :].astype(jnp.float32)
        lse = lse_ref[at, :]
        dqs = []
        for h in range(2):
            mine = low if h == 0 else jnp.logical_not(low)
            qx = jnp.concatenate([jnp.where(mine, q, 0.0).astype(jnp.bfloat16), one], axis=1)
            s = dotf(qx, kx_ref[...], 1, 1)
            p = jnp.exp2(s * SCALE2 - lse[:, h*HEAD_DIM:h*HEAD_DIM+1])
            dp = dotf(jnp.where(mine, do, 0.0).astype(jnp.bfloat16), v_ref[...], 1, 1)
            delta = jnp.sum(jnp.where(mine, doo, 0.0), axis=1, keepdims=True)
            ds = (p * (dp - delta)).astype(jnp.bfloat16)
            pb = p.astype(jnp.bfloat16)
            hs = slice(h*HEAD_DIM, (h+1)*HEAD_DIM)
            dqs.append(dotf(ds, k_ref[...]))
            dk_ref[hs, :] += dotf(qt_ref[hs, at], ds)
            dv_ref[hs, :] += dotf(dot_ref[hs, at], pb)
        dq_ref[at, :] = (jnp.where(low, dqs[0], dqs[1]) * SCALE).astype(jnp.bfloat16)
        return 0
    lax.fori_loop(0, length // rows, step, 0, unroll=True)
    dk_out[...] = (dk_ref[...] * SCALE).T.astype(jnp.bfloat16)
    dv_out[...] = dv_ref[...].T.astype(jnp.bfloat16)

def attend_back(
    mixed, context_grad, context, log_totals, lengths, width, start, pairs, earlier, rows=256
):
    length = mixed.shape[0]
    every = width // LANES
    spec = lambda o: pl.BlockSpec((length, LANES), lambda p, o=o: (0, p + o + start))
    scratch = lambda a, b, t: pltpu.VMEM((a, b), t)
    return pl.pallas_call(
        functools.partial(back_kernel, rows),
        grid=(pairs,),
        in_specs=[pl.BlockSpec(memory_space=pltpu.SMEM), spec(0), spec(every), spec(2 * every)]
        + [spec(0)] * 3
        + [pl.BlockSpec(memory_space=pl.ANY)] * len(earlier),
        out_specs=[spec(0)] * 3,
        out_shape=[jax.ShapeDtypeStruct((length, width), jnp.bfloat16)] * 3,
        input_output_aliases={7 + i: i for i in range(len(earlier))},
        scratch_shapes=[
            scratch(length, 2 * LANES, jnp.bfloat16),
            scratch(LANES, length, jnp.bfloat16),
            scratch(LANES, length, jnp.bfloat16),
            scratch(LANES, length, jnp.float32),
            scratch(LANES, length, jnp.float32),
        ],
        compiler_params=pltpu.CompilerParams(vmem_limit_bytes=VMEM_LIMIT),
        cost_estimate=BRIEF,
    )(lengths, mixed, mixed, mixed, context_grad, context, log_totals, *earlier)


ROOT_HALF = math.sqrt(0.5)
DENSITY = 1.0 / math.sqrt(2.0 * math.pi)

def gelu_both(values):
    below = 0.5 + 0.5 * lax.erf(values * ROOT_HALF)
    return values * below, below + values * (DENSITY * jnp.exp(-0.5 * values * values))

def norm_parts(values):
    average = jnp.mean(values, axis=-1, keepdims=True)
    centred = values - average
    spread = lax.rsqrt(jnp.mean(centred * centred, axis=-1, keepdims=True) + EPS)
    return centred * spread, spread

def norm_back(normed, spread, scaled):
    return spread * (scaled - jnp.mean(scaled, axis=-1, keepdims=True)
                     - normed * jnp.mean(scaled * normed, axis=-1, keepdims=True))

def column_sums(values):
    rows, width = values.shape
    return jnp.sum(values.reshape(rows // 8, 8, width), axis=0)

def chars_kernel(half, codes_ref, table_ref, inlet_ref, recur_ref, embed_ref, rep_ref, states_ref, coef_ref):
    rows = codes_ref.shape[0]
    triple = 3 * half
    width = embed_ref.shape[1] // CHARS
    letters = lax.broadcasted_iota(jnp.int32, (rows, table_ref.shape[1]), 1)
    embeds = []
    for slot in range(CHARS):
        picked = jnp.where(codes_ref[:, slot : slot + 1] == letters, 1.0, 0.0).astype(jnp.bfloat16)
        embed = dotf(picked, table_ref[...], 1, 1).astype(jnp.bfloat16)
        embed_ref[:, slot * width : (slot + 1) * width] = embed
        embeds.append(embed)
    low = jnp.bfloat16
    states = [None, None]
    for step, side in itertools.product(range(CHARS), range(2)):
        slot = step if side == 0 else CHARS - 1 - step
        base = side * triple
        state = states[side]
        gates = dotf(embeds[slot], inlet_ref[base : base + triple, :], 1, 1)
        if state is None:
            update = jax.nn.sigmoid(gates[:, half : 2 * half])
            fresh = jnp.tanh(gates[:, 2 * half :])
            new = (1.0 - update) * fresh
            coef_ref[side, 0] = ((1.0 - update) * (1.0 - fresh * fresh)).astype(low)
            coef_ref[side, 1] = (-fresh * update * (1.0 - update)).astype(low)
        else:
            recur = dotf(state, recur_ref[base : base + triple, :], 1, 1)
            reset = jax.nn.sigmoid(gates[:, :half] + recur[:, :half])
            update = jax.nn.sigmoid(gates[:, half : 2 * half] + recur[:, half : 2 * half])
            recur_new = recur[:, 2 * half :]
            fresh = jnp.tanh(gates[:, 2 * half :] + reset * recur_new)
            before = state.astype(jnp.float32)
            new = (1.0 - update) * fresh + update * before
            at = 2 + 5 * (step - 1)
            coef_ref[side, at] = ((1.0 - update) * (1.0 - fresh * fresh)).astype(low)
            coef_ref[side, at + 1] = ((before - fresh) * update * (1.0 - update)).astype(low)
            coef_ref[side, at + 2] = (recur_new * reset * (1.0 - reset)).astype(low)
            coef_ref[side, at + 3] = reset.astype(low)
            coef_ref[side, at + 4] = update.astype(low)
        states[side] = new.astype(low)
        if step < CHARS - 1:
            states_ref[side, step] = states[side]
    for side in range(2):
        rep_ref[:, side * half : (side + 1) * half] = states[side]


COEFS = 2 + 5 * (CHARS - 1)

def chars_forward(codes, table, inlet, recur, rows=256):
    length = codes.shape[0]
    embed, half = inlet.shape[1], recur.shape[1]
    low = jnp.bfloat16
    full = lambda a: pl.BlockSpec(a.shape, lambda b: (0, 0))
    return pl.pallas_call(
        functools.partial(chars_kernel, half),
        grid=(length // rows,),
        in_specs=[pl.BlockSpec((rows, CHARS), lambda b: (b, 0)), full(table), full(inlet), full(recur)],
        out_specs=[
            pl.BlockSpec((rows, CHARS * embed), lambda b: (b, 0)),
            pl.BlockSpec((rows, 2 * half), lambda b: (b, 0)),
            pl.BlockSpec((2, CHARS - 1, rows, half), lambda b: (0, 0, b, 0)),
            pl.BlockSpec((2, COEFS, rows, half), lambda b: (0, 0, b, 0)),
        ],
        out_shape=[
            jax.ShapeDtypeStruct((length, CHARS * embed), low),
            jax.ShapeDtypeStruct((length, 2 * half), low),
            jax.ShapeDtypeStruct((2, CHARS - 1, length, half), low),
            jax.ShapeDtypeStruct((2, COEFS, length, half), low),
        ],
        compiler_params=pltpu.CompilerParams(vmem_limit_bytes=VMEM_LIMIT),
        cost_estimate=BRIEF,
    )(codes, table, inlet, recur)

def chars_back_kernel(half, codes_ref, inlet_ref, recur_ref, embed_ref, states_ref, coef_ref, grad_ref,
                      table_out, inlet_out, recur_out, gates_ref, lets_ref, steps_ref, table_acc, inlet_acc, recur_acc):
    rows = codes_ref.shape[0]
    triple = 3 * half
    width = embed_ref.shape[1] // CHARS
    low = jnp.bfloat16
    first, last = pl.program_id(0) == 0, pl.program_id(0) == pl.num_programs(0) - 1

    @pl.when(first)
    def _():
        table_acc[...] = jnp.zeros_like(table_acc)
        inlet_acc[...] = jnp.zeros_like(inlet_acc)
        recur_acc[...] = jnp.zeros_like(recur_acc)

    grads = [grad_ref[:, side * half : (side + 1) * half] for side in range(2)]
    for step, side in itertools.product(range(CHARS - 1, -1, -1), range(2)):
        slot = step if side == 0 else CHARS - 1 - step
        base = side * triple
        grad = grads[side]
        at = 2 + 5 * (step - 1) if step else 0
        load = lambda k: coef_ref[side, at + k].astype(jnp.float32)
        fresh_pre = grad * load(0)
        update_pre = (grad * load(1)).astype(low)
        spot = slice(slot * rows, (slot + 1) * rows)
        gates_ref[spot, base + half : base + 2 * half] = update_pre
        gates_ref[spot, base + 2 * half : base + triple] = fresh_pre.astype(low)
        if step == 0:
            gates_ref[spot, base : base + half] = jnp.zeros((rows, half), low)
            continue
        reset_pre = (fresh_pre * load(2)).astype(low)
        gates_ref[spot, base : base + half] = reset_pre
        recur_grad = jnp.concatenate(
            [reset_pre, update_pre, (fresh_pre * load(3)).astype(low)], axis=1)
        steps_ref[side, (step - 1) * rows : step * rows] = recur_grad
        grads[side] = grad * load(4) + dotf(recur_grad, recur_ref[base : base + triple, :])
    for side in range(2):
        base = side * triple
        states = states_ref[side].reshape(-1, half)
        recur_acc[:, base : base + triple] += dotf(states, steps_ref[side], 0, 0)
    embed_all = jnp.concatenate([embed_ref[:, j * width : (j + 1) * width] for j in range(CHARS)], axis=0)
    inlet_acc[...] += dotf(embed_all, gates_ref[...], 0, 0)
    embed_grad = dotf(gates_ref[...], inlet_ref[...]).astype(low)
    letters = lax.broadcasted_iota(jnp.int32, (rows, table_acc.shape[1]), 1)
    for slot in range(CHARS):
        lets_ref[slot * rows : (slot + 1) * rows, :] = jnp.where(
            codes_ref[:, slot : slot + 1] == letters, 1.0, 0.0).astype(low)
    table_acc[...] += dotf(embed_grad, lets_ref[...], 0, 0)

    @pl.when(last)
    def _():
        table_out[...] = table_acc[...].astype(low)
        for start in range(0, 2 * triple, half):
            cols = slice(start, start + half)
            inlet_out[cols, :] = inlet_acc[:, cols].T.astype(low)
            recur_out[cols, :] = recur_acc[:, cols].T.astype(low)


def chars_back(codes, inlet, recur, embeds, states, coefs, grad, letters, rows=256):
    length = codes.shape[0]
    embed, half = inlet.shape[1], recur.shape[1]
    low = jnp.bfloat16
    full = lambda a: pl.BlockSpec(a.shape, lambda b: (0, 0))
    outs = [(embed, letters), inlet.shape, recur.shape]
    return pl.pallas_call(
        functools.partial(chars_back_kernel, half),
        grid=(length // rows,),
        in_specs=[
            pl.BlockSpec((rows, CHARS), lambda b: (b, 0)), full(inlet), full(recur),
            pl.BlockSpec((rows, CHARS * embed), lambda b: (b, 0)),
            pl.BlockSpec((2, CHARS - 1, rows, half), lambda b: (0, 0, b, 0)),
            pl.BlockSpec((2, COEFS, rows, half), lambda b: (0, 0, b, 0)),
            pl.BlockSpec((rows, 2 * half), lambda b: (b, 0)),
        ],
        out_specs=[pl.BlockSpec(s, lambda b: (0, 0)) for s in outs],
        out_shape=[jax.ShapeDtypeStruct(s, low) for s in outs],
        scratch_shapes=[
            pltpu.VMEM((CHARS * rows, 6 * half), low),
            pltpu.VMEM((CHARS * rows, letters), low),
            pltpu.VMEM((2, (CHARS - 1) * rows, 3 * half), low),
            pltpu.VMEM((embed, letters), jnp.float32),
            pltpu.VMEM(inlet.shape[::-1], jnp.float32),
            pltpu.VMEM(recur.shape[::-1], jnp.float32),
        ],
        compiler_params=pltpu.CompilerParams(vmem_limit_bytes=VMEM_LIMIT),
        cost_estimate=BRIEF,
    )(codes, inlet, recur, embeds, states, coefs, grad)

def flat(ref, part=0, parts=1):
    count = ref.shape[0] // parts
    block = ref[part * count : (part + 1) * count]
    return block.reshape(-1, block.shape[-1])


PAD = 8


def spread_rows(rows_ref, wide_ref):
    length, width = rows_ref.shape
    blank = jnp.zeros((PAD, width), jnp.float32)
    wide_ref[:PAD] = blank
    wide_ref[PAD + length :] = blank
    for start in range(0, length, 256):
        block = rows_ref[start : start + 256]
        wide_ref[PAD + start : PAD + start + block.shape[0]] = block.astype(jnp.float32)


def neighbours(wide_ref, rows):
    base = pl.multiple_of(pl.program_id(0) * rows, rows)
    window = wide_ref[pl.ds(base, rows + 2 * PAD)]
    return [window[PAD + i : PAD + i + rows].astype(jnp.bfloat16) for i in (-1, 0, 1)]


def feed_kernel(blocks, joined_ref, first_ref, rep_ref, token_cot_ref, char_cot_ref, gains_ref,
                up_ref, branch_ref, tap0_ref, tap1_ref, tap2_ref, down_ref,
                token_ref, char_ref, summed_ref, merged_ref, hidden_ref, feed_grad_ref, hidden_grad_ref,
                branch_grad_ref, merging_grad_ref, summed_grad_ref, char_grad_ref, sums_ref, slope_ref, wide_ref):
    low = jnp.bfloat16
    width = first_ref.shape[1]
    step = up_ref.shape[1] // blocks
    merging_refs = (tap0_ref, tap1_ref, tap2_ref)

    @pl.when(pl.program_id(0) == 0)
    def _():
        sums_ref[...] = jnp.zeros_like(sums_ref)
        spread_rows(joined_ref, wide_ref)

    merging_pre = 0.0
    for moved, ref in zip(neighbours(wide_ref, first_ref.shape[0]), merging_refs):
        merging_pre = merging_pre + dotf(moved, flat(ref))
    merged, merging_slope = gelu_both(merging_pre)
    merged_low = merged.astype(low)
    merged_ref[...] = merged_low
    summed = first_ref[...] + merged
    summed_low = summed.astype(low)
    summed_ref[...] = summed_low
    total = summed
    for c in range(blocks):
        cols = slice(c * step, (c + 1) * step)
        hidden, slope = gelu_both(dotf(summed_low, up_ref[:, cols]))
        slope_ref[:, cols] = slope
        hidden_low = hidden.astype(low)
        hidden_ref[:, cols] = hidden_low
        total = total + dotf(hidden_low, flat(down_ref, c, blocks))
    normed, spread = norm_parts(total)
    gain, shift = gains_ref[2:3, :], gains_ref[3:4, :]
    token_ref[...] = (normed * gain + shift).astype(low)
    cot = token_cot_ref[...].astype(jnp.float32)
    sums_ref[0] += column_sums(cot * normed)
    sums_ref[1] += column_sums(cot)
    token_grad = norm_back(normed, spread, cot * gain)
    feed_grad = token_grad.astype(low)
    feed_grad_ref[...] = feed_grad
    total = token_grad
    for c in range(blocks):
        cols = slice(c * step, (c + 1) * step)
        hidden_grad = (slope_ref[:, cols] * dotf(feed_grad, flat(down_ref, c, blocks), 1, 1)).astype(low)
        hidden_grad_ref[:, cols] = hidden_grad
        total = total + dotf(hidden_grad, up_ref[:, cols], 1, 1)
    summed_grad_ref[...] = total
    normed, spread = norm_parts(rep_ref[...].astype(jnp.float32) + dotf(merged_low, branch_ref[...]))
    gain, shift = gains_ref[4:5, :], gains_ref[5:6, :]
    char_ref[...] = (normed * gain + shift).astype(low)
    cot = char_cot_ref[...].astype(jnp.float32)
    sums_ref[2] += column_sums(cot * normed)
    sums_ref[3] += column_sums(cot)
    char_grad = norm_back(normed, spread, cot * gain)
    char_grad_ref[...] = char_grad
    branch_grad = char_grad.astype(low)
    branch_grad_ref[...] = branch_grad
    merging_grad_ref[...] = (merging_slope * (total + dotf(branch_grad, branch_ref[...], 1, 1))).astype(low)

def feed(joined, first, rep, token_cot, char_cot, gains, up, branch, merging, down, rows=256, blocks=2):
    length, width = first.shape
    ff = up.shape[1]
    low, wide = jnp.bfloat16, jnp.float32
    row = lambda w: pl.BlockSpec((rows, w), lambda b: (b, 0))
    full = lambda a: pl.BlockSpec(a.shape, lambda b: (0,) * a.ndim, pipeline_mode=pl.Buffered(1))
    outs = [(width, low), (width, low), (width, low), (width, low), (ff, low), (width, low), (ff, low),
            (width, low), (width, low), (width, wide), (width, wide)]
    return pl.pallas_call(
        functools.partial(feed_kernel, blocks),
        grid=(length // rows,),
        in_specs=[full(joined), row(width), row(width), row(width), row(width), full(gains),
                  full(up), full(branch)] + [spec for _, spec in merging + [down]],
        out_specs=[row(w) for w, _ in outs] + [pl.BlockSpec((4, 8, width), lambda b: (0, 0, 0))],
        out_shape=[jax.ShapeDtypeStruct((length, w), t) for w, t in outs] + [jax.ShapeDtypeStruct((4, 8, width), wide)],
        scratch_shapes=[pltpu.VMEM((rows, ff), wide), pltpu.VMEM((length + 2 * PAD, joined.shape[1]), wide)],
        compiler_params=pltpu.CompilerParams(vmem_limit_bytes=VMEM_LIMIT),
        cost_estimate=BRIEF,
    )(joined, first, rep, token_cot, char_cot, gains, up, branch, *[part for part, _ in merging + [down]])


def early_kernel(hidden_ref, joined_ref, feed_grad_ref, merging_grad_ref, out_ref, wide_ref, moved_ref):
    low = jnp.bfloat16
    count, _, width = out_ref.shape
    length = feed_grad_ref.shape[0]

    @pl.when(pl.program_id(0) == 0)
    def _():
        spread_rows(merging_grad_ref, wide_ref)
        for start in range(0, length, 256):
            window = wide_ref[start : start + 256 + 2 * PAD]
            for i, shift in enumerate((1, 0, -1)):
                moved_ref[i, start : start + 256] = window[PAD + shift : PAD + shift + 256].astype(low)

    def put(start, terms):
        terms = terms.astype(low).reshape(count, -1, width)
        out_ref[:, start : start + terms.shape[1]] = terms

    down = hidden_ref.shape[1] // count
    rows = joined_ref.shape[1] // count
    put(0, dotf(hidden_ref[...], feed_grad_ref[...], 0, 0))
    for i in range(moved_ref.shape[0]):
        put(down + i * rows, dotf(joined_ref[...], moved_ref[i], 0, 0))


def early_parts(hidden, joined, feed_grad, merging_grad, devices, taps=3, groups=4):
    length, width = feed_grad.shape
    low = jnp.bfloat16
    down, rows = hidden.shape[1] // devices, joined.shape[1] // devices
    if down % 16 or rows % 16:
        pairs = [(hidden, feed_grad)]
        pairs += [(joined[:-1], merging_grad[1:]), (joined, merging_grad), (joined[1:], merging_grad[:-1])]
        return jnp.concatenate([shares(outer_sum(*pair), devices) for pair in pairs], axis=1)
    columns = lambda a: pl.BlockSpec((length, a.shape[1] // groups), lambda g: (0, g))
    full = pl.BlockSpec((length, width), lambda g: (0, 0))
    shape = (devices, down + taps * rows, width)
    return pl.pallas_call(
        early_kernel,
        grid=(groups,),
        in_specs=[columns(hidden), columns(joined), full, full],
        out_specs=pl.BlockSpec((devices // groups,) + shape[1:], lambda g: (g, 0, 0)),
        out_shape=jax.ShapeDtypeStruct(shape, low),
        scratch_shapes=[
            pltpu.VMEM((length + 2 * PAD, width), jnp.float32),
            pltpu.VMEM((taps, length, width), low),
        ],
        compiler_params=pltpu.CompilerParams(vmem_limit_bytes=VMEM_LIMIT),
        cost_estimate=BRIEF,
    )(hidden, joined, feed_grad, merging_grad)


def merging_back_kernel(length_ref, grad_ref, summed_ref, char_ref, pre_ref, gains_ref, output_ref,
                        tap0_ref, tap1_ref, tap2_ref,
                        pre_grad_ref, attended_ref, context_ref, rep_ref, sums_ref, wide_ref):
    rows, width = pre_ref.shape
    low = jnp.bfloat16

    @pl.when(pl.program_id(0) == 0)
    def _():
        sums_ref[...] = jnp.zeros_like(sums_ref)
        spread_rows(grad_ref, wide_ref)

    joined = 0.0
    for moved, ref in zip(neighbours(wide_ref, rows), (tap2_ref, tap1_ref, tap0_ref)):
        joined = joined + dotf(moved, flat(ref), 1, 1)
    place = pl.program_id(0) * rows + lax.broadcasted_iota(jnp.int32, (rows, 1), 0)
    joined = jnp.where(place < length_ref[0], joined, 0.0)
    rep_ref[...] = char_ref[...] + joined[:, width:]
    first_grad = summed_ref[...] + joined[:, :width]
    normed, spread = norm_parts(pre_ref[...])
    sums_ref[0] += column_sums(first_grad * normed)
    sums_ref[1] += column_sums(first_grad)
    pre_grad = norm_back(normed, spread, first_grad * gains_ref[0:1, :])
    pre_grad_ref[...] = pre_grad
    attended = pre_grad.astype(low)
    attended_ref[...] = attended
    context_ref[...] = dotf(attended, output_ref[...], 1, 1).astype(low)


def merging_back(lengths, grad, summed_grad, char_grad, pre, gains, output, merging, rows=256):
    length, width = pre.shape
    low, wide = jnp.bfloat16, jnp.float32
    row = pl.BlockSpec((rows, width), lambda b: (b, 0))
    full = lambda a: pl.BlockSpec(a.shape, lambda b: (0, 0), pipeline_mode=pl.Buffered(1))
    kinds = (wide, low, low, wide)
    return pl.pallas_call(
        merging_back_kernel,
        grid=(length // rows,),
        in_specs=[pl.BlockSpec(memory_space=pltpu.SMEM), full(grad), row, row, row, full(gains), full(output)]
        + [spec for _, spec in merging],
        out_specs=[row] * 4 + [pl.BlockSpec((2, 8, width), lambda b: (0, 0, 0))],
        out_shape=[jax.ShapeDtypeStruct((length, width), t) for t in kinds]
        + [jax.ShapeDtypeStruct((2, 8, width), wide)],
        scratch_shapes=[pltpu.VMEM((length + 2 * PAD, width), wide)],
        compiler_params=pltpu.CompilerParams(vmem_limit_bytes=VMEM_LIMIT),
        cost_estimate=BRIEF,
    )(lengths, grad, summed_grad, char_grad, pre, gains, output, *[part for part, _ in merging])


def side_by_side(rows, groups):
    r = rows.shape[-2] // groups
    return jnp.concatenate(
        [rows[..., i * r : (i + 1) * r, :] for i in range(groups)], axis=-1
    )


def one_below_other(rows, groups):
    w = rows.shape[-1] // groups
    return jnp.concatenate(
        [rows[..., i * w : (i + 1) * w] for i in range(groups)], axis=-2
    )


def whole(part):
    return part.reshape(-1, part.shape[-1])


def shares(full, devices):
    return full.reshape(devices, -1, full.shape[-1]).astype(jnp.bfloat16)


class Grid:
    def __init__(self, sizes):
        dp, fsdp = sizes
        z = 4 if dp % 4 == 0 else 1
        core = 2 if fsdp % 2 == 0 else 1
        self.fsdp = fsdp
        self.shape = (z, dp // z, fsdp // core, core)
        self.devices = dp * fsdp

    def own(self):
        z, x, y, core = self.shape
        dp, fsdp = lax.axis_index("dp"), lax.axis_index("fsdp")
        return dp // x, dp % x, fsdp // core, fsdp % core

    def send(self, values, shift):
        pairs = []
        for source, place in enumerate(itertools.product(*map(range, self.shape))):
            target = 0
            for at, by, size in zip(place, shift, self.shape):
                target = target * size + (at + by) % size
            pairs.append((source, target))
        return lax.ppermute(values, AXES, pairs)

    def plane(self):
        z, x, y, core = self.shape
        return [(i, j) for i in range(x) for j in range(y) if i or j]


def column_sends(grid, part):
    return [grid.send(part, (s, 0, 0, 0)) for s in range(1, grid.shape[0])]


def column_of(grid, part, came):
    nz = grid.shape[0]
    z = grid.own()[0]
    column = jnp.zeros((nz,) + part.shape, part.dtype)
    for s, piece in enumerate([part] + came):
        column = lax.dynamic_update_slice(column, piece[None], ((z - s) % nz, 0, 0))
    return column


def plane_sends(grid, column):
    return [grid.send(column, (0, i, j, 0)) for i, j in grid.plane()]


def plane_of(grid, column, came):
    nz, nx, ny, _ = grid.shape
    _, x, y, _ = grid.own()
    layer = jnp.zeros((nz, nx, ny) + column.shape[1:], column.dtype)
    for (i, j), piece in zip([(0, 0)] + grid.plane(), [column] + came):
        layer = lax.dynamic_update_slice(
            layer, piece[:, None, None], (0, (x - i) % nx, (y - j) % ny, 0, 0)
        )
    return layer


def cores_sends(grid, layer):
    return [grid.send(layer, (0, 0, 0, s)) for s in range(1, grid.shape[3])]


def cores_of(grid, layer, came):
    ncore = grid.shape[3]
    core = grid.own()[3]
    full = jnp.zeros(grid.shape + layer.shape[3:], layer.dtype)
    for s, piece in enumerate([layer] + came):
        full = lax.dynamic_update_slice(
            full, piece[:, :, :, None], (0, 0, 0, (core - s) % ncore, 0, 0)
        )
    return full.reshape(-1, layer.shape[-1])


def core_terms(grid, parts):
    ncore = grid.shape[3]
    core = grid.own()[3]
    parts = parts.reshape(grid.shape + parts.shape[1:])
    terms = [lax.dynamic_index_in_dim(parts, core, 3, False)]
    for s in range(1, ncore):
        chunk = lax.dynamic_index_in_dim(parts, (core + s) % ncore, 3, False)
        terms.append(grid.send(chunk, (0, 0, 0, s)))
    return terms


def plane_terms(grid, layer):
    nz, nx, ny, _ = grid.shape
    _, x, y, _ = grid.own()
    rows, width = layer.shape[3:]

    def of(i, j):
        return lax.dynamic_slice(layer, (0, i, j, 0, 0), (nz, 1, 1, rows, width))[:, 0, 0]

    return [of(x, y)] + [
        grid.send(of((x + i) % nx, (y + j) % ny), (0, i, j, 0)) for i, j in grid.plane()
    ]


def column_terms(grid, column):
    nz = grid.shape[0]
    z = grid.own()[0]
    terms = [lax.dynamic_index_in_dim(column, z, 0, False)]
    for s in range(1, nz):
        chunk = lax.dynamic_index_in_dim(column, (z + s) % nz, 0, False)
        terms.append(grid.send(chunk, (s, 0, 0, 0)))
    return terms


def added(terms):
    return functools.reduce(lambda a, b: a + b, [t.astype(jnp.float32) for t in terms])


def added_low(terms):
    return added(terms).astype(jnp.bfloat16)


def after(first, *then):
    return lax.optimization_barrier((first,) + then)


def on_device(
    sizes,
    token_states,
    char_codes,
    lengths,
    token_cotangent,
    char_cotangent,
    char_table,
    recur_input,
    recur_state,
    project_weight,
    output_weight,
    merging_weight,
    up_weight,
    down_weight,
    char_weight,
    attend_gain,
    attend_shift,
    feed_gain,
    feed_shift,
    char_gain,
    char_shift,
):
    length, width = token_states.shape[1:]
    half = width // 2
    triple = 3 * half
    letters_count = char_table.shape[0]
    r = project_weight.shape[0]
    grid = Grid(sizes)
    devices = grid.devices
    ff_blocks = up_weight.shape[1] // width
    low = jnp.bfloat16

    taps, tap_rows = merging_weight.shape[:2]
    down_rows = down_weight.shape[0]
    second_rows = jnp.concatenate(
        [
            down_weight,
            merging_weight.reshape(-1, width),
            one_below_other(up_weight, ff_blocks),
            char_weight,
        ],
        axis=0,
    )
    second_all = lax.all_gather(second_rows, AXES, axis=0)
    gains = jnp.stack(
        [attend_gain, attend_shift, feed_gain, feed_shift, char_gain, char_shift]
    ).reshape(1, 6 * r)
    own_table = char_table.T
    gain_rows = jnp.pad(gains, ((0, own_table.shape[0] - 1), (0, 0)))
    table_rows = jnp.concatenate([own_table, gain_rows], axis=1)
    table_rows = jnp.pad(table_rows, ((0, 0), (0, triple - table_rows.shape[1])))
    char_rows = jnp.concatenate(
        [
            side_by_side(recur_input.T, 3),
            side_by_side(recur_state.T, 3),
            one_below_other(table_rows, 3),
        ],
        axis=1,
    )
    char_rows = jnp.concatenate([char_rows, side_by_side(output_weight, 3)], axis=0)
    project_came = column_sends(grid, project_weight)
    project_came, char_rows = after(project_came, char_rows)
    char_came = column_sends(grid, char_rows)
    project_column = column_of(grid, project_weight, project_came)
    project_came = plane_sends(grid, project_column)
    project_came, char_came = after(project_came, char_came)
    char_column = column_of(grid, char_rows, char_came)
    char_came = plane_sends(grid, char_column)
    project_layer = plane_of(grid, project_column, project_came)
    project_full = cores_of(grid, project_layer, cores_sends(grid, project_layer))
    states, codes = token_states[0], char_codes[0]
    mixed = product(states, project_full).astype(low)
    context_low, log_totals = attend(mixed, lengths, width)
    char_came, context_low = after(char_came, context_low)
    char_layer = plane_of(grid, char_column, char_came)
    first_all = cores_of(grid, char_layer, cores_sends(grid, char_layer))
    first_all = first_all.reshape(devices, -1, 3 * width)
    output_full = whole(one_below_other(first_all[:, r:], 3))
    chars_all = first_all[:, :r]
    inlet_full = whole(one_below_other(chars_all[:, :, :width], 3))
    recur_full = whole(one_below_other(chars_all[:, :, width : width + triple], 3))
    table_all = side_by_side(chars_all[:, :, width + triple :], 3)
    table_full = whole(table_all[:, :, : pl.cdiv(letters_count, LANES) * LANES])
    gains_all = table_all[:, 0, letters_count : letters_count + 6 * r]
    gains_all = gains_all.reshape(devices, 6, r).transpose(1, 0, 2).reshape(6, width)
    gains_all = gains_all.astype(jnp.float32)

    def second(start, rows):
        return second_all[:, start : start + rows]

    up_start = down_rows + taps * tap_rows
    upper_full = whole(side_by_side(second(up_start, ff_blocks * r), ff_blocks))
    branch_full = whole(second(up_start + ff_blocks * r, r))

    def rows_spec(start, rows):
        if rows % 16 == 0 and start % rows == 0:
            place = start // rows
            return second_all, pl.BlockSpec(
                (devices, rows, width), lambda b: (0, place, 0), pipeline_mode=pl.Buffered(1)
            )
        part = second(start, rows).reshape(ff_blocks, -1, width)
        return part, pl.BlockSpec(part.shape, lambda b: (0, 0, 0), pipeline_mode=pl.Buffered(1))

    valid = lax.broadcasted_iota(jnp.int32, (length, 1), 0) < lengths
    embeds, chars_rep, char_states, coefs = chars_forward(
        codes, table_full, inlet_full, recur_full
    )
    first_pre = states.astype(jnp.float32) + product(context_low, output_full)
    first = norm_parts(first_pre)[0] * gains_all[0] + gains_all[1]
    joined = jnp.where(
        valid, jnp.concatenate([first.astype(low), chars_rep], axis=-1), jnp.zeros((), low)
    )
    merging_parts = [rows_spec(down_rows + i * tap_rows, tap_rows) for i in range(taps)]
    (
        token_stream,
        char_stream,
        summed_low,
        merged_low,
        hidden_low,
        feed_grad,
        hidden_grad,
        branch_grad,
        merging_grad,
        summed_grad,
        char_pre_grad,
        gain_sums,
    ) = feed(
        joined,
        first,
        chars_rep,
        token_cotangent[0],
        char_cotangent[0],
        gains_all,
        upper_full,
        branch_full,
        merging_parts,
        rows_spec(0, down_rows),
    )
    feed_gain_grad, feed_shift_grad, char_gain_grad, char_shift_grad = jnp.sum(gain_sums, axis=1)
    early = early_parts(hidden_low, joined, feed_grad, merging_grad, devices)
    early, merging_grad, summed_low = after(early, merging_grad, summed_low)
    early = lax.psum_scatter(early, AXES, scatter_dimension=0, tiled=True)[0]
    up_parts = shares(outer_sum(summed_low, hidden_grad), devices)
    up_parts, merging_grad = after(up_parts, merging_grad)
    up_terms = core_terms(grid, up_parts)
    first_pre_grad, attended_grad, context_grad, rep_grad, attend_sums = merging_back(
        lengths,
        merging_grad,
        summed_grad,
        char_pre_grad,
        first_pre,
        gains_all,
        output_full,
        merging_parts,
    )
    up_terms, rep_grad, merged_low, attended_grad = after(
        up_terms, rep_grad, merged_low, attended_grad
    )
    attend_gain_grad, attend_shift_grad = jnp.sum(attend_sums, axis=1)
    branch_weight_grad = outer_sum(merged_low, branch_grad)
    output_weight_grad = outer_sum(context_low, attended_grad)
    up_layer, rep_grad = after(added_low(up_terms), rep_grad)
    up_terms = plane_terms(grid, up_layer)
    char_grads = chars_back(
        codes, inlet_full, recur_full, embeds, char_states, coefs, rep_grad, table_full.shape[1]
    )
    up_terms, char_grads, context_grad = after(up_terms, char_grads, context_grad)
    table_grad, inlet_grad, recur_weight_grad = char_grads
    up_column = added_low(up_terms)
    gain_grads = jnp.stack(
        [
            attend_gain_grad,
            attend_shift_grad,
            feed_gain_grad,
            feed_shift_grad,
            char_gain_grad,
            char_shift_grad,
        ]
    )
    gain_shares = gain_grads.reshape(6, devices, r).transpose(1, 0, 2).reshape(devices, 1, 6 * r)
    table_shares = shares(table_grad, devices)[:, :, :letters_count]
    gain_shares = jnp.pad(
        gain_shares.astype(low), ((0, 0), (0, table_shares.shape[1] - 1), (0, 0))
    )
    table_shares = jnp.concatenate([table_shares, gain_shares], axis=2)
    table_shares = jnp.pad(
        table_shares, ((0, 0), (0, 0), (0, triple - table_shares.shape[2]))
    )
    late = jnp.concatenate(
        [
            jnp.concatenate(
                [
                    side_by_side(shares(inlet_grad, devices), 3),
                    side_by_side(shares(recur_weight_grad, devices), 3),
                    one_below_other(table_shares, 3),
                ],
                axis=2,
            ),
            side_by_side(shares(output_weight_grad, devices), 3),
            side_by_side(shares(branch_weight_grad, devices), 3),
        ],
        axis=1,
    )
    def back(start, pairs, context_grad, earlier):
        return attend_back(
            mixed, context_grad, context_low, log_totals, lengths, width, start, pairs, earlier
        )

    every = width // LANES
    cut = every // 6
    up_column, late, context_grad = after(up_column, late, context_grad)
    up_terms = column_terms(grid, up_column)
    late_terms = core_terms(grid, late)
    grads = back(0, cut, context_grad, ())
    late_terms, grads, context_grad = after(late_terms, grads, context_grad)
    late_layer, context_grad = after(added_low(late_terms), context_grad)
    late_terms = plane_terms(grid, late_layer)
    grads = back(cut, every - cut, context_grad, grads)
    late_terms, up_terms, grads = after(late_terms, up_terms, grads)
    late_column, grads = after(added_low(late_terms), grads)
    late_terms = column_terms(grid, late_column)
    mixed_grad = jnp.concatenate(grads, axis=-1)
    project_parts = shares(outer_sum(states, mixed_grad), devices)
    project_layer = added_low(core_terms(grid, project_parts))
    project_terms = plane_terms(grid, project_layer)
    project_terms, late_terms, early = after(project_terms, late_terms, early)
    up_own, late = added(up_terms), added(late_terms)
    own_project = added(column_terms(grid, added_low(project_terms)))
    input_gradient = (first_pre_grad + back_product(mixed_grad, project_full)).astype(low)
    early = early.astype(jnp.float32)
    own_chars = late[:r]
    own_table_rows = side_by_side(own_chars[:, width + triple :], 3)
    own_gains = own_table_rows[0, letters_count : letters_count + 6 * r].reshape(6, r)
    return (
        token_stream[None],
        char_stream[None],
        input_gradient[None],
        own_table_rows[:, :letters_count].T,
        one_below_other(own_chars[:, :width], 3).T,
        one_below_other(own_chars[:, width : width + triple], 3).T,
        own_project,
        one_below_other(late[r : r + r // 3], 3),
        early[down_rows:].reshape(merging_weight.shape),
        up_own,
        early[:down_rows],
        one_below_other(late[r + r // 3 :], 3),
        own_gains[0],
        own_gains[1],
        own_gains[2],
        own_gains[3],
        own_gains[4],
        own_gains[5],
    )

def solution(mesh):
    placed = (
        P(AXES, None, None),
        P(AXES, None, None),
        P(AXES),
        P(AXES, None, None),
        P(AXES, None, None),
        P(None, AXES),
        P(None, AXES),
        P(None, AXES),
        P(AXES, None),
        P(AXES, None),
        P(None, AXES, None),
        P(AXES, None),
        P(AXES, None),
        P(AXES, None),
        P(AXES),
        P(AXES),
        P(AXES),
        P(AXES),
        P(AXES),
        P(AXES),
    )
    sizes = (mesh.shape["dp"], mesh.shape["fsdp"])
    return jax.shard_map(
        functools.partial(on_device, sizes),
        mesh=mesh,
        in_specs=placed,
        out_specs=(
            P(AXES, None, None),
            P(AXES, None, None),
            P(AXES, None, None),
            P(None, AXES),
            P(None, AXES),
            P(None, AXES),
            P(AXES, None),
            P(AXES, None),
            P(None, AXES, None),
            P(AXES, None),
            P(AXES, None),
            P(AXES, None),
            P(AXES),
            P(AXES),
            P(AXES),
            P(AXES),
            P(AXES),
            P(AXES),
        ),
        check_vma=False,
    )
```

```python
import functools
import itertools
import math

import jax
import jax.numpy as jnp
from jax import lax
from jax.experimental import pallas as pl
from jax.experimental.pallas import tpu as pltpu
from jax.sharding import PartitionSpec as P

HEAD_DIM = 64
CHARS = 4
LANES = 128
EPS = 1e-05
MASKED = -1e30
SCALE = 1.0 / math.sqrt(HEAD_DIM)
SCALE2 = math.log2(math.e) / math.sqrt(HEAD_DIM)
AXES = ("dp", "fsdp")
VMEM_LIMIT = 56 * 1024 * 1024
BRIEF = pl.CostEstimate(flops=200 * 10**9, bytes_accessed=10**6, transcendentals=0)

def product(left, right):
    return jnp.dot(left, right, preferred_element_type=jnp.float32)


def outer_sum(left, right):
    return jnp.einsum("li,lo->io", left, right, preferred_element_type=jnp.float32)


def back_product(grad_rows, weight):
    return jnp.einsum("lo,io->li", grad_rows, weight, preferred_element_type=jnp.float32)


def dotf(a,b,ca=1,cb=0):
    return lax.dot_general(a,b,(((ca,),(cb,)),((),())),preferred_element_type=jnp.float32)

def lane_half(shape):
    return lax.broadcasted_iota(jnp.int32, shape, 1) < HEAD_DIM

def attend_kernel(rows, length_ref, q_ref, k_ref, v_ref, ctx_ref, lse_ref, kx_ref, vx_ref):
    length = k_ref.shape[0]
    lane = lax.broadcasted_iota(jnp.int32, (length, LANES), 1)
    place = lax.broadcasted_iota(jnp.int32, (length, LANES), 0)
    kx_ref[:, :LANES] = k_ref[...]
    kx_ref[:, LANES:] = jnp.where((lane == 0) & (place >= length_ref[0]), MASKED, 0.0).astype(jnp.bfloat16)
    vx_ref[:, :LANES] = v_ref[...]
    vx_ref[:, LANES:] = jnp.ones((length, LANES), jnp.bfloat16)
    low = lane_half((rows, LANES))
    one = jnp.where(lax.broadcasted_iota(jnp.int32, (rows, LANES), 1) == 0, 1.0, 0.0).astype(jnp.bfloat16)
    def step(c, _):
        at = pl.ds(pl.multiple_of(c * rows, rows), rows)
        q = q_ref[at, :].astype(jnp.float32)
        outs = []
        for h in range(2):
            mine = low if h == 0 else jnp.logical_not(low)
            qx = jnp.concatenate([jnp.where(mine, q, 0.0).astype(jnp.bfloat16), one], axis=1)
            s = dotf(qx, kx_ref[...], 1, 1)
            peak = jnp.max(s, axis=1, keepdims=True) * SCALE2
            p = jnp.exp2(s * SCALE2 - peak).astype(jnp.bfloat16)
            o = dotf(p, vx_ref[...])
            total = o[:, LANES:]
            outs.append((o[:, :LANES] / total, peak + jnp.log2(total)))
        ctx_ref[at, :] = jnp.where(low, outs[0][0], outs[1][0]).astype(jnp.bfloat16)
        lse_ref[at, :] = jnp.where(low, outs[0][1], outs[1][1])
        return 0
    lax.fori_loop(0, length // rows, step, 0, unroll=True)

def attend(mixed, lengths, width, rows=256):
    length = mixed.shape[0]
    pairs = width // LANES
    spec = lambda o: pl.BlockSpec((length, LANES), lambda p, o=o: (0, p+o))
    return pl.pallas_call(
        functools.partial(attend_kernel, rows),
        grid=(pairs,),
        in_specs=[pl.BlockSpec(memory_space=pltpu.SMEM), spec(0), spec(pairs), spec(2 * pairs)],
        out_specs=[spec(0), spec(0)],
        out_shape=[jax.ShapeDtypeStruct((length, width), jnp.bfloat16), jax.ShapeDtypeStruct((length, width), jnp.float32)],
        scratch_shapes=[pltpu.VMEM((length, 2*LANES), jnp.bfloat16), pltpu.VMEM((length, 2*LANES), jnp.bfloat16)],
        compiler_params=pltpu.CompilerParams(vmem_limit_bytes=VMEM_LIMIT),
        cost_estimate=BRIEF,
    )(lengths, mixed, mixed, mixed)

def back_kernel(rows, length_ref, q_ref, k_ref, v_ref, do_ref, o_ref, lse_ref, *rest):
    dq_ref, dk_out, dv_out, kx_ref, qt_ref, dot_ref, dk_ref, dv_ref = rest[-8:]
    length = k_ref.shape[0]
    lane = lax.broadcasted_iota(jnp.int32, (length, LANES), 1)
    place = lax.broadcasted_iota(jnp.int32, (length, LANES), 0)
    kx_ref[:, :LANES] = k_ref[...]
    kx_ref[:, LANES:] = jnp.where((lane == 0) & (place >= length_ref[0]), MASKED, 0.0).astype(jnp.bfloat16)
    qt_ref[...] = q_ref[...].T
    dot_ref[...] = do_ref[...].T
    dk_ref[...] = jnp.zeros_like(dk_ref)
    dv_ref[...] = jnp.zeros_like(dv_ref)
    low = lane_half((rows, LANES))
    one = jnp.where(lax.broadcasted_iota(jnp.int32, (rows, LANES), 1) == 0, 1.0, 0.0).astype(jnp.bfloat16)
    def step(c, _):
        at = pl.ds(pl.multiple_of(c * rows, rows), rows)
        q = q_ref[at, :].astype(jnp.float32)
        do = do_ref[at, :].astype(jnp.float32)
        doo = do * o_ref[at, :].astype(jnp.float32)
        lse = lse_ref[at, :]
        dqs = []
        for h in range(2):
            mine = low if h == 0 else jnp.logical_not(low)
            qx = jnp.concatenate([jnp.where(mine, q, 0.0).astype(jnp.bfloat16), one], axis=1)
            s = dotf(qx, kx_ref[...], 1, 1)
            p = jnp.exp2(s * SCALE2 - lse[:, h*HEAD_DIM:h*HEAD_DIM+1])
            dp = dotf(jnp.where(mine, do, 0.0).astype(jnp.bfloat16), v_ref[...], 1, 1)
            delta = jnp.sum(jnp.where(mine, doo, 0.0), axis=1, keepdims=True)
            ds = (p * (dp - delta)).astype(jnp.bfloat16)
            pb = p.astype(jnp.bfloat16)
            hs = slice(h*HEAD_DIM, (h+1)*HEAD_DIM)
            dqs.append(dotf(ds, k_ref[...]))
            dk_ref[hs, :] += dotf(qt_ref[hs, at], ds)
            dv_ref[hs, :] += dotf(dot_ref[hs, at], pb)
        dq_ref[at, :] = (jnp.where(low, dqs[0], dqs[1]) * SCALE).astype(jnp.bfloat16)
        return 0
    lax.fori_loop(0, length // rows, step, 0, unroll=True)
    dk_out[...] = (dk_ref[...] * SCALE).T.astype(jnp.bfloat16)
    dv_out[...] = dv_ref[...].T.astype(jnp.bfloat16)

def attend_back(
    mixed, context_grad, context, log_totals, lengths, width, start, pairs, earlier, rows=256
):
    length = mixed.shape[0]
    every = width // LANES
    spec = lambda o: pl.BlockSpec((length, LANES), lambda p, o=o: (0, p + o + start))
    scratch = lambda a, b, t: pltpu.VMEM((a, b), t)
    return pl.pallas_call(
        functools.partial(back_kernel, rows),
        grid=(pairs,),
        in_specs=[pl.BlockSpec(memory_space=pltpu.SMEM), spec(0), spec(every), spec(2 * every)]
        + [spec(0)] * 3
        + [pl.BlockSpec(memory_space=pl.ANY)] * len(earlier),
        out_specs=[spec(0)] * 3,
        out_shape=[jax.ShapeDtypeStruct((length, width), jnp.bfloat16)] * 3,
        input_output_aliases={7 + i: i for i in range(len(earlier))},
        scratch_shapes=[
            scratch(length, 2 * LANES, jnp.bfloat16),
            scratch(LANES, length, jnp.bfloat16),
            scratch(LANES, length, jnp.bfloat16),
            scratch(LANES, length, jnp.float32),
            scratch(LANES, length, jnp.float32),
        ],
        compiler_params=pltpu.CompilerParams(vmem_limit_bytes=VMEM_LIMIT),
        cost_estimate=BRIEF,
    )(lengths, mixed, mixed, mixed, context_grad, context, log_totals, *earlier)


ROOT_HALF = math.sqrt(0.5)
DENSITY = 1.0 / math.sqrt(2.0 * math.pi)

def gelu_both(values):
    below = 0.5 + 0.5 * lax.erf(values * ROOT_HALF)
    return values * below, below + values * (DENSITY * jnp.exp(-0.5 * values * values))

def norm_parts(values):
    average = jnp.mean(values, axis=-1, keepdims=True)
    centred = values - average
    spread = lax.rsqrt(jnp.mean(centred * centred, axis=-1, keepdims=True) + EPS)
    return centred * spread, spread

def norm_back(normed, spread, scaled):
    return spread * (scaled - jnp.mean(scaled, axis=-1, keepdims=True)
                     - normed * jnp.mean(scaled * normed, axis=-1, keepdims=True))

def column_sums(values):
    rows, width = values.shape
    return jnp.sum(values.reshape(rows // 8, 8, width), axis=0)

def chars_kernel(half, codes_ref, table_ref, inlet_ref, recur_ref, embed_ref, rep_ref, states_ref, coef_ref):
    rows = codes_ref.shape[0]
    triple = 3 * half
    width = embed_ref.shape[1] // CHARS
    letters = lax.broadcasted_iota(jnp.int32, (rows, table_ref.shape[1]), 1)
    embeds = []
    for slot in range(CHARS):
        picked = jnp.where(codes_ref[:, slot : slot + 1] == letters, 1.0, 0.0).astype(jnp.bfloat16)
        embed = dotf(picked, table_ref[...], 1, 1).astype(jnp.bfloat16)
        embed_ref[:, slot * width : (slot + 1) * width] = embed
        embeds.append(embed)
    low = jnp.bfloat16
    states = [None, None]
    for step, side in itertools.product(range(CHARS), range(2)):
        slot = step if side == 0 else CHARS - 1 - step
        base = side * triple
        state = states[side]
        gates = dotf(embeds[slot], inlet_ref[base : base + triple, :], 1, 1)
        if state is None:
            update = jax.nn.sigmoid(gates[:, half : 2 * half])
            fresh = jnp.tanh(gates[:, 2 * half :])
            new = (1.0 - update) * fresh
            coef_ref[side, 0] = ((1.0 - update) * (1.0 - fresh * fresh)).astype(low)
            coef_ref[side, 1] = (-fresh * update * (1.0 - update)).astype(low)
        else:
            recur = dotf(state, recur_ref[base : base + triple, :], 1, 1)
            reset = jax.nn.sigmoid(gates[:, :half] + recur[:, :half])
            update = jax.nn.sigmoid(gates[:, half : 2 * half] + recur[:, half : 2 * half])
            recur_new = recur[:, 2 * half :]
            fresh = jnp.tanh(gates[:, 2 * half :] + reset * recur_new)
            before = state.astype(jnp.float32)
            new = (1.0 - update) * fresh + update * before
            at = 2 + 5 * (step - 1)
            coef_ref[side, at] = ((1.0 - update) * (1.0 - fresh * fresh)).astype(low)
            coef_ref[side, at + 1] = ((before - fresh) * update * (1.0 - update)).astype(low)
            coef_ref[side, at + 2] = (recur_new * reset * (1.0 - reset)).astype(low)
            coef_ref[side, at + 3] = reset.astype(low)
            coef_ref[side, at + 4] = update.astype(low)
        states[side] = new.astype(low)
        if step < CHARS - 1:
            states_ref[side, step] = states[side]
    for side in range(2):
        rep_ref[:, side * half : (side + 1) * half] = states[side]


COEFS = 2 + 5 * (CHARS - 1)

def chars_forward(codes, table, inlet, recur, rows=256):
    length = codes.shape[0]
    embed, half = inlet.shape[1], recur.shape[1]
    low = jnp.bfloat16
    full = lambda a: pl.BlockSpec(a.shape, lambda b: (0, 0))
    return pl.pallas_call(
        functools.partial(chars_kernel, half),
        grid=(length // rows,),
        in_specs=[pl.BlockSpec((rows, CHARS), lambda b: (b, 0)), full(table), full(inlet), full(recur)],
        out_specs=[
            pl.BlockSpec((rows, CHARS * embed), lambda b: (b, 0)),
            pl.BlockSpec((rows, 2 * half), lambda b: (b, 0)),
            pl.BlockSpec((2, CHARS - 1, rows, half), lambda b: (0, 0, b, 0)),
            pl.BlockSpec((2, COEFS, rows, half), lambda b: (0, 0, b, 0)),
        ],
        out_shape=[
            jax.ShapeDtypeStruct((length, CHARS * embed), low),
            jax.ShapeDtypeStruct((length, 2 * half), low),
            jax.ShapeDtypeStruct((2, CHARS - 1, length, half), low),
            jax.ShapeDtypeStruct((2, COEFS, length, half), low),
        ],
        compiler_params=pltpu.CompilerParams(vmem_limit_bytes=VMEM_LIMIT),
        cost_estimate=BRIEF,
    )(codes, table, inlet, recur)

def chars_back_kernel(half, codes_ref, inlet_ref, recur_ref, embed_ref, states_ref, coef_ref, grad_ref,
                      table_out, inlet_out, recur_out, gates_ref, lets_ref, steps_ref, table_acc, inlet_acc, recur_acc):
    rows = codes_ref.shape[0]
    triple = 3 * half
    width = embed_ref.shape[1] // CHARS
    low = jnp.bfloat16
    first, last = pl.program_id(0) == 0, pl.program_id(0) == pl.num_programs(0) - 1

    @pl.when(first)
    def _():
        table_acc[...] = jnp.zeros_like(table_acc)
        inlet_acc[...] = jnp.zeros_like(inlet_acc)
        recur_acc[...] = jnp.zeros_like(recur_acc)

    grads = [grad_ref[:, side * half : (side + 1) * half] for side in range(2)]
    for step, side in itertools.product(range(CHARS - 1, -1, -1), range(2)):
        slot = step if side == 0 else CHARS - 1 - step
        base = side * triple
        grad = grads[side]
        at = 2 + 5 * (step - 1) if step else 0
        load = lambda k: coef_ref[side, at + k].astype(jnp.float32)
        fresh_pre = grad * load(0)
        update_pre = (grad * load(1)).astype(low)
        spot = slice(slot * rows, (slot + 1) * rows)
        gates_ref[spot, base + half : base + 2 * half] = update_pre
        gates_ref[spot, base + 2 * half : base + triple] = fresh_pre.astype(low)
        if step == 0:
            gates_ref[spot, base : base + half] = jnp.zeros((rows, half), low)
            continue
        reset_pre = (fresh_pre * load(2)).astype(low)
        gates_ref[spot, base : base + half] = reset_pre
        recur_grad = jnp.concatenate(
            [reset_pre, update_pre, (fresh_pre * load(3)).astype(low)], axis=1)
        steps_ref[side, (step - 1) * rows : step * rows] = recur_grad
        grads[side] = grad * load(4) + dotf(recur_grad, recur_ref[base : base + triple, :])
    for side in range(2):
        base = side * triple
        states = states_ref[side].reshape(-1, half)
        recur_acc[:, base : base + triple] += dotf(states, steps_ref[side], 0, 0)
    embed_all = jnp.concatenate([embed_ref[:, j * width : (j + 1) * width] for j in range(CHARS)], axis=0)
    inlet_acc[...] += dotf(embed_all, gates_ref[...], 0, 0)
    embed_grad = dotf(gates_ref[...], inlet_ref[...]).astype(low)
    letters = lax.broadcasted_iota(jnp.int32, (rows, table_acc.shape[1]), 1)
    for slot in range(CHARS):
        lets_ref[slot * rows : (slot + 1) * rows, :] = jnp.where(
            codes_ref[:, slot : slot + 1] == letters, 1.0, 0.0).astype(low)
    table_acc[...] += dotf(embed_grad, lets_ref[...], 0, 0)

    @pl.when(last)
    def _():
        table_out[...] = table_acc[...].astype(low)
        for start in range(0, 2 * triple, half):
            cols = slice(start, start + half)
            inlet_out[cols, :] = inlet_acc[:, cols].T.astype(low)
            recur_out[cols, :] = recur_acc[:, cols].T.astype(low)


def chars_back(codes, inlet, recur, embeds, states, coefs, grad, letters, rows=256):
    length = codes.shape[0]
    embed, half = inlet.shape[1], recur.shape[1]
    low = jnp.bfloat16
    full = lambda a: pl.BlockSpec(a.shape, lambda b: (0, 0))
    outs = [(embed, letters), inlet.shape, recur.shape]
    return pl.pallas_call(
        functools.partial(chars_back_kernel, half),
        grid=(length // rows,),
        in_specs=[
            pl.BlockSpec((rows, CHARS), lambda b: (b, 0)), full(inlet), full(recur),
            pl.BlockSpec((rows, CHARS * embed), lambda b: (b, 0)),
            pl.BlockSpec((2, CHARS - 1, rows, half), lambda b: (0, 0, b, 0)),
            pl.BlockSpec((2, COEFS, rows, half), lambda b: (0, 0, b, 0)),
            pl.BlockSpec((rows, 2 * half), lambda b: (b, 0)),
        ],
        out_specs=[pl.BlockSpec(s, lambda b: (0, 0)) for s in outs],
        out_shape=[jax.ShapeDtypeStruct(s, low) for s in outs],
        scratch_shapes=[
            pltpu.VMEM((CHARS * rows, 6 * half), low),
            pltpu.VMEM((CHARS * rows, letters), low),
            pltpu.VMEM((2, (CHARS - 1) * rows, 3 * half), low),
            pltpu.VMEM((embed, letters), jnp.float32),
            pltpu.VMEM(inlet.shape[::-1], jnp.float32),
            pltpu.VMEM(recur.shape[::-1], jnp.float32),
        ],
        compiler_params=pltpu.CompilerParams(vmem_limit_bytes=VMEM_LIMIT),
        cost_estimate=BRIEF,
    )(codes, inlet, recur, embeds, states, coefs, grad)

def flat(ref, part=0, parts=1):
    count = ref.shape[0] // parts
    block = ref[part * count : (part + 1) * count]
    return block.reshape(-1, block.shape[-1])


PAD = 8


def spread_rows(rows_ref, wide_ref):
    length, width = rows_ref.shape
    blank = jnp.zeros((PAD, width), jnp.float32)
    wide_ref[:PAD] = blank
    wide_ref[PAD + length :] = blank
    for start in range(0, length, 256):
        block = rows_ref[start : start + 256]
        wide_ref[PAD + start : PAD + start + block.shape[0]] = block.astype(jnp.float32)


def neighbours(wide_ref, rows):
    base = pl.multiple_of(pl.program_id(0) * rows, rows)
    window = wide_ref[pl.ds(base, rows + 2 * PAD)]
    return [window[PAD + i : PAD + i + rows].astype(jnp.bfloat16) for i in (-1, 0, 1)]


def feed_kernel(blocks, joined_ref, first_ref, rep_ref, token_cot_ref, char_cot_ref, gains_ref,
                up_ref, branch_ref, tap0_ref, tap1_ref, tap2_ref, down_ref,
                token_ref, char_ref, summed_ref, merged_ref, hidden_ref, feed_grad_ref, hidden_grad_ref,
                branch_grad_ref, merging_grad_ref, summed_grad_ref, char_grad_ref, sums_ref, slope_ref, wide_ref):
    low = jnp.bfloat16
    width = first_ref.shape[1]
    step = up_ref.shape[1] // blocks
    merging_refs = (tap0_ref, tap1_ref, tap2_ref)

    @pl.when(pl.program_id(0) == 0)
    def _():
        sums_ref[...] = jnp.zeros_like(sums_ref)
        spread_rows(joined_ref, wide_ref)

    merging_pre = 0.0
    for moved, ref in zip(neighbours(wide_ref, first_ref.shape[0]), merging_refs):
        merging_pre = merging_pre + dotf(moved, flat(ref))
    merged, merging_slope = gelu_both(merging_pre)
    merged_low = merged.astype(low)
    merged_ref[...] = merged_low
    summed = first_ref[...] + merged
    summed_low = summed.astype(low)
    summed_ref[...] = summed_low
    total = summed
    for c in range(blocks):
        cols = slice(c * step, (c + 1) * step)
        hidden, slope = gelu_both(dotf(summed_low, up_ref[:, cols]))
        slope_ref[:, cols] = slope
        hidden_low = hidden.astype(low)
        hidden_ref[:, cols] = hidden_low
        total = total + dotf(hidden_low, flat(down_ref, c, blocks))
    normed, spread = norm_parts(total)
    gain, shift = gains_ref[2:3, :], gains_ref[3:4, :]
    token_ref[...] = (normed * gain + shift).astype(low)
    cot = token_cot_ref[...].astype(jnp.float32)
    sums_ref[0] += column_sums(cot * normed)
    sums_ref[1] += column_sums(cot)
    token_grad = norm_back(normed, spread, cot * gain)
    feed_grad = token_grad.astype(low)
    feed_grad_ref[...] = feed_grad
    total = token_grad
    for c in range(blocks):
        cols = slice(c * step, (c + 1) * step)
        hidden_grad = (slope_ref[:, cols] * dotf(feed_grad, flat(down_ref, c, blocks), 1, 1)).astype(low)
        hidden_grad_ref[:, cols] = hidden_grad
        total = total + dotf(hidden_grad, up_ref[:, cols], 1, 1)
    summed_grad_ref[...] = total
    normed, spread = norm_parts(rep_ref[...].astype(jnp.float32) + dotf(merged_low, branch_ref[...]))
    gain, shift = gains_ref[4:5, :], gains_ref[5:6, :]
    char_ref[...] = (normed * gain + shift).astype(low)
    cot = char_cot_ref[...].astype(jnp.float32)
    sums_ref[2] += column_sums(cot * normed)
    sums_ref[3] += column_sums(cot)
    char_grad = norm_back(normed, spread, cot * gain)
    char_grad_ref[...] = char_grad
    branch_grad = char_grad.astype(low)
    branch_grad_ref[...] = branch_grad
    merging_grad_ref[...] = (merging_slope * (total + dotf(branch_grad, branch_ref[...], 1, 1))).astype(low)

def feed(joined, first, rep, token_cot, char_cot, gains, up, branch, merging, down, rows=256, blocks=2):
    length, width = first.shape
    ff = up.shape[1]
    low, wide = jnp.bfloat16, jnp.float32
    row = lambda w: pl.BlockSpec((rows, w), lambda b: (b, 0))
    full = lambda a: pl.BlockSpec(a.shape, lambda b: (0,) * a.ndim, pipeline_mode=pl.Buffered(1))
    outs = [(width, low), (width, low), (width, low), (width, low), (ff, low), (width, low), (ff, low),
            (width, low), (width, low), (width, wide), (width, wide)]
    return pl.pallas_call(
        functools.partial(feed_kernel, blocks),
        grid=(length // rows,),
        in_specs=[full(joined), row(width), row(width), row(width), row(width), full(gains),
                  full(up), full(branch)] + [spec for _, spec in merging + [down]],
        out_specs=[row(w) for w, _ in outs] + [pl.BlockSpec((4, 8, width), lambda b: (0, 0, 0))],
        out_shape=[jax.ShapeDtypeStruct((length, w), t) for w, t in outs] + [jax.ShapeDtypeStruct((4, 8, width), wide)],
        scratch_shapes=[pltpu.VMEM((rows, ff), wide), pltpu.VMEM((length + 2 * PAD, joined.shape[1]), wide)],
        compiler_params=pltpu.CompilerParams(vmem_limit_bytes=VMEM_LIMIT),
        cost_estimate=BRIEF,
    )(joined, first, rep, token_cot, char_cot, gains, up, branch, *[part for part, _ in merging + [down]])


def early_kernel(hidden_ref, joined_ref, feed_grad_ref, merging_grad_ref, out_ref, wide_ref, moved_ref):
    low = jnp.bfloat16
    count, _, width = out_ref.shape
    length = feed_grad_ref.shape[0]

    @pl.when(pl.program_id(0) == 0)
    def _():
        spread_rows(merging_grad_ref, wide_ref)
        for start in range(0, length, 256):
            window = wide_ref[start : start + 256 + 2 * PAD]
            for i, shift in enumerate((1, 0, -1)):
                moved_ref[i, start : start + 256] = window[PAD + shift : PAD + shift + 256].astype(low)

    def put(start, terms):
        terms = terms.astype(low).reshape(count, -1, width)
        out_ref[:, start : start + terms.shape[1]] = terms

    down = hidden_ref.shape[1] // count
    rows = joined_ref.shape[1] // count
    put(0, dotf(hidden_ref[...], feed_grad_ref[...], 0, 0))
    for i in range(moved_ref.shape[0]):
        put(down + i * rows, dotf(joined_ref[...], moved_ref[i], 0, 0))


def early_parts(hidden, joined, feed_grad, merging_grad, devices, taps=3, groups=4):
    length, width = feed_grad.shape
    low = jnp.bfloat16
    down, rows = hidden.shape[1] // devices, joined.shape[1] // devices
    if down % 16 or rows % 16:
        pairs = [(hidden, feed_grad)]
        pairs += [(joined[:-1], merging_grad[1:]), (joined, merging_grad), (joined[1:], merging_grad[:-1])]
        return jnp.concatenate([shares(outer_sum(*pair), devices) for pair in pairs], axis=1)
    columns = lambda a: pl.BlockSpec((length, a.shape[1] // groups), lambda g: (0, g))
    full = pl.BlockSpec((length, width), lambda g: (0, 0))
    shape = (devices, down + taps * rows, width)
    return pl.pallas_call(
        early_kernel,
        grid=(groups,),
        in_specs=[columns(hidden), columns(joined), full, full],
        out_specs=pl.BlockSpec((devices // groups,) + shape[1:], lambda g: (g, 0, 0)),
        out_shape=jax.ShapeDtypeStruct(shape, low),
        scratch_shapes=[
            pltpu.VMEM((length + 2 * PAD, width), jnp.float32),
            pltpu.VMEM((taps, length, width), low),
        ],
        compiler_params=pltpu.CompilerParams(vmem_limit_bytes=VMEM_LIMIT),
        cost_estimate=BRIEF,
    )(hidden, joined, feed_grad, merging_grad)


def merging_back_kernel(length_ref, grad_ref, summed_ref, char_ref, pre_ref, gains_ref, output_ref,
                        tap0_ref, tap1_ref, tap2_ref,
                        pre_grad_ref, attended_ref, context_ref, rep_ref, sums_ref, wide_ref):
    rows, width = pre_ref.shape
    low = jnp.bfloat16

    @pl.when(pl.program_id(0) == 0)
    def _():
        sums_ref[...] = jnp.zeros_like(sums_ref)
        spread_rows(grad_ref, wide_ref)

    joined = 0.0
    for moved, ref in zip(neighbours(wide_ref, rows), (tap2_ref, tap1_ref, tap0_ref)):
        joined = joined + dotf(moved, flat(ref), 1, 1)
    place = pl.program_id(0) * rows + lax.broadcasted_iota(jnp.int32, (rows, 1), 0)
    joined = jnp.where(place < length_ref[0], joined, 0.0)
    rep_ref[...] = char_ref[...] + joined[:, width:]
    first_grad = summed_ref[...] + joined[:, :width]
    normed, spread = norm_parts(pre_ref[...])
    sums_ref[0] += column_sums(first_grad * normed)
    sums_ref[1] += column_sums(first_grad)
    pre_grad = norm_back(normed, spread, first_grad * gains_ref[0:1, :])
    pre_grad_ref[...] = pre_grad
    attended = pre_grad.astype(low)
    attended_ref[...] = attended
    context_ref[...] = dotf(attended, output_ref[...], 1, 1).astype(low)


def merging_back(lengths, grad, summed_grad, char_grad, pre, gains, output, merging, rows=256):
    length, width = pre.shape
    low, wide = jnp.bfloat16, jnp.float32
    row = pl.BlockSpec((rows, width), lambda b: (b, 0))
    full = lambda a: pl.BlockSpec(a.shape, lambda b: (0, 0), pipeline_mode=pl.Buffered(1))
    kinds = (wide, low, low, wide)
    return pl.pallas_call(
        merging_back_kernel,
        grid=(length // rows,),
        in_specs=[pl.BlockSpec(memory_space=pltpu.SMEM), full(grad), row, row, row, full(gains), full(output)]
        + [spec for _, spec in merging],
        out_specs=[row] * 4 + [pl.BlockSpec((2, 8, width), lambda b: (0, 0, 0))],
        out_shape=[jax.ShapeDtypeStruct((length, width), t) for t in kinds]
        + [jax.ShapeDtypeStruct((2, 8, width), wide)],
        scratch_shapes=[pltpu.VMEM((length + 2 * PAD, width), wide)],
        compiler_params=pltpu.CompilerParams(vmem_limit_bytes=VMEM_LIMIT),
        cost_estimate=BRIEF,
    )(lengths, grad, summed_grad, char_grad, pre, gains, output, *[part for part, _ in merging])


def side_by_side(rows, groups):
    r = rows.shape[-2] // groups
    return jnp.concatenate(
        [rows[..., i * r : (i + 1) * r, :] for i in range(groups)], axis=-1
    )


def one_below_other(rows, groups):
    w = rows.shape[-1] // groups
    return jnp.concatenate(
        [rows[..., i * w : (i + 1) * w] for i in range(groups)], axis=-2
    )


def whole(part):
    return part.reshape(-1, part.shape[-1])


def shares(full, devices):
    return full.reshape(devices, -1, full.shape[-1]).astype(jnp.bfloat16)


class Grid:
    def __init__(self, sizes):
        dp, fsdp = sizes
        z = 4 if dp % 4 == 0 else 1
        core = 2 if fsdp % 2 == 0 else 1
        self.fsdp = fsdp
        self.shape = (z, dp // z, fsdp // core, core)
        self.devices = dp * fsdp

    def own(self):
        z, x, y, core = self.shape
        dp, fsdp = lax.axis_index("dp"), lax.axis_index("fsdp")
        return dp // x, dp % x, fsdp // core, fsdp % core

    def send(self, values, shift):
        pairs = []
        for source, place in enumerate(itertools.product(*map(range, self.shape))):
            target = 0
            for at, by, size in zip(place, shift, self.shape):
                target = target * size + (at + by) % size
            pairs.append((source, target))
        return lax.ppermute(values, AXES, pairs)

    def plane(self):
        z, x, y, core = self.shape
        return [(i, j) for i in range(x) for j in range(y) if i or j]


def column_sends(grid, part):
    return [grid.send(part, (s, 0, 0, 0)) for s in range(1, grid.shape[0])]


def column_of(grid, part, came):
    nz = grid.shape[0]
    z = grid.own()[0]
    column = jnp.zeros((nz,) + part.shape, part.dtype)
    for s, piece in enumerate([part] + came):
        column = lax.dynamic_update_slice(column, piece[None], ((z - s) % nz, 0, 0))
    return column


def plane_sends(grid, column):
    return [grid.send(column, (0, i, j, 0)) for i, j in grid.plane()]


def plane_of(grid, column, came):
    nz, nx, ny, _ = grid.shape
    _, x, y, _ = grid.own()
    layer = jnp.zeros((nz, nx, ny) + column.shape[1:], column.dtype)
    for (i, j), piece in zip([(0, 0)] + grid.plane(), [column] + came):
        layer = lax.dynamic_update_slice(
            layer, piece[:, None, None], (0, (x - i) % nx, (y - j) % ny, 0, 0)
        )
    return layer


def cores_sends(grid, layer):
    return [grid.send(layer, (0, 0, 0, s)) for s in range(1, grid.shape[3])]


def cores_of(grid, layer, came):
    ncore = grid.shape[3]
    core = grid.own()[3]
    full = jnp.zeros(grid.shape + layer.shape[3:], layer.dtype)
    for s, piece in enumerate([layer] + came):
        full = lax.dynamic_update_slice(
            full, piece[:, :, :, None], (0, 0, 0, (core - s) % ncore, 0, 0)
        )
    return full.reshape(-1, layer.shape[-1])


def core_terms(grid, parts):
    ncore = grid.shape[3]
    core = grid.own()[3]
    parts = parts.reshape(grid.shape + parts.shape[1:])
    terms = [lax.dynamic_index_in_dim(parts, core, 3, False)]
    for s in range(1, ncore):
        chunk = lax.dynamic_index_in_dim(parts, (core + s) % ncore, 3, False)
        terms.append(grid.send(chunk, (0, 0, 0, s)))
    return terms


def plane_terms(grid, layer):
    nz, nx, ny, _ = grid.shape
    _, x, y, _ = grid.own()
    rows, width = layer.shape[3:]

    def of(i, j):
        return lax.dynamic_slice(layer, (0, i, j, 0, 0), (nz, 1, 1, rows, width))[:, 0, 0]

    return [of(x, y)] + [
        grid.send(of((x + i) % nx, (y + j) % ny), (0, i, j, 0)) for i, j in grid.plane()
    ]


def column_terms(grid, column):
    nz = grid.shape[0]
    z = grid.own()[0]
    terms = [lax.dynamic_index_in_dim(column, z, 0, False)]
    for s in range(1, nz):
        chunk = lax.dynamic_index_in_dim(column, (z + s) % nz, 0, False)
        terms.append(grid.send(chunk, (s, 0, 0, 0)))
    return terms


def added(terms):
    return functools.reduce(lambda a, b: a + b, [t.astype(jnp.float32) for t in terms])


def added_low(terms):
    return added(terms).astype(jnp.bfloat16)


def after(first, *then):
    return lax.optimization_barrier((first,) + then)


def on_device(
    sizes,
    token_states,
    char_codes,
    lengths,
    token_cotangent,
    char_cotangent,
    char_table,
    recur_input,
    recur_state,
    project_weight,
    output_weight,
    merging_weight,
    up_weight,
    down_weight,
    char_weight,
    attend_gain,
    attend_shift,
    feed_gain,
    feed_shift,
    char_gain,
    char_shift,
):
    length, width = token_states.shape[1:]
    half = width // 2
    triple = 3 * half
    letters_count = char_table.shape[0]
    r = project_weight.shape[0]
    grid = Grid(sizes)
    devices = grid.devices
    ff_blocks = up_weight.shape[1] // width
    low = jnp.bfloat16

    taps, tap_rows = merging_weight.shape[:2]
    down_rows = down_weight.shape[0]
    second_rows = jnp.concatenate(
        [
            down_weight,
            merging_weight.reshape(-1, width),
            one_below_other(up_weight, ff_blocks),
            char_weight,
        ],
        axis=0,
    )
    second_all = lax.all_gather(second_rows, AXES, axis=0)
    gains = jnp.stack(
        [attend_gain, attend_shift, feed_gain, feed_shift, char_gain, char_shift]
    ).reshape(1, 6 * r)
    own_table = char_table.T
    gain_rows = jnp.pad(gains, ((0, own_table.shape[0] - 1), (0, 0)))
    table_rows = jnp.concatenate([own_table, gain_rows], axis=1)
    table_rows = jnp.pad(table_rows, ((0, 0), (0, triple - table_rows.shape[1])))
    char_rows = jnp.concatenate(
        [
            side_by_side(recur_input.T, 3),
            side_by_side(recur_state.T, 3),
            one_below_other(table_rows, 3),
        ],
        axis=1,
    )
    char_rows = jnp.concatenate([char_rows, side_by_side(output_weight, 3)], axis=0)
    project_came = column_sends(grid, project_weight)
    project_came, char_rows = after(project_came, char_rows)
    char_came = column_sends(grid, char_rows)
    project_column = column_of(grid, project_weight, project_came)
    project_came = plane_sends(grid, project_column)
    project_came, char_came = after(project_came, char_came)
    char_column = column_of(grid, char_rows, char_came)
    char_came = plane_sends(grid, char_column)
    project_layer = plane_of(grid, project_column, project_came)
    project_full = cores_of(grid, project_layer, cores_sends(grid, project_layer))
    states, codes = token_states[0], char_codes[0]
    mixed = product(states, project_full).astype(low)
    context_low, log_totals = attend(mixed, lengths, width)
    char_came, context_low = after(char_came, context_low)
    char_layer = plane_of(grid, char_column, char_came)
    first_all = cores_of(grid, char_layer, cores_sends(grid, char_layer))
    first_all = first_all.reshape(devices, -1, 3 * width)
    output_full = whole(one_below_other(first_all[:, r:], 3))
    chars_all = first_all[:, :r]
    inlet_full = whole(one_below_other(chars_all[:, :, :width], 3))
    recur_full = whole(one_below_other(chars_all[:, :, width : width + triple], 3))
    table_all = side_by_side(chars_all[:, :, width + triple :], 3)
    table_full = whole(table_all[:, :, : pl.cdiv(letters_count, LANES) * LANES])
    gains_all = table_all[:, 0, letters_count : letters_count + 6 * r]
    gains_all = gains_all.reshape(devices, 6, r).transpose(1, 0, 2).reshape(6, width)
    gains_all = gains_all.astype(jnp.float32)

    def second(start, rows):
        return second_all[:, start : start + rows]

    up_start = down_rows + taps * tap_rows
    upper_full = whole(side_by_side(second(up_start, ff_blocks * r), ff_blocks))
    branch_full = whole(second(up_start + ff_blocks * r, r))

    def rows_spec(start, rows):
        if rows % 16 == 0 and start % rows == 0:
            place = start // rows
            return second_all, pl.BlockSpec(
                (devices, rows, width), lambda b: (0, place, 0), pipeline_mode=pl.Buffered(1)
            )
        part = second(start, rows).reshape(ff_blocks, -1, width)
        return part, pl.BlockSpec(part.shape, lambda b: (0, 0, 0), pipeline_mode=pl.Buffered(1))

    valid = lax.broadcasted_iota(jnp.int32, (length, 1), 0) < lengths
    embeds, chars_rep, char_states, coefs = chars_forward(
        codes, table_full, inlet_full, recur_full
    )
    first_pre = states.astype(jnp.float32) + product(context_low, output_full)
    first = norm_parts(first_pre)[0] * gains_all[0] + gains_all[1]
    joined = jnp.where(
        valid, jnp.concatenate([first.astype(low), chars_rep], axis=-1), jnp.zeros((), low)
    )
    merging_parts = [rows_spec(down_rows + i * tap_rows, tap_rows) for i in range(taps)]
    (
        token_stream,
        char_stream,
        summed_low,
        merged_low,
        hidden_low,
        feed_grad,
        hidden_grad,
        branch_grad,
        merging_grad,
        summed_grad,
        char_pre_grad,
        gain_sums,
    ) = feed(
        joined,
        first,
        chars_rep,
        token_cotangent[0],
        char_cotangent[0],
        gains_all,
        upper_full,
        branch_full,
        merging_parts,
        rows_spec(0, down_rows),
    )
    feed_gain_grad, feed_shift_grad, char_gain_grad, char_shift_grad = jnp.sum(gain_sums, axis=1)
    early = early_parts(hidden_low, joined, feed_grad, merging_grad, devices)
    early, merging_grad, summed_low = after(early, merging_grad, summed_low)
    early = lax.psum_scatter(early, AXES, scatter_dimension=0, tiled=True)[0]
    up_parts = shares(outer_sum(summed_low, hidden_grad), devices)
    up_parts, merging_grad = after(up_parts, merging_grad)
    up_terms = core_terms(grid, up_parts)
    first_pre_grad, attended_grad, context_grad, rep_grad, attend_sums = merging_back(
        lengths,
        merging_grad,
        summed_grad,
        char_pre_grad,
        first_pre,
        gains_all,
        output_full,
        merging_parts,
    )
    up_terms, rep_grad, merged_low, attended_grad = after(
        up_terms, rep_grad, merged_low, attended_grad
    )
    attend_gain_grad, attend_shift_grad = jnp.sum(attend_sums, axis=1)
    branch_weight_grad = outer_sum(merged_low, branch_grad)
    output_weight_grad = outer_sum(context_low, attended_grad)
    up_layer, rep_grad = after(added_low(up_terms), rep_grad)
    up_terms = plane_terms(grid, up_layer)
    char_grads = chars_back(
        codes, inlet_full, recur_full, embeds, char_states, coefs, rep_grad, table_full.shape[1]
    )
    up_terms, char_grads, context_grad = after(up_terms, char_grads, context_grad)
    table_grad, inlet_grad, recur_weight_grad = char_grads
    up_column = added_low(up_terms)
    gain_grads = jnp.stack(
        [
            attend_gain_grad,
            attend_shift_grad,
            feed_gain_grad,
            feed_shift_grad,
            char_gain_grad,
            char_shift_grad,
        ]
    )
    gain_shares = gain_grads.reshape(6, devices, r).transpose(1, 0, 2).reshape(devices, 1, 6 * r)
    table_shares = shares(table_grad, devices)[:, :, :letters_count]
    gain_shares = jnp.pad(
        gain_shares.astype(low), ((0, 0), (0, table_shares.shape[1] - 1), (0, 0))
    )
    table_shares = jnp.concatenate([table_shares, gain_shares], axis=2)
    table_shares = jnp.pad(
        table_shares, ((0, 0), (0, 0), (0, triple - table_shares.shape[2]))
    )
    late = jnp.concatenate(
        [
            jnp.concatenate(
                [
                    side_by_side(shares(inlet_grad, devices), 3),
                    side_by_side(shares(recur_weight_grad, devices), 3),
                    one_below_other(table_shares, 3),
                ],
                axis=2,
            ),
            side_by_side(shares(output_weight_grad, devices), 3),
            side_by_side(shares(branch_weight_grad, devices), 3),
        ],
        axis=1,
    )
    def back(start, pairs, context_grad, earlier):
        return attend_back(
            mixed, context_grad, context_low, log_totals, lengths, width, start, pairs, earlier
        )

    every = width // LANES
    cut = every // 6
    up_column, late, context_grad = after(up_column, late, context_grad)
    up_terms = column_terms(grid, up_column)
    late_terms = core_terms(grid, late)
    grads = back(0, cut, context_grad, ())
    late_terms, up_terms, grads, context_grad = after(late_terms, up_terms, grads, context_grad)
    late_layer, context_grad = after(added_low(late_terms), context_grad)
    late_terms = plane_terms(grid, late_layer)
    grads = back(cut, every - cut, context_grad, grads)
    mixed_grad = jnp.concatenate(grads, axis=-1)
    project_parts = shares(outer_sum(states, mixed_grad), devices)
    late_terms, project_parts = after(late_terms, project_parts)
    late_terms = column_terms(grid, added_low(late_terms))
    project_layer = added_low(core_terms(grid, project_parts))
    project_layer, mixed_grad = after(project_layer, mixed_grad)
    project_terms = plane_terms(grid, project_layer)
    project_terms, late_terms, early = after(project_terms, late_terms, early)
    up_own, late = added(up_terms), added(late_terms)
    own_project = added(column_terms(grid, added_low(project_terms)))
    input_gradient = (first_pre_grad + back_product(mixed_grad, project_full)).astype(low)
    early = early.astype(jnp.float32)
    own_chars = late[:r]
    own_table_rows = side_by_side(own_chars[:, width + triple :], 3)
    own_gains = own_table_rows[0, letters_count : letters_count + 6 * r].reshape(6, r)
    return (
        token_stream[None],
        char_stream[None],
        input_gradient[None],
        own_table_rows[:, :letters_count].T,
        one_below_other(own_chars[:, :width], 3).T,
        one_below_other(own_chars[:, width : width + triple], 3).T,
        own_project,
        one_below_other(late[r : r + r // 3], 3),
        early[down_rows:].reshape(merging_weight.shape),
        up_own,
        early[:down_rows],
        one_below_other(late[r + r // 3 :], 3),
        own_gains[0],
        own_gains[1],
        own_gains[2],
        own_gains[3],
        own_gains[4],
        own_gains[5],
    )

def solution(mesh):
    placed = (
        P(AXES, None, None),
        P(AXES, None, None),
        P(AXES),
        P(AXES, None, None),
        P(AXES, None, None),
        P(None, AXES),
        P(None, AXES),
        P(None, AXES),
        P(AXES, None),
        P(AXES, None),
        P(None, AXES, None),
        P(AXES, None),
        P(AXES, None),
        P(AXES, None),
        P(AXES),
        P(AXES),
        P(AXES),
        P(AXES),
        P(AXES),
        P(AXES),
    )
    sizes = (mesh.shape["dp"], mesh.shape["fsdp"])
    return jax.shard_map(
        functools.partial(on_device, sizes),
        mesh=mesh,
        in_specs=placed,
        out_specs=(
            P(AXES, None, None),
            P(AXES, None, None),
            P(AXES, None, None),
            P(None, AXES),
            P(None, AXES),
            P(None, AXES),
            P(AXES, None),
            P(AXES, None),
            P(None, AXES, None),
            P(AXES, None),
            P(AXES, None),
            P(AXES, None),
            P(AXES),
            P(AXES),
            P(AXES),
            P(AXES),
            P(AXES),
            P(AXES),
        ),
        check_vma=False,
    )
```

```python
import functools
import itertools
import math

import jax
import jax.numpy as jnp
from jax import lax
from jax.experimental import pallas as pl
from jax.experimental.pallas import tpu as pltpu
from jax.sharding import PartitionSpec as P

HEAD_DIM = 64
CHARS = 4
LANES = 128
EPS = 1e-05
MASKED = -1e30
SCALE = 1.0 / math.sqrt(HEAD_DIM)
SCALE2 = math.log2(math.e) / math.sqrt(HEAD_DIM)
AXES = ("dp", "fsdp")
VMEM_LIMIT = 56 * 1024 * 1024
BRIEF = pl.CostEstimate(flops=200 * 10**9, bytes_accessed=10**6, transcendentals=0)

def product(left, right):
    return jnp.dot(left, right, preferred_element_type=jnp.float32)


def outer_sum(left, right):
    return jnp.einsum("li,lo->io", left, right, preferred_element_type=jnp.float32)


def back_product(grad_rows, weight):
    return jnp.einsum("lo,io->li", grad_rows, weight, preferred_element_type=jnp.float32)


def dotf(a,b,ca=1,cb=0):
    return lax.dot_general(a,b,(((ca,),(cb,)),((),())),preferred_element_type=jnp.float32)

def lane_half(shape):
    return lax.broadcasted_iota(jnp.int32, shape, 1) < HEAD_DIM

def attend_kernel(rows, length_ref, q_ref, k_ref, v_ref, ctx_ref, lse_ref, kx_ref, vx_ref):
    length = k_ref.shape[0]
    lane = lax.broadcasted_iota(jnp.int32, (length, LANES), 1)
    place = lax.broadcasted_iota(jnp.int32, (length, LANES), 0)
    kx_ref[:, :LANES] = k_ref[...]
    kx_ref[:, LANES:] = jnp.where((lane == 0) & (place >= length_ref[0]), MASKED, 0.0).astype(jnp.bfloat16)
    vx_ref[:, :LANES] = v_ref[...]
    vx_ref[:, LANES:] = jnp.ones((length, LANES), jnp.bfloat16)
    low = lane_half((rows, LANES))
    one = jnp.where(lax.broadcasted_iota(jnp.int32, (rows, LANES), 1) == 0, 1.0, 0.0).astype(jnp.bfloat16)
    def step(c, _):
        at = pl.ds(pl.multiple_of(c * rows, rows), rows)
        q = q_ref[at, :].astype(jnp.float32)
        outs = []
        for h in range(2):
            mine = low if h == 0 else jnp.logical_not(low)
            qx = jnp.concatenate([jnp.where(mine, q, 0.0).astype(jnp.bfloat16), one], axis=1)
            s = dotf(qx, kx_ref[...], 1, 1)
            peak = jnp.max(s, axis=1, keepdims=True) * SCALE2
            p = jnp.exp2(s * SCALE2 - peak).astype(jnp.bfloat16)
            o = dotf(p, vx_ref[...])
            total = o[:, LANES:]
            outs.append((o[:, :LANES] / total, peak + jnp.log2(total)))
        ctx_ref[at, :] = jnp.where(low, outs[0][0], outs[1][0]).astype(jnp.bfloat16)
        lse_ref[at, :] = jnp.where(low, outs[0][1], outs[1][1])
        return 0
    lax.fori_loop(0, length // rows, step, 0, unroll=True)

def attend(mixed, lengths, width, rows=256):
    length = mixed.shape[0]
    pairs = width // LANES
    spec = lambda o: pl.BlockSpec((length, LANES), lambda p, o=o: (0, p+o))
    return pl.pallas_call(
        functools.partial(attend_kernel, rows),
        grid=(pairs,),
        in_specs=[pl.BlockSpec(memory_space=pltpu.SMEM), spec(0), spec(pairs), spec(2 * pairs)],
        out_specs=[spec(0), spec(0)],
        out_shape=[jax.ShapeDtypeStruct((length, width), jnp.bfloat16), jax.ShapeDtypeStruct((length, width), jnp.float32)],
        scratch_shapes=[pltpu.VMEM((length, 2*LANES), jnp.bfloat16), pltpu.VMEM((length, 2*LANES), jnp.bfloat16)],
        compiler_params=pltpu.CompilerParams(vmem_limit_bytes=VMEM_LIMIT),
        cost_estimate=BRIEF,
    )(lengths, mixed, mixed, mixed)

def back_kernel(rows, length_ref, q_ref, k_ref, v_ref, do_ref, o_ref, lse_ref, *rest):
    dq_ref, dk_out, dv_out, kx_ref, qt_ref, dot_ref, dk_ref, dv_ref = rest[-8:]
    length = k_ref.shape[0]
    lane = lax.broadcasted_iota(jnp.int32, (length, LANES), 1)
    place = lax.broadcasted_iota(jnp.int32, (length, LANES), 0)
    kx_ref[:, :LANES] = k_ref[...]
    kx_ref[:, LANES:] = jnp.where((lane == 0) & (place >= length_ref[0]), MASKED, 0.0).astype(jnp.bfloat16)
    qt_ref[...] = q_ref[...].T
    dot_ref[...] = do_ref[...].T
    dk_ref[...] = jnp.zeros_like(dk_ref)
    dv_ref[...] = jnp.zeros_like(dv_ref)
    low = lane_half((rows, LANES))
    one = jnp.where(lax.broadcasted_iota(jnp.int32, (rows, LANES), 1) == 0, 1.0, 0.0).astype(jnp.bfloat16)
    def step(c, _):
        at = pl.ds(pl.multiple_of(c * rows, rows), rows)
        q = q_ref[at, :].astype(jnp.float32)
        do = do_ref[at, :].astype(jnp.float32)
        doo = do * o_ref[at, :].astype(jnp.float32)
        lse = lse_ref[at, :]
        dqs = []
        for h in range(2):
            mine = low if h == 0 else jnp.logical_not(low)
            qx = jnp.concatenate([jnp.where(mine, q, 0.0).astype(jnp.bfloat16), one], axis=1)
            s = dotf(qx, kx_ref[...], 1, 1)
            p = jnp.exp2(s * SCALE2 - lse[:, h*HEAD_DIM:h*HEAD_DIM+1])
            dp = dotf(jnp.where(mine, do, 0.0).astype(jnp.bfloat16), v_ref[...], 1, 1)
            delta = jnp.sum(jnp.where(mine, doo, 0.0), axis=1, keepdims=True)
            ds = (p * (dp - delta)).astype(jnp.bfloat16)
            pb = p.astype(jnp.bfloat16)
            hs = slice(h*HEAD_DIM, (h+1)*HEAD_DIM)
            dqs.append(dotf(ds, k_ref[...]))
            dk_ref[hs, :] += dotf(qt_ref[hs, at], ds)
            dv_ref[hs, :] += dotf(dot_ref[hs, at], pb)
        dq_ref[at, :] = (jnp.where(low, dqs[0], dqs[1]) * SCALE).astype(jnp.bfloat16)
        return 0
    lax.fori_loop(0, length // rows, step, 0, unroll=True)
    dk_out[...] = (dk_ref[...] * SCALE).T.astype(jnp.bfloat16)
    dv_out[...] = dv_ref[...].T.astype(jnp.bfloat16)

def attend_back(
    mixed, context_grad, context, log_totals, lengths, width, start, pairs, earlier, rows=256
):
    length = mixed.shape[0]
    every = width // LANES
    spec = lambda o: pl.BlockSpec((length, LANES), lambda p, o=o: (0, p + o + start))
    scratch = lambda a, b, t: pltpu.VMEM((a, b), t)
    return pl.pallas_call(
        functools.partial(back_kernel, rows),
        grid=(pairs,),
        in_specs=[pl.BlockSpec(memory_space=pltpu.SMEM), spec(0), spec(every), spec(2 * every)]
        + [spec(0)] * 3
        + [pl.BlockSpec(memory_space=pl.ANY)] * len(earlier),
        out_specs=[spec(0)] * 3,
        out_shape=[jax.ShapeDtypeStruct((length, width), jnp.bfloat16)] * 3,
        input_output_aliases={7 + i: i for i in range(len(earlier))},
        scratch_shapes=[
            scratch(length, 2 * LANES, jnp.bfloat16),
            scratch(LANES, length, jnp.bfloat16),
            scratch(LANES, length, jnp.bfloat16),
            scratch(LANES, length, jnp.float32),
            scratch(LANES, length, jnp.float32),
        ],
        compiler_params=pltpu.CompilerParams(vmem_limit_bytes=VMEM_LIMIT),
        cost_estimate=BRIEF,
    )(lengths, mixed, mixed, mixed, context_grad, context, log_totals, *earlier)


ROOT_HALF = math.sqrt(0.5)
DENSITY = 1.0 / math.sqrt(2.0 * math.pi)

def gelu_both(values):
    below = 0.5 + 0.5 * lax.erf(values * ROOT_HALF)
    return values * below, below + values * (DENSITY * jnp.exp(-0.5 * values * values))

def norm_parts(values):
    average = jnp.mean(values, axis=-1, keepdims=True)
    centred = values - average
    spread = lax.rsqrt(jnp.mean(centred * centred, axis=-1, keepdims=True) + EPS)
    return centred * spread, spread

def norm_back(normed, spread, scaled):
    return spread * (scaled - jnp.mean(scaled, axis=-1, keepdims=True)
                     - normed * jnp.mean(scaled * normed, axis=-1, keepdims=True))

def column_sums(values):
    rows, width = values.shape
    return jnp.sum(values.reshape(rows // 8, 8, width), axis=0)

def chars_kernel(half, codes_ref, table_ref, inlet_ref, recur_ref, embed_ref, rep_ref, states_ref, coef_ref):
    rows = codes_ref.shape[0]
    triple = 3 * half
    width = embed_ref.shape[1] // CHARS
    letters = lax.broadcasted_iota(jnp.int32, (rows, table_ref.shape[1]), 1)
    embeds = []
    for slot in range(CHARS):
        picked = jnp.where(codes_ref[:, slot : slot + 1] == letters, 1.0, 0.0).astype(jnp.bfloat16)
        embed = dotf(picked, table_ref[...], 1, 1).astype(jnp.bfloat16)
        embed_ref[:, slot * width : (slot + 1) * width] = embed
        embeds.append(embed)
    low = jnp.bfloat16
    states = [None, None]
    for step, side in itertools.product(range(CHARS), range(2)):
        slot = step if side == 0 else CHARS - 1 - step
        base = side * triple
        state = states[side]
        gates = dotf(embeds[slot], inlet_ref[base : base + triple, :], 1, 1)
        if state is None:
            update = jax.nn.sigmoid(gates[:, half : 2 * half])
            fresh = jnp.tanh(gates[:, 2 * half :])
            new = (1.0 - update) * fresh
            coef_ref[side, 0] = ((1.0 - update) * (1.0 - fresh * fresh)).astype(low)
            coef_ref[side, 1] = (-fresh * update * (1.0 - update)).astype(low)
        else:
            recur = dotf(state, recur_ref[base : base + triple, :], 1, 1)
            reset = jax.nn.sigmoid(gates[:, :half] + recur[:, :half])
            update = jax.nn.sigmoid(gates[:, half : 2 * half] + recur[:, half : 2 * half])
            recur_new = recur[:, 2 * half :]
            fresh = jnp.tanh(gates[:, 2 * half :] + reset * recur_new)
            before = state.astype(jnp.float32)
            new = (1.0 - update) * fresh + update * before
            at = 2 + 5 * (step - 1)
            coef_ref[side, at] = ((1.0 - update) * (1.0 - fresh * fresh)).astype(low)
            coef_ref[side, at + 1] = ((before - fresh) * update * (1.0 - update)).astype(low)
            coef_ref[side, at + 2] = (recur_new * reset * (1.0 - reset)).astype(low)
            coef_ref[side, at + 3] = reset.astype(low)
            coef_ref[side, at + 4] = update.astype(low)
        states[side] = new.astype(low)
        if step < CHARS - 1:
            states_ref[side, step] = states[side]
    for side in range(2):
        rep_ref[:, side * half : (side + 1) * half] = states[side]


COEFS = 2 + 5 * (CHARS - 1)

def chars_forward(codes, table, inlet, recur, rows=256):
    length = codes.shape[0]
    embed, half = inlet.shape[1], recur.shape[1]
    low = jnp.bfloat16
    full = lambda a: pl.BlockSpec(a.shape, lambda b: (0, 0))
    return pl.pallas_call(
        functools.partial(chars_kernel, half),
        grid=(length // rows,),
        in_specs=[pl.BlockSpec((rows, CHARS), lambda b: (b, 0)), full(table), full(inlet), full(recur)],
        out_specs=[
            pl.BlockSpec((rows, CHARS * embed), lambda b: (b, 0)),
            pl.BlockSpec((rows, 2 * half), lambda b: (b, 0)),
            pl.BlockSpec((2, CHARS - 1, rows, half), lambda b: (0, 0, b, 0)),
            pl.BlockSpec((2, COEFS, rows, half), lambda b: (0, 0, b, 0)),
        ],
        out_shape=[
            jax.ShapeDtypeStruct((length, CHARS * embed), low),
            jax.ShapeDtypeStruct((length, 2 * half), low),
            jax.ShapeDtypeStruct((2, CHARS - 1, length, half), low),
            jax.ShapeDtypeStruct((2, COEFS, length, half), low),
        ],
        compiler_params=pltpu.CompilerParams(vmem_limit_bytes=VMEM_LIMIT),
        cost_estimate=BRIEF,
    )(codes, table, inlet, recur)

def chars_back_kernel(half, codes_ref, inlet_ref, recur_ref, embed_ref, states_ref, coef_ref, grad_ref,
                      table_out, inlet_out, recur_out, gates_ref, lets_ref, steps_ref, table_acc, inlet_acc, recur_acc):
    rows = codes_ref.shape[0]
    triple = 3 * half
    width = embed_ref.shape[1] // CHARS
    low = jnp.bfloat16
    first, last = pl.program_id(0) == 0, pl.program_id(0) == pl.num_programs(0) - 1

    @pl.when(first)
    def _():
        table_acc[...] = jnp.zeros_like(table_acc)
        inlet_acc[...] = jnp.zeros_like(inlet_acc)
        recur_acc[...] = jnp.zeros_like(recur_acc)

    grads = [grad_ref[:, side * half : (side + 1) * half] for side in range(2)]
    for step, side in itertools.product(range(CHARS - 1, -1, -1), range(2)):
        slot = step if side == 0 else CHARS - 1 - step
        base = side * triple
        grad = grads[side]
        at = 2 + 5 * (step - 1) if step else 0
        load = lambda k: coef_ref[side, at + k].astype(jnp.float32)
        fresh_pre = grad * load(0)
        update_pre = (grad * load(1)).astype(low)
        spot = slice(slot * rows, (slot + 1) * rows)
        gates_ref[spot, base + half : base + 2 * half] = update_pre
        gates_ref[spot, base + 2 * half : base + triple] = fresh_pre.astype(low)
        if step == 0:
            gates_ref[spot, base : base + half] = jnp.zeros((rows, half), low)
            continue
        reset_pre = (fresh_pre * load(2)).astype(low)
        gates_ref[spot, base : base + half] = reset_pre
        recur_grad = jnp.concatenate(
            [reset_pre, update_pre, (fresh_pre * load(3)).astype(low)], axis=1)
        steps_ref[side, (step - 1) * rows : step * rows] = recur_grad
        grads[side] = grad * load(4) + dotf(recur_grad, recur_ref[base : base + triple, :])
    for side in range(2):
        base = side * triple
        states = states_ref[side].reshape(-1, half)
        recur_acc[:, base : base + triple] += dotf(states, steps_ref[side], 0, 0)
    embed_all = jnp.concatenate([embed_ref[:, j * width : (j + 1) * width] for j in range(CHARS)], axis=0)
    inlet_acc[...] += dotf(embed_all, gates_ref[...], 0, 0)
    embed_grad = dotf(gates_ref[...], inlet_ref[...]).astype(low)
    letters = lax.broadcasted_iota(jnp.int32, (rows, table_acc.shape[1]), 1)
    for slot in range(CHARS):
        lets_ref[slot * rows : (slot + 1) * rows, :] = jnp.where(
            codes_ref[:, slot : slot + 1] == letters, 1.0, 0.0).astype(low)
    table_acc[...] += dotf(embed_grad, lets_ref[...], 0, 0)

    @pl.when(last)
    def _():
        table_out[...] = table_acc[...].astype(low)
        for start in range(0, 2 * triple, half):
            cols = slice(start, start + half)
            inlet_out[cols, :] = inlet_acc[:, cols].T.astype(low)
            recur_out[cols, :] = recur_acc[:, cols].T.astype(low)


def chars_back(codes, inlet, recur, embeds, states, coefs, grad, letters, rows=256):
    length = codes.shape[0]
    embed, half = inlet.shape[1], recur.shape[1]
    low = jnp.bfloat16
    full = lambda a: pl.BlockSpec(a.shape, lambda b: (0, 0))
    outs = [(embed, letters), inlet.shape, recur.shape]
    return pl.pallas_call(
        functools.partial(chars_back_kernel, half),
        grid=(length // rows,),
        in_specs=[
            pl.BlockSpec((rows, CHARS), lambda b: (b, 0)), full(inlet), full(recur),
            pl.BlockSpec((rows, CHARS * embed), lambda b: (b, 0)),
            pl.BlockSpec((2, CHARS - 1, rows, half), lambda b: (0, 0, b, 0)),
            pl.BlockSpec((2, COEFS, rows, half), lambda b: (0, 0, b, 0)),
            pl.BlockSpec((rows, 2 * half), lambda b: (b, 0)),
        ],
        out_specs=[pl.BlockSpec(s, lambda b: (0, 0)) for s in outs],
        out_shape=[jax.ShapeDtypeStruct(s, low) for s in outs],
        scratch_shapes=[
            pltpu.VMEM((CHARS * rows, 6 * half), low),
            pltpu.VMEM((CHARS * rows, letters), low),
            pltpu.VMEM((2, (CHARS - 1) * rows, 3 * half), low),
            pltpu.VMEM((embed, letters), jnp.float32),
            pltpu.VMEM(inlet.shape[::-1], jnp.float32),
            pltpu.VMEM(recur.shape[::-1], jnp.float32),
        ],
        compiler_params=pltpu.CompilerParams(vmem_limit_bytes=VMEM_LIMIT),
        cost_estimate=BRIEF,
    )(codes, inlet, recur, embeds, states, coefs, grad)

def flat(ref, part=0, parts=1):
    count = ref.shape[0] // parts
    block = ref[part * count : (part + 1) * count]
    return block.reshape(-1, block.shape[-1])


PAD = 8


def spread_rows(rows_ref, wide_ref):
    length, width = rows_ref.shape
    blank = jnp.zeros((PAD, width), jnp.float32)
    wide_ref[:PAD] = blank
    wide_ref[PAD + length :] = blank
    for start in range(0, length, 256):
        block = rows_ref[start : start + 256]
        wide_ref[PAD + start : PAD + start + block.shape[0]] = block.astype(jnp.float32)


def neighbours(wide_ref, rows):
    base = pl.multiple_of(pl.program_id(0) * rows, rows)
    window = wide_ref[pl.ds(base, rows + 2 * PAD)]
    return [window[PAD + i : PAD + i + rows].astype(jnp.bfloat16) for i in (-1, 0, 1)]


def feed_kernel(blocks, joined_ref, first_ref, rep_ref, token_cot_ref, char_cot_ref, gains_ref,
                up_there, branch_ref, tap0_ref, tap1_ref, tap2_ref, down_there,
                token_ref, char_ref, summed_ref, merged_ref, hidden_ref, feed_grad_ref, hidden_grad_ref,
                branch_grad_ref, merging_grad_ref, summed_grad_ref, char_grad_ref, sums_ref, slope_ref, wide_ref,
                up_ref, down_ref, done):
    low = jnp.bfloat16
    width = first_ref.shape[1]
    step = up_ref.shape[1] // blocks
    merging_refs = (tap0_ref, tap1_ref, tap2_ref)

    copies = [
        pltpu.make_async_copy(up_there, up_ref, done.at[0]),
        pltpu.make_async_copy(down_there.at[:, : down_ref.shape[1]], down_ref, done.at[1]),
    ]

    @pl.when(pl.program_id(0) == 0)
    def _():
        for copy in copies:
            copy.start()
        sums_ref[...] = jnp.zeros_like(sums_ref)
        spread_rows(joined_ref, wide_ref)

    merging_pre = 0.0
    for moved, ref in zip(neighbours(wide_ref, first_ref.shape[0]), merging_refs):
        merging_pre = merging_pre + dotf(moved, flat(ref))
    merged, merging_slope = gelu_both(merging_pre)
    merged_low = merged.astype(low)
    merged_ref[...] = merged_low
    summed = first_ref[...] + merged
    summed_low = summed.astype(low)
    summed_ref[...] = summed_low

    @pl.when(pl.program_id(0) == 0)
    def _():
        for copy in copies:
            copy.wait()

    total = summed
    for c in range(blocks):
        cols = slice(c * step, (c + 1) * step)
        hidden, slope = gelu_both(dotf(summed_low, up_ref[:, cols]))
        slope_ref[:, cols] = slope
        hidden_low = hidden.astype(low)
        hidden_ref[:, cols] = hidden_low
        total = total + dotf(hidden_low, flat(down_ref, c, blocks))
    normed, spread = norm_parts(total)
    gain, shift = gains_ref[2:3, :], gains_ref[3:4, :]
    token_ref[...] = (normed * gain + shift).astype(low)
    cot = token_cot_ref[...].astype(jnp.float32)
    sums_ref[0] += column_sums(cot * normed)
    sums_ref[1] += column_sums(cot)
    token_grad = norm_back(normed, spread, cot * gain)
    feed_grad = token_grad.astype(low)
    feed_grad_ref[...] = feed_grad
    total = token_grad
    for c in range(blocks):
        cols = slice(c * step, (c + 1) * step)
        hidden_grad = (slope_ref[:, cols] * dotf(feed_grad, flat(down_ref, c, blocks), 1, 1)).astype(low)
        hidden_grad_ref[:, cols] = hidden_grad
        total = total + dotf(hidden_grad, up_ref[:, cols], 1, 1)
    summed_grad_ref[...] = total
    normed, spread = norm_parts(rep_ref[...].astype(jnp.float32) + dotf(merged_low, branch_ref[...]))
    gain, shift = gains_ref[4:5, :], gains_ref[5:6, :]
    char_ref[...] = (normed * gain + shift).astype(low)
    cot = char_cot_ref[...].astype(jnp.float32)
    sums_ref[2] += column_sums(cot * normed)
    sums_ref[3] += column_sums(cot)
    char_grad = norm_back(normed, spread, cot * gain)
    char_grad_ref[...] = char_grad
    branch_grad = char_grad.astype(low)
    branch_grad_ref[...] = branch_grad
    merging_grad_ref[...] = (merging_slope * (total + dotf(branch_grad, branch_ref[...], 1, 1))).astype(low)

def feed(joined, first, rep, token_cot, char_cot, gains, up, branch, merging, down, rows=256, blocks=2):
    length, width = first.shape
    ff = up.shape[1]
    low, wide = jnp.bfloat16, jnp.float32
    row = lambda w: pl.BlockSpec((rows, w), lambda b: (b, 0))
    full = lambda a: pl.BlockSpec(a.shape, lambda b: (0,) * a.ndim, pipeline_mode=pl.Buffered(1))
    there = pl.BlockSpec(memory_space=pl.ANY)
    outs = [(width, low), (width, low), (width, low), (width, low), (ff, low), (width, low), (ff, low),
            (width, low), (width, low), (width, wide), (width, wide)]
    return pl.pallas_call(
        functools.partial(feed_kernel, blocks),
        grid=(length // rows,),
        in_specs=[full(joined), row(width), row(width), row(width), row(width), full(gains),
                  there, full(branch)] + [spec for _, spec in merging] + [there],
        out_specs=[row(w) for w, _ in outs] + [pl.BlockSpec((4, 8, width), lambda b: (0, 0, 0))],
        out_shape=[jax.ShapeDtypeStruct((length, w), t) for w, t in outs] + [jax.ShapeDtypeStruct((4, 8, width), wide)],
        scratch_shapes=[
            pltpu.VMEM((rows, ff), wide),
            pltpu.VMEM((length + 2 * PAD, joined.shape[1]), wide),
            pltpu.VMEM(up.shape, low),
            pltpu.VMEM(down[1].block_shape, low),
            pltpu.SemaphoreType.DMA((2,)),
        ],
        compiler_params=pltpu.CompilerParams(vmem_limit_bytes=VMEM_LIMIT),
        cost_estimate=BRIEF,
    )(joined, first, rep, token_cot, char_cot, gains, up, branch, *[part for part, _ in merging + [down]])


def early_kernel(hidden_ref, joined_ref, feed_grad_ref, merging_grad_ref, out_ref, wide_ref, moved_ref):
    low = jnp.bfloat16
    count, _, width = out_ref.shape
    length = feed_grad_ref.shape[0]

    @pl.when(pl.program_id(0) == 0)
    def _():
        spread_rows(merging_grad_ref, wide_ref)
        for start in range(0, length, 256):
            window = wide_ref[start : start + 256 + 2 * PAD]
            for i, shift in enumerate((1, 0, -1)):
                moved_ref[i, start : start + 256] = window[PAD + shift : PAD + shift + 256].astype(low)

    def put(start, terms):
        terms = terms.astype(low).reshape(count, -1, width)
        out_ref[:, start : start + terms.shape[1]] = terms

    down = hidden_ref.shape[1] // count
    rows = joined_ref.shape[1] // count
    put(0, dotf(hidden_ref[...], feed_grad_ref[...], 0, 0))
    for i in range(moved_ref.shape[0]):
        put(down + i * rows, dotf(joined_ref[...], moved_ref[i], 0, 0))


def early_parts(hidden, joined, feed_grad, merging_grad, devices, taps=3, groups=4):
    length, width = feed_grad.shape
    low = jnp.bfloat16
    down, rows = hidden.shape[1] // devices, joined.shape[1] // devices
    if down % 16 or rows % 16:
        pairs = [(hidden, feed_grad)]
        pairs += [(joined[:-1], merging_grad[1:]), (joined, merging_grad), (joined[1:], merging_grad[:-1])]
        return jnp.concatenate([shares(outer_sum(*pair), devices) for pair in pairs], axis=1)
    columns = lambda a: pl.BlockSpec((length, a.shape[1] // groups), lambda g: (0, g))
    full = pl.BlockSpec((length, width), lambda g: (0, 0))
    shape = (devices, down + taps * rows, width)
    return pl.pallas_call(
        early_kernel,
        grid=(groups,),
        in_specs=[columns(hidden), columns(joined), full, full],
        out_specs=pl.BlockSpec((devices // groups,) + shape[1:], lambda g: (g, 0, 0)),
        out_shape=jax.ShapeDtypeStruct(shape, low),
        scratch_shapes=[
            pltpu.VMEM((length + 2 * PAD, width), jnp.float32),
            pltpu.VMEM((taps, length, width), low),
        ],
        compiler_params=pltpu.CompilerParams(vmem_limit_bytes=VMEM_LIMIT),
        cost_estimate=BRIEF,
    )(hidden, joined, feed_grad, merging_grad)


def merging_back_kernel(length_ref, grad_ref, summed_ref, char_ref, pre_ref, gains_ref, output_ref,
                        tap0_ref, tap1_ref, tap2_ref,
                        pre_grad_ref, attended_ref, context_ref, rep_ref, sums_ref, wide_ref):
    rows, width = pre_ref.shape
    low = jnp.bfloat16

    @pl.when(pl.program_id(0) == 0)
    def _():
        sums_ref[...] = jnp.zeros_like(sums_ref)
        spread_rows(grad_ref, wide_ref)

    joined = 0.0
    for moved, ref in zip(neighbours(wide_ref, rows), (tap2_ref, tap1_ref, tap0_ref)):
        joined = joined + dotf(moved, flat(ref), 1, 1)
    place = pl.program_id(0) * rows + lax.broadcasted_iota(jnp.int32, (rows, 1), 0)
    joined = jnp.where(place < length_ref[0], joined, 0.0)
    rep_ref[...] = char_ref[...] + joined[:, width:]
    first_grad = summed_ref[...] + joined[:, :width]
    normed, spread = norm_parts(pre_ref[...])
    sums_ref[0] += column_sums(first_grad * normed)
    sums_ref[1] += column_sums(first_grad)
    pre_grad = norm_back(normed, spread, first_grad * gains_ref[0:1, :])
    pre_grad_ref[...] = pre_grad
    attended = pre_grad.astype(low)
    attended_ref[...] = attended
    context_ref[...] = dotf(attended, output_ref[...], 1, 1).astype(low)


def merging_back(lengths, grad, summed_grad, char_grad, pre, gains, output, merging, rows=256):
    length, width = pre.shape
    low, wide = jnp.bfloat16, jnp.float32
    row = pl.BlockSpec((rows, width), lambda b: (b, 0))
    full = lambda a: pl.BlockSpec(a.shape, lambda b: (0, 0), pipeline_mode=pl.Buffered(1))
    kinds = (wide, low, low, wide)
    return pl.pallas_call(
        merging_back_kernel,
        grid=(length // rows,),
        in_specs=[pl.BlockSpec(memory_space=pltpu.SMEM), full(grad), row, row, row, full(gains), full(output)]
        + [spec for _, spec in merging],
        out_specs=[row] * 4 + [pl.BlockSpec((2, 8, width), lambda b: (0, 0, 0))],
        out_shape=[jax.ShapeDtypeStruct((length, width), t) for t in kinds]
        + [jax.ShapeDtypeStruct((2, 8, width), wide)],
        scratch_shapes=[pltpu.VMEM((length + 2 * PAD, width), wide)],
        compiler_params=pltpu.CompilerParams(vmem_limit_bytes=VMEM_LIMIT),
        cost_estimate=BRIEF,
    )(lengths, grad, summed_grad, char_grad, pre, gains, output, *[part for part, _ in merging])


def side_by_side(rows, groups):
    r = rows.shape[-2] // groups
    return jnp.concatenate(
        [rows[..., i * r : (i + 1) * r, :] for i in range(groups)], axis=-1
    )


def one_below_other(rows, groups):
    w = rows.shape[-1] // groups
    return jnp.concatenate(
        [rows[..., i * w : (i + 1) * w] for i in range(groups)], axis=-2
    )


def whole(part):
    return part.reshape(-1, part.shape[-1])


def shares(full, devices):
    return full.reshape(devices, -1, full.shape[-1]).astype(jnp.bfloat16)


class Grid:
    def __init__(self, sizes):
        dp, fsdp = sizes
        z = 4 if dp % 4 == 0 else 1
        core = 2 if fsdp % 2 == 0 else 1
        self.fsdp = fsdp
        self.shape = (z, dp // z, fsdp // core, core)
        self.devices = dp * fsdp

    def own(self):
        z, x, y, core = self.shape
        dp, fsdp = lax.axis_index("dp"), lax.axis_index("fsdp")
        return dp // x, dp % x, fsdp // core, fsdp % core

    def send(self, values, shift):
        pairs = []
        for source, place in enumerate(itertools.product(*map(range, self.shape))):
            target = 0
            for at, by, size in zip(place, shift, self.shape):
                target = target * size + (at + by) % size
            pairs.append((source, target))
        return lax.ppermute(values, AXES, pairs)

    def plane(self):
        z, x, y, core = self.shape
        return [(i, j) for i in range(x) for j in range(y) if i or j]


def column_sends(grid, part):
    return [grid.send(part, (s, 0, 0, 0)) for s in range(1, grid.shape[0])]


def column_of(grid, part, came):
    nz = grid.shape[0]
    z = grid.own()[0]
    column = jnp.zeros((nz,) + part.shape, part.dtype)
    for s, piece in enumerate([part] + came):
        column = lax.dynamic_update_slice(column, piece[None], ((z - s) % nz, 0, 0))
    return column


def plane_sends(grid, column):
    return [grid.send(column, (0, i, j, 0)) for i, j in grid.plane()]


def plane_of(grid, column, came):
    nz, nx, ny, _ = grid.shape
    _, x, y, _ = grid.own()
    layer = jnp.zeros((nz, nx, ny) + column.shape[1:], column.dtype)
    for (i, j), piece in zip([(0, 0)] + grid.plane(), [column] + came):
        layer = lax.dynamic_update_slice(
            layer, piece[:, None, None], (0, (x - i) % nx, (y - j) % ny, 0, 0)
        )
    return layer


def cores_sends(grid, layer):
    return [grid.send(layer, (0, 0, 0, s)) for s in range(1, grid.shape[3])]


def cores_of(grid, layer, came):
    ncore = grid.shape[3]
    core = grid.own()[3]
    full = jnp.zeros(grid.shape + layer.shape[3:], layer.dtype)
    for s, piece in enumerate([layer] + came):
        full = lax.dynamic_update_slice(
            full, piece[:, :, :, None], (0, 0, 0, (core - s) % ncore, 0, 0)
        )
    return full.reshape(-1, layer.shape[-1])


def core_terms(grid, parts):
    ncore = grid.shape[3]
    core = grid.own()[3]
    parts = parts.reshape(grid.shape + parts.shape[1:])
    terms = [lax.dynamic_index_in_dim(parts, core, 3, False)]
    for s in range(1, ncore):
        chunk = lax.dynamic_index_in_dim(parts, (core + s) % ncore, 3, False)
        terms.append(grid.send(chunk, (0, 0, 0, s)))
    return terms


def plane_terms(grid, layer):
    nz, nx, ny, _ = grid.shape
    _, x, y, _ = grid.own()
    rows, width = layer.shape[3:]

    def of(i, j):
        return lax.dynamic_slice(layer, (0, i, j, 0, 0), (nz, 1, 1, rows, width))[:, 0, 0]

    return [of(x, y)] + [
        grid.send(of((x + i) % nx, (y + j) % ny), (0, i, j, 0)) for i, j in grid.plane()
    ]


def column_terms(grid, column):
    nz = grid.shape[0]
    z = grid.own()[0]
    terms = [lax.dynamic_index_in_dim(column, z, 0, False)]
    for s in range(1, nz):
        chunk = lax.dynamic_index_in_dim(column, (z + s) % nz, 0, False)
        terms.append(grid.send(chunk, (s, 0, 0, 0)))
    return terms


def added(terms):
    return functools.reduce(lambda a, b: a + b, [t.astype(jnp.float32) for t in terms])


def added_low(terms):
    return added(terms).astype(jnp.bfloat16)


def after(first, *then):
    return lax.optimization_barrier((first,) + then)


def on_device(
    sizes,
    token_states,
    char_codes,
    lengths,
    token_cotangent,
    char_cotangent,
    char_table,
    recur_input,
    recur_state,
    project_weight,
    output_weight,
    merging_weight,
    up_weight,
    down_weight,
    char_weight,
    attend_gain,
    attend_shift,
    feed_gain,
    feed_shift,
    char_gain,
    char_shift,
):
    length, width = token_states.shape[1:]
    half = width // 2
    triple = 3 * half
    letters_count = char_table.shape[0]
    r = project_weight.shape[0]
    grid = Grid(sizes)
    devices = grid.devices
    ff_blocks = up_weight.shape[1] // width
    low = jnp.bfloat16

    taps, tap_rows = merging_weight.shape[:2]
    down_rows = down_weight.shape[0]
    second_rows = jnp.concatenate(
        [
            down_weight,
            merging_weight.reshape(-1, width),
            one_below_other(up_weight, ff_blocks),
            char_weight,
        ],
        axis=0,
    )
    second_all = lax.all_gather(second_rows, AXES, axis=0)
    gains = jnp.stack(
        [attend_gain, attend_shift, feed_gain, feed_shift, char_gain, char_shift]
    ).reshape(1, 6 * r)
    own_table = char_table.T
    gain_rows = jnp.pad(gains, ((0, own_table.shape[0] - 1), (0, 0)))
    table_rows = jnp.concatenate([own_table, gain_rows], axis=1)
    table_rows = jnp.pad(table_rows, ((0, 0), (0, triple - table_rows.shape[1])))
    char_rows = jnp.concatenate(
        [
            side_by_side(recur_input.T, 3),
            side_by_side(recur_state.T, 3),
            one_below_other(table_rows, 3),
        ],
        axis=1,
    )
    char_rows = jnp.concatenate([char_rows, side_by_side(output_weight, 3)], axis=0)
    project_came = column_sends(grid, project_weight)
    project_came, char_rows = after(project_came, char_rows)
    char_came = column_sends(grid, char_rows)
    project_column = column_of(grid, project_weight, project_came)
    project_came = plane_sends(grid, project_column)
    project_came, char_came = after(project_came, char_came)
    char_column = column_of(grid, char_rows, char_came)
    char_came = plane_sends(grid, char_column)
    project_layer = plane_of(grid, project_column, project_came)
    project_full = cores_of(grid, project_layer, cores_sends(grid, project_layer))
    states, codes = token_states[0], char_codes[0]
    mixed = product(states, project_full).astype(low)
    context_low, log_totals = attend(mixed, lengths, width)
    char_came, context_low = after(char_came, context_low)
    char_layer = plane_of(grid, char_column, char_came)
    first_all = cores_of(grid, char_layer, cores_sends(grid, char_layer))
    first_all = first_all.reshape(devices, -1, 3 * width)
    output_full = whole(one_below_other(first_all[:, r:], 3))
    chars_all = first_all[:, :r]
    inlet_full = whole(one_below_other(chars_all[:, :, :width], 3))
    recur_full = whole(one_below_other(chars_all[:, :, width : width + triple], 3))
    table_all = side_by_side(chars_all[:, :, width + triple :], 3)
    table_full = whole(table_all[:, :, : pl.cdiv(letters_count, LANES) * LANES])
    gains_all = table_all[:, 0, letters_count : letters_count + 6 * r]
    gains_all = gains_all.reshape(devices, 6, r).transpose(1, 0, 2).reshape(6, width)
    gains_all = gains_all.astype(jnp.float32)

    def second(start, rows):
        return second_all[:, start : start + rows]

    up_start = down_rows + taps * tap_rows
    upper_full = whole(side_by_side(second(up_start, ff_blocks * r), ff_blocks))
    branch_full = whole(second(up_start + ff_blocks * r, r))

    def rows_spec(start, rows):
        if rows % 16 == 0 and start % rows == 0:
            place = start // rows
            return second_all, pl.BlockSpec(
                (devices, rows, width), lambda b: (0, place, 0), pipeline_mode=pl.Buffered(1)
            )
        part = second(start, rows).reshape(ff_blocks, -1, width)
        return part, pl.BlockSpec(part.shape, lambda b: (0, 0, 0), pipeline_mode=pl.Buffered(1))

    valid = lax.broadcasted_iota(jnp.int32, (length, 1), 0) < lengths
    embeds, chars_rep, char_states, coefs = chars_forward(
        codes, table_full, inlet_full, recur_full
    )
    first_pre = states.astype(jnp.float32) + product(context_low, output_full)
    first = norm_parts(first_pre)[0] * gains_all[0] + gains_all[1]
    joined = jnp.where(
        valid, jnp.concatenate([first.astype(low), chars_rep], axis=-1), jnp.zeros((), low)
    )
    merging_parts = [rows_spec(down_rows + i * tap_rows, tap_rows) for i in range(taps)]
    (
        token_stream,
        char_stream,
        summed_low,
        merged_low,
        hidden_low,
        feed_grad,
        hidden_grad,
        branch_grad,
        merging_grad,
        summed_grad,
        char_pre_grad,
        gain_sums,
    ) = feed(
        joined,
        first,
        chars_rep,
        token_cotangent[0],
        char_cotangent[0],
        gains_all,
        upper_full,
        branch_full,
        merging_parts,
        rows_spec(0, down_rows),
    )
    feed_gain_grad, feed_shift_grad, char_gain_grad, char_shift_grad = jnp.sum(gain_sums, axis=1)
    early = early_parts(hidden_low, joined, feed_grad, merging_grad, devices)
    early, merging_grad, summed_low = after(early, merging_grad, summed_low)
    early = lax.psum_scatter(early, AXES, scatter_dimension=0, tiled=True)[0]
    up_parts = shares(outer_sum(summed_low, hidden_grad), devices)
    up_parts, merging_grad = after(up_parts, merging_grad)
    up_terms = core_terms(grid, up_parts)
    first_pre_grad, attended_grad, context_grad, rep_grad, attend_sums = merging_back(
        lengths,
        merging_grad,
        summed_grad,
        char_pre_grad,
        first_pre,
        gains_all,
        output_full,
        merging_parts,
    )
    up_terms, rep_grad, merged_low, attended_grad = after(
        up_terms, rep_grad, merged_low, attended_grad
    )
    attend_gain_grad, attend_shift_grad = jnp.sum(attend_sums, axis=1)
    branch_weight_grad = outer_sum(merged_low, branch_grad)
    output_weight_grad = outer_sum(context_low, attended_grad)
    up_layer, rep_grad = after(added_low(up_terms), rep_grad)
    up_terms = plane_terms(grid, up_layer)
    char_grads = chars_back(
        codes, inlet_full, recur_full, embeds, char_states, coefs, rep_grad, table_full.shape[1]
    )
    up_terms, char_grads, context_grad = after(up_terms, char_grads, context_grad)
    table_grad, inlet_grad, recur_weight_grad = char_grads
    up_column = added_low(up_terms)
    gain_grads = jnp.stack(
        [
            attend_gain_grad,
            attend_shift_grad,
            feed_gain_grad,
            feed_shift_grad,
            char_gain_grad,
            char_shift_grad,
        ]
    )
    gain_shares = gain_grads.reshape(6, devices, r).transpose(1, 0, 2).reshape(devices, 1, 6 * r)
    table_shares = shares(table_grad, devices)[:, :, :letters_count]
    gain_shares = jnp.pad(
        gain_shares.astype(low), ((0, 0), (0, table_shares.shape[1] - 1), (0, 0))
    )
    table_shares = jnp.concatenate([table_shares, gain_shares], axis=2)
    table_shares = jnp.pad(
        table_shares, ((0, 0), (0, 0), (0, triple - table_shares.shape[2]))
    )
    late = jnp.concatenate(
        [
            jnp.concatenate(
                [
                    side_by_side(shares(inlet_grad, devices), 3),
                    side_by_side(shares(recur_weight_grad, devices), 3),
                    one_below_other(table_shares, 3),
                ],
                axis=2,
            ),
            side_by_side(shares(output_weight_grad, devices), 3),
            side_by_side(shares(branch_weight_grad, devices), 3),
        ],
        axis=1,
    )
    def back(start, pairs, context_grad, earlier):
        return attend_back(
            mixed, context_grad, context_low, log_totals, lengths, width, start, pairs, earlier
        )

    every = width // LANES
    cut = every // 6
    up_column, late, context_grad = after(up_column, late, context_grad)
    up_terms = column_terms(grid, up_column)
    late_terms = core_terms(grid, late)
    grads = back(0, cut, context_grad, ())
    late_terms, up_terms, grads, context_grad = after(late_terms, up_terms, grads, context_grad)
    late_layer, context_grad = after(added_low(late_terms), context_grad)
    late_terms = plane_terms(grid, late_layer)
    grads = back(cut, every - cut, context_grad, grads)
    late_terms[3:], grads = after(late_terms[3:], grads)
    mixed_grad = jnp.concatenate(grads, axis=-1)
    project_parts = shares(outer_sum(states, mixed_grad), devices)
    late_terms, project_parts = after(late_terms, project_parts)
    late_terms = column_terms(grid, added_low(late_terms))
    project_layer = added_low(core_terms(grid, project_parts))
    project_layer, mixed_grad = after(project_layer, mixed_grad)
    project_terms = plane_terms(grid, project_layer)
    project_terms, late_terms = after(project_terms, late_terms)
    up_own, late = added(up_terms), added(late_terms)
    project_terms = column_terms(grid, added_low(project_terms))
    _, early = after(project_terms[1], early)
    early_own = (
        early[:down_rows].astype(jnp.float32),
        early[down_rows:].astype(jnp.float32).reshape(merging_weight.shape),
    )
    project_terms, early_own = after(project_terms, early_own)
    own_project = added(project_terms)
    input_gradient = (first_pre_grad + back_product(mixed_grad, project_full)).astype(low)
    own_chars = late[:r]
    own_table_rows = side_by_side(own_chars[:, width + triple :], 3)
    own_gains = own_table_rows[0, letters_count : letters_count + 6 * r].reshape(6, r)
    return (
        token_stream[None],
        char_stream[None],
        input_gradient[None],
        own_table_rows[:, :letters_count].T,
        one_below_other(own_chars[:, :width], 3).T,
        one_below_other(own_chars[:, width : width + triple], 3).T,
        own_project,
        one_below_other(late[r : r + r // 3], 3),
        early_own[1],
        up_own,
        early_own[0],
        one_below_other(late[r + r // 3 :], 3),
        own_gains[0],
        own_gains[1],
        own_gains[2],
        own_gains[3],
        own_gains[4],
        own_gains[5],
    )

def solution(mesh):
    placed = (
        P(AXES, None, None),
        P(AXES, None, None),
        P(AXES),
        P(AXES, None, None),
        P(AXES, None, None),
        P(None, AXES),
        P(None, AXES),
        P(None, AXES),
        P(AXES, None),
        P(AXES, None),
        P(None, AXES, None),
        P(AXES, None),
        P(AXES, None),
        P(AXES, None),
        P(AXES),
        P(AXES),
        P(AXES),
        P(AXES),
        P(AXES),
        P(AXES),
    )
    sizes = (mesh.shape["dp"], mesh.shape["fsdp"])
    return jax.shard_map(
        functools.partial(on_device, sizes),
        mesh=mesh,
        in_specs=placed,
        out_specs=(
            P(AXES, None, None),
            P(AXES, None, None),
            P(AXES, None, None),
            P(None, AXES),
            P(None, AXES),
            P(None, AXES),
            P(AXES, None),
            P(AXES, None),
            P(None, AXES, None),
            P(AXES, None),
            P(AXES, None),
            P(AXES, None),
            P(AXES),
            P(AXES),
            P(AXES),
            P(AXES),
            P(AXES),
            P(AXES),
        ),
        check_vma=False,
    )
```

```python
import functools
import itertools
import math

import jax
import jax.numpy as jnp
from jax import lax
from jax.experimental import pallas as pl
from jax.experimental.pallas import tpu as pltpu
from jax.sharding import PartitionSpec as P

HEAD_DIM = 64
CHARS = 4
LANES = 128
EPS = 1e-05
MASKED = -1e30
SCALE = 1.0 / math.sqrt(HEAD_DIM)
SCALE2 = math.log2(math.e) / math.sqrt(HEAD_DIM)
AXES = ("dp", "fsdp")
VMEM_LIMIT = 56 * 1024 * 1024
BRIEF = pl.CostEstimate(flops=200 * 10**9, bytes_accessed=10**6, transcendentals=0)

def product(left, right):
    return jnp.dot(left, right, preferred_element_type=jnp.float32)


def outer_sum(left, right):
    return jnp.einsum("li,lo->io", left, right, preferred_element_type=jnp.float32)


def back_product(grad_rows, weight):
    return jnp.einsum("lo,io->li", grad_rows, weight, preferred_element_type=jnp.float32)


def dotf(a,b,ca=1,cb=0):
    return lax.dot_general(a,b,(((ca,),(cb,)),((),())),preferred_element_type=jnp.float32)

def lane_half(shape):
    return lax.broadcasted_iota(jnp.int32, shape, 1) < HEAD_DIM

def attend_kernel(rows, length_ref, q_ref, k_ref, v_ref, ctx_ref, lse_ref, kx_ref, vx_ref):
    length = k_ref.shape[0]
    lane = lax.broadcasted_iota(jnp.int32, (length, LANES), 1)
    place = lax.broadcasted_iota(jnp.int32, (length, LANES), 0)
    kx_ref[:, :LANES] = k_ref[...]
    kx_ref[:, LANES:] = jnp.where((lane == 0) & (place >= length_ref[0]), MASKED, 0.0).astype(jnp.bfloat16)
    vx_ref[:, :LANES] = v_ref[...]
    vx_ref[:, LANES:] = jnp.ones((length, LANES), jnp.bfloat16)
    low = lane_half((rows, LANES))
    one = jnp.where(lax.broadcasted_iota(jnp.int32, (rows, LANES), 1) == 0, 1.0, 0.0).astype(jnp.bfloat16)
    def step(c, _):
        at = pl.ds(pl.multiple_of(c * rows, rows), rows)
        q = q_ref[at, :].astype(jnp.float32)
        outs = []
        for h in range(2):
            mine = low if h == 0 else jnp.logical_not(low)
            qx = jnp.concatenate([jnp.where(mine, q, 0.0).astype(jnp.bfloat16), one], axis=1)
            s = dotf(qx, kx_ref[...], 1, 1)
            peak = jnp.max(s, axis=1, keepdims=True) * SCALE2
            p = jnp.exp2(s * SCALE2 - peak).astype(jnp.bfloat16)
            o = dotf(p, vx_ref[...])
            total = o[:, LANES:]
            outs.append((o[:, :LANES] / total, peak + jnp.log2(total)))
        ctx_ref[at, :] = jnp.where(low, outs[0][0], outs[1][0]).astype(jnp.bfloat16)
        lse_ref[at, :] = jnp.where(low, outs[0][1], outs[1][1])
        return 0
    lax.fori_loop(0, length // rows, step, 0, unroll=True)

def attend(mixed, lengths, width, rows=256):
    length = mixed.shape[0]
    pairs = width // LANES
    spec = lambda o: pl.BlockSpec((length, LANES), lambda p, o=o: (0, p+o))
    return pl.pallas_call(
        functools.partial(attend_kernel, rows),
        grid=(pairs,),
        in_specs=[pl.BlockSpec(memory_space=pltpu.SMEM), spec(0), spec(pairs), spec(2 * pairs)],
        out_specs=[spec(0), spec(0)],
        out_shape=[jax.ShapeDtypeStruct((length, width), jnp.bfloat16), jax.ShapeDtypeStruct((length, width), jnp.float32)],
        scratch_shapes=[pltpu.VMEM((length, 2*LANES), jnp.bfloat16), pltpu.VMEM((length, 2*LANES), jnp.bfloat16)],
        compiler_params=pltpu.CompilerParams(vmem_limit_bytes=VMEM_LIMIT),
        cost_estimate=BRIEF,
    )(lengths, mixed, mixed, mixed)

def back_kernel(rows, length_ref, q_ref, k_ref, v_ref, do_ref, o_ref, lse_ref, *rest):
    dq_ref, dk_out, dv_out, kx_ref, qt_ref, dot_ref, dk_ref, dv_ref = rest[-8:]
    length = k_ref.shape[0]
    lane = lax.broadcasted_iota(jnp.int32, (length, LANES), 1)
    place = lax.broadcasted_iota(jnp.int32, (length, LANES), 0)
    kx_ref[:, :LANES] = k_ref[...]
    kx_ref[:, LANES:] = jnp.where((lane == 0) & (place >= length_ref[0]), MASKED, 0.0).astype(jnp.bfloat16)
    qt_ref[...] = q_ref[...].T
    dot_ref[...] = do_ref[...].T
    dk_ref[...] = jnp.zeros_like(dk_ref)
    dv_ref[...] = jnp.zeros_like(dv_ref)
    low = lane_half((rows, LANES))
    one = jnp.where(lax.broadcasted_iota(jnp.int32, (rows, LANES), 1) == 0, 1.0, 0.0).astype(jnp.bfloat16)
    def step(c, _):
        at = pl.ds(pl.multiple_of(c * rows, rows), rows)
        q = q_ref[at, :].astype(jnp.float32)
        do = do_ref[at, :].astype(jnp.float32)
        doo = do * o_ref[at, :].astype(jnp.float32)
        lse = lse_ref[at, :]
        dqs = []
        for h in range(2):
            mine = low if h == 0 else jnp.logical_not(low)
            qx = jnp.concatenate([jnp.where(mine, q, 0.0).astype(jnp.bfloat16), one], axis=1)
            s = dotf(qx, kx_ref[...], 1, 1)
            p = jnp.exp2(s * SCALE2 - lse[:, h*HEAD_DIM:h*HEAD_DIM+1])
            dp = dotf(jnp.where(mine, do, 0.0).astype(jnp.bfloat16), v_ref[...], 1, 1)
            delta = jnp.sum(jnp.where(mine, doo, 0.0), axis=1, keepdims=True)
            ds = (p * (dp - delta)).astype(jnp.bfloat16)
            pb = p.astype(jnp.bfloat16)
            hs = slice(h*HEAD_DIM, (h+1)*HEAD_DIM)
            dqs.append(dotf(ds, k_ref[...]))
            dk_ref[hs, :] += dotf(qt_ref[hs, at], ds)
            dv_ref[hs, :] += dotf(dot_ref[hs, at], pb)
        dq_ref[at, :] = (jnp.where(low, dqs[0], dqs[1]) * SCALE).astype(jnp.bfloat16)
        return 0
    lax.fori_loop(0, length // rows, step, 0, unroll=True)
    dk_out[...] = (dk_ref[...] * SCALE).T.astype(jnp.bfloat16)
    dv_out[...] = dv_ref[...].T.astype(jnp.bfloat16)

def attend_back(
    mixed, context_grad, context, log_totals, lengths, width, start, pairs, earlier, rows=256
):
    length = mixed.shape[0]
    every = width // LANES
    spec = lambda o: pl.BlockSpec((length, LANES), lambda p, o=o: (0, p + o + start))
    scratch = lambda a, b, t: pltpu.VMEM((a, b), t)
    return pl.pallas_call(
        functools.partial(back_kernel, rows),
        grid=(pairs,),
        in_specs=[pl.BlockSpec(memory_space=pltpu.SMEM), spec(0), spec(every), spec(2 * every)]
        + [spec(0)] * 3
        + [pl.BlockSpec(memory_space=pl.ANY)] * len(earlier),
        out_specs=[spec(0)] * 3,
        out_shape=[jax.ShapeDtypeStruct((length, width), jnp.bfloat16)] * 3,
        input_output_aliases={7 + i: i for i in range(len(earlier))},
        scratch_shapes=[
            scratch(length, 2 * LANES, jnp.bfloat16),
            scratch(LANES, length, jnp.bfloat16),
            scratch(LANES, length, jnp.bfloat16),
            scratch(LANES, length, jnp.float32),
            scratch(LANES, length, jnp.float32),
        ],
        compiler_params=pltpu.CompilerParams(vmem_limit_bytes=VMEM_LIMIT),
        cost_estimate=BRIEF,
    )(lengths, mixed, mixed, mixed, context_grad, context, log_totals, *earlier)


ROOT_HALF = math.sqrt(0.5)
DENSITY = 1.0 / math.sqrt(2.0 * math.pi)

def gelu_both(values):
    below = 0.5 + 0.5 * lax.erf(values * ROOT_HALF)
    return values * below, below + values * (DENSITY * jnp.exp(-0.5 * values * values))

def norm_parts(values):
    average = jnp.mean(values, axis=-1, keepdims=True)
    centred = values - average
    spread = lax.rsqrt(jnp.mean(centred * centred, axis=-1, keepdims=True) + EPS)
    return centred * spread, spread

def norm_back(normed, spread, scaled):
    return spread * (scaled - jnp.mean(scaled, axis=-1, keepdims=True)
                     - normed * jnp.mean(scaled * normed, axis=-1, keepdims=True))

def column_sums(values):
    rows, width = values.shape
    return jnp.sum(values.reshape(rows // 8, 8, width), axis=0)

def chars_kernel(half, codes_ref, table_ref, inlet_ref, recur_ref, embed_ref, rep_ref, states_ref, coef_ref):
    rows = codes_ref.shape[0]
    triple = 3 * half
    width = embed_ref.shape[1] // CHARS
    letters = lax.broadcasted_iota(jnp.int32, (rows, table_ref.shape[1]), 1)
    embeds = []
    for slot in range(CHARS):
        picked = jnp.where(codes_ref[:, slot : slot + 1] == letters, 1.0, 0.0).astype(jnp.bfloat16)
        embed = dotf(picked, table_ref[...], 1, 1).astype(jnp.bfloat16)
        embed_ref[:, slot * width : (slot + 1) * width] = embed
        embeds.append(embed)
    low = jnp.bfloat16
    states = [None, None]
    for step, side in itertools.product(range(CHARS), range(2)):
        slot = step if side == 0 else CHARS - 1 - step
        base = side * triple
        state = states[side]
        gates = dotf(embeds[slot], inlet_ref[base : base + triple, :], 1, 1)
        if state is None:
            update = jax.nn.sigmoid(gates[:, half : 2 * half])
            fresh = jnp.tanh(gates[:, 2 * half :])
            new = (1.0 - update) * fresh
            coef_ref[side, 0] = ((1.0 - update) * (1.0 - fresh * fresh)).astype(low)
            coef_ref[side, 1] = (-fresh * update * (1.0 - update)).astype(low)
        else:
            recur = dotf(state, recur_ref[base : base + triple, :], 1, 1)
            reset = jax.nn.sigmoid(gates[:, :half] + recur[:, :half])
            update = jax.nn.sigmoid(gates[:, half : 2 * half] + recur[:, half : 2 * half])
            recur_new = recur[:, 2 * half :]
            fresh = jnp.tanh(gates[:, 2 * half :] + reset * recur_new)
            before = state.astype(jnp.float32)
            new = (1.0 - update) * fresh + update * before
            at = 2 + 5 * (step - 1)
            coef_ref[side, at] = ((1.0 - update) * (1.0 - fresh * fresh)).astype(low)
            coef_ref[side, at + 1] = ((before - fresh) * update * (1.0 - update)).astype(low)
            coef_ref[side, at + 2] = (recur_new * reset * (1.0 - reset)).astype(low)
            coef_ref[side, at + 3] = reset.astype(low)
            coef_ref[side, at + 4] = update.astype(low)
        states[side] = new.astype(low)
        if step < CHARS - 1:
            states_ref[side, step] = states[side]
    for side in range(2):
        rep_ref[:, side * half : (side + 1) * half] = states[side]


COEFS = 2 + 5 * (CHARS - 1)

def chars_forward(codes, table, inlet, recur, rows=256):
    length = codes.shape[0]
    embed, half = inlet.shape[1], recur.shape[1]
    low = jnp.bfloat16
    full = lambda a: pl.BlockSpec(a.shape, lambda b: (0, 0))
    return pl.pallas_call(
        functools.partial(chars_kernel, half),
        grid=(length // rows,),
        in_specs=[pl.BlockSpec((rows, CHARS), lambda b: (b, 0)), full(table), full(inlet), full(recur)],
        out_specs=[
            pl.BlockSpec((rows, CHARS * embed), lambda b: (b, 0)),
            pl.BlockSpec((rows, 2 * half), lambda b: (b, 0)),
            pl.BlockSpec((2, CHARS - 1, rows, half), lambda b: (0, 0, b, 0)),
            pl.BlockSpec((2, COEFS, rows, half), lambda b: (0, 0, b, 0)),
        ],
        out_shape=[
            jax.ShapeDtypeStruct((length, CHARS * embed), low),
            jax.ShapeDtypeStruct((length, 2 * half), low),
            jax.ShapeDtypeStruct((2, CHARS - 1, length, half), low),
            jax.ShapeDtypeStruct((2, COEFS, length, half), low),
        ],
        compiler_params=pltpu.CompilerParams(vmem_limit_bytes=VMEM_LIMIT),
        cost_estimate=BRIEF,
    )(codes, table, inlet, recur)

def chars_back_kernel(half, codes_ref, inlet_ref, recur_ref, embed_ref, states_ref, coef_ref, grad_ref,
                      table_out, inlet_out, recur_out, gates_ref, lets_ref, steps_ref, table_acc, inlet_acc, recur_acc):
    rows = codes_ref.shape[0]
    triple = 3 * half
    width = embed_ref.shape[1] // CHARS
    low = jnp.bfloat16
    first, last = pl.program_id(0) == 0, pl.program_id(0) == pl.num_programs(0) - 1

    @pl.when(first)
    def _():
        table_acc[...] = jnp.zeros_like(table_acc)
        inlet_acc[...] = jnp.zeros_like(inlet_acc)
        recur_acc[...] = jnp.zeros_like(recur_acc)

    grads = [grad_ref[:, side * half : (side + 1) * half] for side in range(2)]
    for step, side in itertools.product(range(CHARS - 1, -1, -1), range(2)):
        slot = step if side == 0 else CHARS - 1 - step
        base = side * triple
        grad = grads[side]
        at = 2 + 5 * (step - 1) if step else 0
        load = lambda k: coef_ref[side, at + k].astype(jnp.float32)
        fresh_pre = grad * load(0)
        update_pre = (grad * load(1)).astype(low)
        spot = slice(slot * rows, (slot + 1) * rows)
        gates_ref[spot, base + half : base + 2 * half] = update_pre
        gates_ref[spot, base + 2 * half : base + triple] = fresh_pre.astype(low)
        if step == 0:
            gates_ref[spot, base : base + half] = jnp.zeros((rows, half), low)
            continue
        reset_pre = (fresh_pre * load(2)).astype(low)
        gates_ref[spot, base : base + half] = reset_pre
        recur_grad = jnp.concatenate(
            [reset_pre, update_pre, (fresh_pre * load(3)).astype(low)], axis=1)
        steps_ref[side, (step - 1) * rows : step * rows] = recur_grad
        grads[side] = grad * load(4) + dotf(recur_grad, recur_ref[base : base + triple, :])
    for side in range(2):
        base = side * triple
        states = states_ref[side].reshape(-1, half)
        recur_acc[:, base : base + triple] += dotf(states, steps_ref[side], 0, 0)
    embed_all = jnp.concatenate([embed_ref[:, j * width : (j + 1) * width] for j in range(CHARS)], axis=0)
    inlet_acc[...] += dotf(embed_all, gates_ref[...], 0, 0)
    embed_grad = dotf(gates_ref[...], inlet_ref[...]).astype(low)
    letters = lax.broadcasted_iota(jnp.int32, (rows, table_acc.shape[1]), 1)
    for slot in range(CHARS):
        lets_ref[slot * rows : (slot + 1) * rows, :] = jnp.where(
            codes_ref[:, slot : slot + 1] == letters, 1.0, 0.0).astype(low)
    table_acc[...] += dotf(embed_grad, lets_ref[...], 0, 0)

    @pl.when(last)
    def _():
        table_out[...] = table_acc[...].astype(low)
        for start in range(0, 2 * triple, half):
            cols = slice(start, start + half)
            inlet_out[cols, :] = inlet_acc[:, cols].T.astype(low)
            recur_out[cols, :] = recur_acc[:, cols].T.astype(low)


def chars_back(codes, inlet, recur, embeds, states, coefs, grad, letters, rows=256):
    length = codes.shape[0]
    embed, half = inlet.shape[1], recur.shape[1]
    low = jnp.bfloat16
    full = lambda a: pl.BlockSpec(a.shape, lambda b: (0, 0))
    outs = [(embed, letters), inlet.shape, recur.shape]
    return pl.pallas_call(
        functools.partial(chars_back_kernel, half),
        grid=(length // rows,),
        in_specs=[
            pl.BlockSpec((rows, CHARS), lambda b: (b, 0)), full(inlet), full(recur),
            pl.BlockSpec((rows, CHARS * embed), lambda b: (b, 0)),
            pl.BlockSpec((2, CHARS - 1, rows, half), lambda b: (0, 0, b, 0)),
            pl.BlockSpec((2, COEFS, rows, half), lambda b: (0, 0, b, 0)),
            pl.BlockSpec((rows, 2 * half), lambda b: (b, 0)),
        ],
        out_specs=[pl.BlockSpec(s, lambda b: (0, 0)) for s in outs],
        out_shape=[jax.ShapeDtypeStruct(s, low) for s in outs],
        scratch_shapes=[
            pltpu.VMEM((CHARS * rows, 6 * half), low),
            pltpu.VMEM((CHARS * rows, letters), low),
            pltpu.VMEM((2, (CHARS - 1) * rows, 3 * half), low),
            pltpu.VMEM((embed, letters), jnp.float32),
            pltpu.VMEM(inlet.shape[::-1], jnp.float32),
            pltpu.VMEM(recur.shape[::-1], jnp.float32),
        ],
        compiler_params=pltpu.CompilerParams(vmem_limit_bytes=VMEM_LIMIT),
        cost_estimate=BRIEF,
    )(codes, inlet, recur, embeds, states, coefs, grad)

def flat(ref, part=0, parts=1):
    count = ref.shape[0] // parts
    block = ref[part * count : (part + 1) * count]
    return block.reshape(-1, block.shape[-1])


PAD = 8


def spread_rows(rows_ref, wide_ref):
    length, width = rows_ref.shape
    blank = jnp.zeros((PAD, width), jnp.float32)
    wide_ref[:PAD] = blank
    wide_ref[PAD + length :] = blank
    for start in range(0, length, 256):
        block = rows_ref[start : start + 256]
        wide_ref[PAD + start : PAD + start + block.shape[0]] = block.astype(jnp.float32)


def neighbours(wide_ref, rows):
    base = pl.multiple_of(pl.program_id(0) * rows, rows)
    window = wide_ref[pl.ds(base, rows + 2 * PAD)]
    return [window[PAD + i : PAD + i + rows].astype(jnp.bfloat16) for i in (-1, 0, 1)]


def feed_kernel(blocks, joined_ref, first_ref, rep_ref, token_cot_ref, char_cot_ref, gains_ref,
                up_there, branch_ref, tap0_ref, tap1_ref, tap2_ref, down_there,
                token_ref, char_ref, summed_ref, merged_ref, hidden_ref, feed_grad_ref, hidden_grad_ref,
                branch_grad_ref, merging_grad_ref, summed_grad_ref, char_grad_ref, sums_ref, slope_ref, wide_ref,
                up_ref, down_ref, done):
    low = jnp.bfloat16
    width = first_ref.shape[1]
    step = up_ref.shape[1] // blocks
    merging_refs = (tap0_ref, tap1_ref, tap2_ref)

    copies = [
        pltpu.make_async_copy(up_there, up_ref, done.at[0]),
        pltpu.make_async_copy(down_there.at[:, : down_ref.shape[1]], down_ref, done.at[1]),
    ]

    @pl.when(pl.program_id(0) == 0)
    def _():
        for copy in copies:
            copy.start()
        sums_ref[...] = jnp.zeros_like(sums_ref)
        spread_rows(joined_ref, wide_ref)

    merging_pre = 0.0
    for moved, ref in zip(neighbours(wide_ref, first_ref.shape[0]), merging_refs):
        merging_pre = merging_pre + dotf(moved, flat(ref))
    merged, merging_slope = gelu_both(merging_pre)
    merged_low = merged.astype(low)
    merged_ref[...] = merged_low
    summed = first_ref[...] + merged
    summed_low = summed.astype(low)
    summed_ref[...] = summed_low

    @pl.when(pl.program_id(0) == 0)
    def _():
        for copy in copies:
            copy.wait()

    total = summed
    for c in range(blocks):
        cols = slice(c * step, (c + 1) * step)
        hidden, slope = gelu_both(dotf(summed_low, up_ref[:, cols]))
        slope_ref[:, cols] = slope
        hidden_low = hidden.astype(low)
        hidden_ref[:, cols] = hidden_low
        total = total + dotf(hidden_low, flat(down_ref, c, blocks))
    normed, spread = norm_parts(total)
    gain, shift = gains_ref[2:3, :], gains_ref[3:4, :]
    token_ref[...] = (normed * gain + shift).astype(low)
    cot = token_cot_ref[...].astype(jnp.float32)
    sums_ref[0] += column_sums(cot * normed)
    sums_ref[1] += column_sums(cot)
    token_grad = norm_back(normed, spread, cot * gain)
    feed_grad = token_grad.astype(low)
    feed_grad_ref[...] = feed_grad
    total = token_grad
    for c in range(blocks):
        cols = slice(c * step, (c + 1) * step)
        hidden_grad = (slope_ref[:, cols] * dotf(feed_grad, flat(down_ref, c, blocks), 1, 1)).astype(low)
        hidden_grad_ref[:, cols] = hidden_grad
        total = total + dotf(hidden_grad, up_ref[:, cols], 1, 1)
    summed_grad_ref[...] = total
    normed, spread = norm_parts(rep_ref[...].astype(jnp.float32) + dotf(merged_low, branch_ref[...]))
    gain, shift = gains_ref[4:5, :], gains_ref[5:6, :]
    char_ref[...] = (normed * gain + shift).astype(low)
    cot = char_cot_ref[...].astype(jnp.float32)
    sums_ref[2] += column_sums(cot * normed)
    sums_ref[3] += column_sums(cot)
    char_grad = norm_back(normed, spread, cot * gain)
    char_grad_ref[...] = char_grad
    branch_grad = char_grad.astype(low)
    branch_grad_ref[...] = branch_grad
    merging_grad_ref[...] = (merging_slope * (total + dotf(branch_grad, branch_ref[...], 1, 1))).astype(low)

def feed(joined, first, rep, token_cot, char_cot, gains, up, branch, merging, down, rows=256, blocks=2):
    length, width = first.shape
    ff = up.shape[1]
    low, wide = jnp.bfloat16, jnp.float32
    row = lambda w: pl.BlockSpec((rows, w), lambda b: (b, 0))
    full = lambda a: pl.BlockSpec(a.shape, lambda b: (0,) * a.ndim, pipeline_mode=pl.Buffered(1))
    there = pl.BlockSpec(memory_space=pl.ANY)
    outs = [(width, low), (width, low), (width, low), (width, low), (ff, low), (width, low), (ff, low),
            (width, low), (width, low), (width, wide), (width, wide)]
    return pl.pallas_call(
        functools.partial(feed_kernel, blocks),
        grid=(length // rows,),
        in_specs=[full(joined), row(width), row(width), row(width), row(width), full(gains),
                  there, full(branch)] + [spec for _, spec in merging] + [there],
        out_specs=[row(w) for w, _ in outs] + [pl.BlockSpec((4, 8, width), lambda b: (0, 0, 0))],
        out_shape=[jax.ShapeDtypeStruct((length, w), t) for w, t in outs] + [jax.ShapeDtypeStruct((4, 8, width), wide)],
        scratch_shapes=[
            pltpu.VMEM((rows, ff), wide),
            pltpu.VMEM((length + 2 * PAD, joined.shape[1]), wide),
            pltpu.VMEM(up.shape, low),
            pltpu.VMEM(down[1].block_shape, low),
            pltpu.SemaphoreType.DMA((2,)),
        ],
        compiler_params=pltpu.CompilerParams(vmem_limit_bytes=VMEM_LIMIT),
        cost_estimate=BRIEF,
    )(joined, first, rep, token_cot, char_cot, gains, up, branch, *[part for part, _ in merging + [down]])


def early_kernel(hidden_ref, joined_ref, feed_grad_ref, merging_grad_ref, out_ref, wide_ref, moved_ref):
    low = jnp.bfloat16
    count, _, width = out_ref.shape
    length = feed_grad_ref.shape[0]

    @pl.when(pl.program_id(0) == 0)
    def _():
        spread_rows(merging_grad_ref, wide_ref)
        for start in range(0, length, 256):
            window = wide_ref[start : start + 256 + 2 * PAD]
            for i, shift in enumerate((1, 0, -1)):
                moved_ref[i, start : start + 256] = window[PAD + shift : PAD + shift + 256].astype(low)

    def put(start, terms):
        terms = terms.astype(low).reshape(count, -1, width)
        out_ref[:, start : start + terms.shape[1]] = terms

    down = hidden_ref.shape[1] // count
    rows = joined_ref.shape[1] // count
    put(0, dotf(hidden_ref[...], feed_grad_ref[...], 0, 0))
    for i in range(moved_ref.shape[0]):
        put(down + i * rows, dotf(joined_ref[...], moved_ref[i], 0, 0))


def early_parts(hidden, joined, feed_grad, merging_grad, devices, taps=3, groups=4):
    length, width = feed_grad.shape
    low = jnp.bfloat16
    down, rows = hidden.shape[1] // devices, joined.shape[1] // devices
    if down % 16 or rows % 16:
        pairs = [(hidden, feed_grad)]
        pairs += [(joined[:-1], merging_grad[1:]), (joined, merging_grad), (joined[1:], merging_grad[:-1])]
        return jnp.concatenate([shares(outer_sum(*pair), devices) for pair in pairs], axis=1)
    columns = lambda a: pl.BlockSpec((length, a.shape[1] // groups), lambda g: (0, g))
    full = pl.BlockSpec((length, width), lambda g: (0, 0))
    shape = (devices, down + taps * rows, width)
    return pl.pallas_call(
        early_kernel,
        grid=(groups,),
        in_specs=[columns(hidden), columns(joined), full, full],
        out_specs=pl.BlockSpec((devices // groups,) + shape[1:], lambda g: (g, 0, 0)),
        out_shape=jax.ShapeDtypeStruct(shape, low),
        scratch_shapes=[
            pltpu.VMEM((length + 2 * PAD, width), jnp.float32),
            pltpu.VMEM((taps, length, width), low),
        ],
        compiler_params=pltpu.CompilerParams(vmem_limit_bytes=VMEM_LIMIT),
        cost_estimate=BRIEF,
    )(hidden, joined, feed_grad, merging_grad)


def merging_back_kernel(length_ref, grad_ref, summed_ref, char_ref, pre_ref, gains_ref, output_ref,
                        tap0_ref, tap1_ref, tap2_ref,
                        pre_grad_ref, attended_ref, context_ref, rep_ref, sums_ref, wide_ref):
    rows, width = pre_ref.shape
    low = jnp.bfloat16

    @pl.when(pl.program_id(0) == 0)
    def _():
        sums_ref[...] = jnp.zeros_like(sums_ref)
        spread_rows(grad_ref, wide_ref)

    joined = 0.0
    for moved, ref in zip(neighbours(wide_ref, rows), (tap2_ref, tap1_ref, tap0_ref)):
        joined = joined + dotf(moved, flat(ref), 1, 1)
    place = pl.program_id(0) * rows + lax.broadcasted_iota(jnp.int32, (rows, 1), 0)
    joined = jnp.where(place < length_ref[0], joined, 0.0)
    rep_ref[...] = char_ref[...] + joined[:, width:]
    first_grad = summed_ref[...] + joined[:, :width]
    normed, spread = norm_parts(pre_ref[...])
    sums_ref[0] += column_sums(first_grad * normed)
    sums_ref[1] += column_sums(first_grad)
    pre_grad = norm_back(normed, spread, first_grad * gains_ref[0:1, :])
    pre_grad_ref[...] = pre_grad
    attended = pre_grad.astype(low)
    attended_ref[...] = attended
    context_ref[...] = dotf(attended, output_ref[...], 1, 1).astype(low)


def merging_back(lengths, grad, summed_grad, char_grad, pre, gains, output, merging, rows=256):
    length, width = pre.shape
    low, wide = jnp.bfloat16, jnp.float32
    row = pl.BlockSpec((rows, width), lambda b: (b, 0))
    full = lambda a: pl.BlockSpec(a.shape, lambda b: (0, 0), pipeline_mode=pl.Buffered(1))
    kinds = (wide, low, low, wide)
    return pl.pallas_call(
        merging_back_kernel,
        grid=(length // rows,),
        in_specs=[pl.BlockSpec(memory_space=pltpu.SMEM), full(grad), row, row, row, full(gains), full(output)]
        + [spec for _, spec in merging],
        out_specs=[row] * 4 + [pl.BlockSpec((2, 8, width), lambda b: (0, 0, 0))],
        out_shape=[jax.ShapeDtypeStruct((length, width), t) for t in kinds]
        + [jax.ShapeDtypeStruct((2, 8, width), wide)],
        scratch_shapes=[pltpu.VMEM((length + 2 * PAD, width), wide)],
        compiler_params=pltpu.CompilerParams(vmem_limit_bytes=VMEM_LIMIT),
        cost_estimate=BRIEF,
    )(lengths, grad, summed_grad, char_grad, pre, gains, output, *[part for part, _ in merging])


def side_by_side(rows, groups):
    r = rows.shape[-2] // groups
    return jnp.concatenate(
        [rows[..., i * r : (i + 1) * r, :] for i in range(groups)], axis=-1
    )


def one_below_other(rows, groups):
    w = rows.shape[-1] // groups
    return jnp.concatenate(
        [rows[..., i * w : (i + 1) * w] for i in range(groups)], axis=-2
    )


def whole(part):
    return part.reshape(-1, part.shape[-1])


def shares(full, devices):
    return full.reshape(devices, -1, full.shape[-1]).astype(jnp.bfloat16)


class Grid:
    def __init__(self, sizes):
        dp, fsdp = sizes
        z = 4 if dp % 4 == 0 else 1
        core = 2 if fsdp % 2 == 0 else 1
        self.fsdp = fsdp
        self.shape = (z, dp // z, fsdp // core, core)
        self.devices = dp * fsdp

    def own(self):
        z, x, y, core = self.shape
        dp, fsdp = lax.axis_index("dp"), lax.axis_index("fsdp")
        return dp // x, dp % x, fsdp // core, fsdp % core

    def send(self, values, shift):
        pairs = []
        for source, place in enumerate(itertools.product(*map(range, self.shape))):
            target = 0
            for at, by, size in zip(place, shift, self.shape):
                target = target * size + (at + by) % size
            pairs.append((source, target))
        return lax.ppermute(values, AXES, pairs)

    def plane(self):
        z, x, y, core = self.shape
        return [(i, j) for i in range(x) for j in range(y) if i or j]


def column_sends(grid, part):
    return [grid.send(part, (s, 0, 0, 0)) for s in range(1, grid.shape[0])]


def column_of(grid, part, came):
    nz = grid.shape[0]
    z = grid.own()[0]
    column = jnp.zeros((nz,) + part.shape, part.dtype)
    for s, piece in enumerate([part] + came):
        column = lax.dynamic_update_slice(column, piece[None], ((z - s) % nz, 0, 0))
    return column


def plane_sends(grid, column):
    return [grid.send(column, (0, i, j, 0)) for i, j in grid.plane()]


def plane_of(grid, column, came):
    nz, nx, ny, _ = grid.shape
    _, x, y, _ = grid.own()
    layer = jnp.zeros((nz, nx, ny) + column.shape[1:], column.dtype)
    for (i, j), piece in zip([(0, 0)] + grid.plane(), [column] + came):
        layer = lax.dynamic_update_slice(
            layer, piece[:, None, None], (0, (x - i) % nx, (y - j) % ny, 0, 0)
        )
    return layer


def cores_sends(grid, layer):
    return [grid.send(layer, (0, 0, 0, s)) for s in range(1, grid.shape[3])]


def cores_of(grid, layer, came):
    ncore = grid.shape[3]
    core = grid.own()[3]
    full = jnp.zeros(grid.shape + layer.shape[3:], layer.dtype)
    for s, piece in enumerate([layer] + came):
        full = lax.dynamic_update_slice(
            full, piece[:, :, :, None], (0, 0, 0, (core - s) % ncore, 0, 0)
        )
    return full.reshape(-1, layer.shape[-1])


def core_terms(grid, parts):
    ncore = grid.shape[3]
    core = grid.own()[3]
    parts = parts.reshape(grid.shape + parts.shape[1:])
    terms = [lax.dynamic_index_in_dim(parts, core, 3, False)]
    for s in range(1, ncore):
        chunk = lax.dynamic_index_in_dim(parts, (core + s) % ncore, 3, False)
        terms.append(grid.send(chunk, (0, 0, 0, s)))
    return terms


def plane_terms(grid, layer):
    nz, nx, ny, _ = grid.shape
    _, x, y, _ = grid.own()
    rows, width = layer.shape[3:]

    def of(i, j):
        return lax.dynamic_slice(layer, (0, i, j, 0, 0), (nz, 1, 1, rows, width))[:, 0, 0]

    return [of(x, y)] + [
        grid.send(of((x + i) % nx, (y + j) % ny), (0, i, j, 0)) for i, j in grid.plane()
    ]


def column_terms(grid, column):
    nz = grid.shape[0]
    z = grid.own()[0]
    terms = [lax.dynamic_index_in_dim(column, z, 0, False)]
    for s in range(1, nz):
        chunk = lax.dynamic_index_in_dim(column, (z + s) % nz, 0, False)
        terms.append(grid.send(chunk, (s, 0, 0, 0)))
    return terms


def added(terms):
    return functools.reduce(lambda a, b: a + b, [t.astype(jnp.float32) for t in terms])


def added_low(terms):
    return added(terms).astype(jnp.bfloat16)


def after(first, *then):
    return lax.optimization_barrier((first,) + then)


def on_device(
    sizes,
    token_states,
    char_codes,
    lengths,
    token_cotangent,
    char_cotangent,
    char_table,
    recur_input,
    recur_state,
    project_weight,
    output_weight,
    merging_weight,
    up_weight,
    down_weight,
    char_weight,
    attend_gain,
    attend_shift,
    feed_gain,
    feed_shift,
    char_gain,
    char_shift,
):
    length, width = token_states.shape[1:]
    half = width // 2
    triple = 3 * half
    letters_count = char_table.shape[0]
    r = project_weight.shape[0]
    grid = Grid(sizes)
    devices = grid.devices
    ff_blocks = up_weight.shape[1] // width
    low = jnp.bfloat16

    taps, tap_rows = merging_weight.shape[:2]
    down_rows = down_weight.shape[0]
    second_rows = jnp.concatenate(
        [
            down_weight,
            merging_weight.reshape(-1, width),
            one_below_other(up_weight, ff_blocks),
            char_weight,
        ],
        axis=0,
    )
    second_all = lax.all_gather(second_rows, AXES, axis=0)
    gains = jnp.stack(
        [attend_gain, attend_shift, feed_gain, feed_shift, char_gain, char_shift]
    ).reshape(1, 6 * r)
    own_table = char_table.T
    gain_rows = jnp.pad(gains, ((0, own_table.shape[0] - 1), (0, 0)))
    table_rows = jnp.concatenate([own_table, gain_rows], axis=1)
    table_rows = jnp.pad(table_rows, ((0, 0), (0, triple - table_rows.shape[1])))
    char_rows = jnp.concatenate(
        [
            side_by_side(recur_input.T, 3),
            side_by_side(recur_state.T, 3),
            one_below_other(table_rows, 3),
        ],
        axis=1,
    )
    char_rows = jnp.concatenate([char_rows, side_by_side(output_weight, 3)], axis=0)
    project_came = column_sends(grid, project_weight)
    project_came, char_rows = after(project_came, char_rows)
    char_came = column_sends(grid, char_rows)
    project_column = column_of(grid, project_weight, project_came)
    project_came = plane_sends(grid, project_column)
    project_came, char_came = after(project_came, char_came)
    char_column = column_of(grid, char_rows, char_came)
    char_came = plane_sends(grid, char_column)
    project_layer = plane_of(grid, project_column, project_came)
    project_full = cores_of(grid, project_layer, cores_sends(grid, project_layer))
    states, codes = token_states[0], char_codes[0]
    mixed = product(states, project_full).astype(low)
    context_low, log_totals = attend(mixed, lengths, width)
    char_came, context_low = after(char_came, context_low)
    char_layer = plane_of(grid, char_column, char_came)
    first_all = cores_of(grid, char_layer, cores_sends(grid, char_layer))
    first_all = first_all.reshape(devices, -1, 3 * width)
    output_full = whole(one_below_other(first_all[:, r:], 3))
    chars_all = first_all[:, :r]
    inlet_full = whole(one_below_other(chars_all[:, :, :width], 3))
    recur_full = whole(one_below_other(chars_all[:, :, width : width + triple], 3))
    table_all = side_by_side(chars_all[:, :, width + triple :], 3)
    table_full = whole(table_all[:, :, : pl.cdiv(letters_count, LANES) * LANES])
    gains_all = table_all[:, 0, letters_count : letters_count + 6 * r]
    gains_all = gains_all.reshape(devices, 6, r).transpose(1, 0, 2).reshape(6, width)
    gains_all = gains_all.astype(jnp.float32)

    def second(start, rows):
        return second_all[:, start : start + rows]

    up_start = down_rows + taps * tap_rows
    upper_full = whole(side_by_side(second(up_start, ff_blocks * r), ff_blocks))
    branch_full = whole(second(up_start + ff_blocks * r, r))

    def rows_spec(start, rows):
        if rows % 16 == 0 and start % rows == 0:
            place = start // rows
            return second_all, pl.BlockSpec(
                (devices, rows, width), lambda b: (0, place, 0), pipeline_mode=pl.Buffered(1)
            )
        part = second(start, rows).reshape(ff_blocks, -1, width)
        return part, pl.BlockSpec(part.shape, lambda b: (0, 0, 0), pipeline_mode=pl.Buffered(1))

    valid = lax.broadcasted_iota(jnp.int32, (length, 1), 0) < lengths
    embeds, chars_rep, char_states, coefs = chars_forward(
        codes, table_full, inlet_full, recur_full
    )
    first_pre = states.astype(jnp.float32) + product(context_low, output_full)
    first = norm_parts(first_pre)[0] * gains_all[0] + gains_all[1]
    joined = jnp.where(
        valid, jnp.concatenate([first.astype(low), chars_rep], axis=-1), jnp.zeros((), low)
    )
    merging_parts = [rows_spec(down_rows + i * tap_rows, tap_rows) for i in range(taps)]
    (
        token_stream,
        char_stream,
        summed_low,
        merged_low,
        hidden_low,
        feed_grad,
        hidden_grad,
        branch_grad,
        merging_grad,
        summed_grad,
        char_pre_grad,
        gain_sums,
    ) = feed(
        joined,
        first,
        chars_rep,
        token_cotangent[0],
        char_cotangent[0],
        gains_all,
        upper_full,
        branch_full,
        merging_parts,
        rows_spec(0, down_rows),
    )
    feed_gain_grad, feed_shift_grad, char_gain_grad, char_shift_grad = jnp.sum(gain_sums, axis=1)
    early = early_parts(hidden_low, joined, feed_grad, merging_grad, devices)
    early, merging_grad, summed_low = after(early, merging_grad, summed_low)
    early = lax.psum_scatter(early, AXES, scatter_dimension=0, tiled=True)[0]
    up_parts = shares(outer_sum(summed_low, hidden_grad), devices)
    up_parts, merging_grad = after(up_parts, merging_grad)
    up_terms = core_terms(grid, up_parts)
    first_pre_grad, attended_grad, context_grad, rep_grad, attend_sums = merging_back(
        lengths,
        merging_grad,
        summed_grad,
        char_pre_grad,
        first_pre,
        gains_all,
        output_full,
        merging_parts,
    )
    up_terms, rep_grad, merged_low, attended_grad = after(
        up_terms, rep_grad, merged_low, attended_grad
    )
    attend_gain_grad, attend_shift_grad = jnp.sum(attend_sums, axis=1)
    branch_weight_grad = outer_sum(merged_low, branch_grad)
    output_weight_grad = outer_sum(context_low, attended_grad)
    up_layer, rep_grad = after(added_low(up_terms), rep_grad)
    up_terms = plane_terms(grid, up_layer)
    char_grads = chars_back(
        codes, inlet_full, recur_full, embeds, char_states, coefs, rep_grad, table_full.shape[1]
    )
    up_terms, char_grads, context_grad = after(up_terms, char_grads, context_grad)
    table_grad, inlet_grad, recur_weight_grad = char_grads
    up_column = added_low(up_terms)
    gain_grads = jnp.stack(
        [
            attend_gain_grad,
            attend_shift_grad,
            feed_gain_grad,
            feed_shift_grad,
            char_gain_grad,
            char_shift_grad,
        ]
    )
    gain_shares = gain_grads.reshape(6, devices, r).transpose(1, 0, 2).reshape(devices, 1, 6 * r)
    table_shares = shares(table_grad, devices)[:, :, :letters_count]
    gain_shares = jnp.pad(
        gain_shares.astype(low), ((0, 0), (0, table_shares.shape[1] - 1), (0, 0))
    )
    table_shares = jnp.concatenate([table_shares, gain_shares], axis=2)
    table_shares = jnp.pad(
        table_shares, ((0, 0), (0, 0), (0, triple - table_shares.shape[2]))
    )
    late = jnp.concatenate(
        [
            jnp.concatenate(
                [
                    side_by_side(shares(inlet_grad, devices), 3),
                    side_by_side(shares(recur_weight_grad, devices), 3),
                    one_below_other(table_shares, 3),
                ],
                axis=2,
            ),
            side_by_side(shares(output_weight_grad, devices), 3),
            side_by_side(shares(branch_weight_grad, devices), 3),
        ],
        axis=1,
    )
    def back(start, pairs, context_grad, earlier):
        return attend_back(
            mixed, context_grad, context_low, log_totals, lengths, width, start, pairs, earlier
        )

    every = width // LANES
    cut = every // 6
    up_column, late, context_grad = after(up_column, late, context_grad)
    up_terms = column_terms(grid, up_column)
    late_terms = core_terms(grid, late)
    grads = back(0, cut, context_grad, ())
    up_near, up_far = up_terms[:2] + up_terms[3:], up_terms[2:3]
    late_terms, up_near, grads, context_grad = after(late_terms, up_near, grads, context_grad)
    late_layer, context_grad = after(added_low(late_terms), context_grad)
    late_terms = plane_terms(grid, late_layer)
    grads = back(cut, every - cut, context_grad, grads)
    late_terms[3:], up_far, grads = after(late_terms[3:], up_far, grads)
    up_terms = up_near + up_far
    mixed_grad = jnp.concatenate(grads, axis=-1)
    project_parts = shares(outer_sum(states, mixed_grad), devices)
    late_terms, project_parts = after(late_terms, project_parts)
    late_terms = column_terms(grid, added_low(late_terms))
    project_layer = added_low(core_terms(grid, project_parts))
    project_layer, mixed_grad = after(project_layer, mixed_grad)
    project_terms = plane_terms(grid, project_layer)
    project_terms, late_terms = after(project_terms, late_terms)
    up_own, late = added(up_terms), added(late_terms)
    project_terms = column_terms(grid, added_low(project_terms))
    _, early = after(project_terms[1], early)
    early_own = (
        early[:down_rows].astype(jnp.float32),
        early[down_rows:].astype(jnp.float32).reshape(merging_weight.shape),
    )
    project_terms, early_own = after(project_terms, early_own)
    own_project = added(project_terms)
    input_gradient = (first_pre_grad + back_product(mixed_grad, project_full)).astype(low)
    own_chars = late[:r]
    own_table_rows = side_by_side(own_chars[:, width + triple :], 3)
    own_gains = own_table_rows[0, letters_count : letters_count + 6 * r].reshape(6, r)
    return (
        token_stream[None],
        char_stream[None],
        input_gradient[None],
        own_table_rows[:, :letters_count].T,
        one_below_other(own_chars[:, :width], 3).T,
        one_below_other(own_chars[:, width : width + triple], 3).T,
        own_project,
        one_below_other(late[r : r + r // 3], 3),
        early_own[1],
        up_own,
        early_own[0],
        one_below_other(late[r + r // 3 :], 3),
        own_gains[0],
        own_gains[1],
        own_gains[2],
        own_gains[3],
        own_gains[4],
        own_gains[5],
    )

def solution(mesh):
    placed = (
        P(AXES, None, None),
        P(AXES, None, None),
        P(AXES),
        P(AXES, None, None),
        P(AXES, None, None),
        P(None, AXES),
        P(None, AXES),
        P(None, AXES),
        P(AXES, None),
        P(AXES, None),
        P(None, AXES, None),
        P(AXES, None),
        P(AXES, None),
        P(AXES, None),
        P(AXES),
        P(AXES),
        P(AXES),
        P(AXES),
        P(AXES),
        P(AXES),
    )
    sizes = (mesh.shape["dp"], mesh.shape["fsdp"])
    return jax.shard_map(
        functools.partial(on_device, sizes),
        mesh=mesh,
        in_specs=placed,
        out_specs=(
            P(AXES, None, None),
            P(AXES, None, None),
            P(AXES, None, None),
            P(None, AXES),
            P(None, AXES),
            P(None, AXES),
            P(AXES, None),
            P(AXES, None),
            P(None, AXES, None),
            P(AXES, None),
            P(AXES, None),
            P(AXES, None),
            P(AXES),
            P(AXES),
            P(AXES),
            P(AXES),
            P(AXES),
            P(AXES),
        ),
        check_vma=False,
    )
```
